128 devices in a mesh: lat: 8 (over y, core), lon: 16 (over z, x).
Axes of the slice: x: 4, y: 4, z: 4, core: 2. Of those that a mesh axis runs over, the one named last changes fastest.
Arguments:
- ocean_forcing: bfloat16 [4, 1024, 8192], P(None, 'lat', 'lon'), may hold values from -3 to 3
- ice_velocity: float32 [2, 128, 131072], P(None, None, ('lat', 'lon')), may hold values from -3 to 3
- ice_stress: float32 [3, 128, 131072], P(None, None, ('lat', 'lon')), may hold values from -4 to 4
- cat_area: float32 [5, 128, 131072], P(None, None, ('lat', 'lon')), may hold values from 0.15 to 0.198
- cat_thick: float32 [5, 128, 131072], P(None, None, ('lat', 'lon')), may hold values from 0.5 to 3
- run_lengths: int32 [8, 16], replicated, may hold values from 1 to 8, 64 in all within a row
Outputs:
- velocity_out: float32 [2, 128, 131072], P(None, None, ('lat', 'lon'))
- stress_out: float32 [3, 128, 131072], P(None, None, ('lat', 'lon'))
- ocean_stress: bfloat16 [2, 1024, 8192], P(None, 'lat', 'lon')
The draws below stay inside these ranges and needn't reach their ends.
Inputs may be any that keep to these rules, and one draw needn't show every extreme that they name: `run_lengths`: in every band the 16 run lengths sum to 64, and one of them is 8.
All inputs are finite; a program needn't handle non-finite values.
Results may differ from the reference program's by a relative error of at most 0.001.
Values may be sent and summed in bfloat16 or wider, within the bound.
No kernel may reach another device: no remote copies, remote signals or barrier semaphores. Data moves between devices by JAX's collectives and lax.ppermute only.
A program may use at most 128 MiB of HBM per device.

```python
import math
import jax
import jax.numpy as jnp
import numpy as np
from jax import lax

BS = 128
CAT = 5
ITERS = 3
SLOTS = 8
NBB = 64
NY = 1024
NX = 8192
SLOTS_ALL = 1024
N_LAT = 8
N_LON = 16


def shard_levels(key, extent, split, low, high):
    def one(axis_at, shards_of):
        steps = jax.random.uniform(jax.random.fold_in(jax.random.fold_in(key, 6), axis_at), (shards_of,), jnp.float32, low / len(split), high / len(split))
        return jnp.repeat(jnp.exp(steps), extent[axis_at] // shards_of).reshape((-1,) + (1,) * (len(extent) - axis_at - 1))

    factor_of = one(*split[0])
    for cut in split[1:]:
        factor_of = factor_of * one(*cut)
    return factor_of


def length_profile(amount, total, most, slope):
    portions = [(1 << 20) // math.isqrt(rank ** slope) + 1 for rank in range(2, amount + 1)]
    rest, counts = total - most - (amount - 1), [1] * (amount - 1)
    while rest > 0:
        candidates = [i for i in range(amount - 1) if counts[i] < most]
        whole, left = sum([portions[i] for i in candidates]), rest
        for i in candidates:
            more = min(most - counts[i], max(1, left * portions[i] // whole), rest)
            counts[i] = counts[i] + more
            rest = rest - more
    return np.array([most] + counts)


def uneven(stream_key, count, total, most, skew):
    if count == 2:
        one = jax.random.randint(stream_key, (), max(1, total - most), min(most, total - 1) + 1)
        return jnp.stack([one, total - one])
    lengths = jnp.asarray(length_profile(count, total, most, skew), jnp.int32)
    twos = (count - 1) // 2
    source_of, sink = lengths[1:1 + 2 * twos:2], lengths[2:2 + 2 * twos:2]
    room = jnp.minimum(source_of - 1, most - sink)
    shifted = jax.random.randint(jax.random.fold_in(stream_key, 1), (twos,), 0, 1 << 20) % (room + 1)
    lengths = lengths.at[1:1 + 2 * twos:2].set(source_of - shifted).at[2:2 + 2 * twos:2].set(sink + shifted)
    return lengths[jax.random.permutation(jax.random.fold_in(stream_key, 2), count)]


def scatter_about(own_key, dims, deviation, reach, cuts=(), held_as=jnp.bfloat16):
    level = shard_levels(own_key, dims, cuts, -0.22, 0.18) if cuts else 1.0
    drawn = jax.random.normal(own_key, dims, jnp.float32) * deviation * level
    return jnp.minimum(jnp.maximum(drawn, -reach), reach).astype(held_as)


def setup_inputs(seed: int = 0) -> dict:
    splits = jax.random.split(jax.random.key(seed), 7)
    return {
        "ocean_forcing": scatter_about(splits[0], (4, NY, NX), 0.5, 3.0, ((1, 8), (2, 16))),
        "ice_velocity": scatter_about(splits[1], (2, BS, SLOTS_ALL * BS), 0.3, 3.0, ((2, 128),), jnp.float32),
        "ice_stress": scatter_about(splits[2], (3, BS, SLOTS_ALL * BS), 0.5, 4.0, ((2, 128),), jnp.float32),
        "cat_area": jnp.clip(0.15 + 0.047999993 * jax.random.uniform(splits[3], (CAT, BS, SLOTS_ALL * BS), jnp.float32) ** shard_levels(splits[3], (CAT, BS, SLOTS_ALL * BS), ((2, 128),), -0.2, 0.2), 0.15, 0.198),
        "cat_thick": jnp.clip(0.5 + 2.5 * jax.random.uniform(splits[4], (CAT, BS, SLOTS_ALL * BS), jnp.float32) ** shard_levels(splits[4], (CAT, BS, SLOTS_ALL * BS), ((2, 128),), -0.2, 0.2), 0.5, 3.0),
        "run_lengths": jax.vmap(lambda own: uneven(own, N_LON, NBB, SLOTS, 2))(jax.random.split(splits[5], N_LAT)).reshape((N_LAT, N_LON)).astype(jnp.int32),
    }


PSTAR = 2.0
CSTAR = 20.0
ECC_SQ = 4.0
DMIN_SQ = 0.01
KAPPA = 0.5
SPEED_SQ = 0.01

def ownership(run_lengths):
    ends = jnp.cumsum(run_lengths, axis=1).astype(jnp.int32)
    starts = ends - run_lengths
    slot_range = jnp.arange(SLOTS, dtype=jnp.int32)
    bands = jnp.arange(N_LAT, dtype=jnp.int32)
    position = starts[:, :, None] + slot_range[None, None, :]
    valid = slot_range[None, None, :] < run_lengths[:, :, None]
    column = jnp.where((bands % 2 == 0)[:, None, None], position, NBB - 1 - position)
    slot_col = jnp.where(valid, column, -1).astype(jnp.int32)
    columns = jnp.arange(NBB, dtype=jnp.int32)
    curve = jnp.where((bands % 2 == 0)[:, None], columns[None, :], NBB - 1 - columns[None, :])
    owner = lax.optimization_barrier(jnp.sum((ends[:, None, :] <= curve[:, :, None]).astype(jnp.int32), axis=2))
    first = jnp.take_along_axis(starts, owner, axis=1)
    grid_slot = ((bands[:, None] * N_LON + owner) * SLOTS + curve - first).astype(jnp.int32)
    return (slot_col, grid_slot)

def onto_grid(slotted, grid_slot):
    fields = slotted.shape[0]
    blocks = slotted.reshape(fields, BS, SLOTS_ALL, BS)
    taken = jnp.take(blocks, grid_slot.reshape(-1), axis=2)
    taken = taken.reshape(fields, BS, N_LAT, NBB, BS).transpose(0, 2, 1, 3, 4)
    return taken.reshape(fields, NY, NX)

def onto_slots(grid, slot_col):
    fields = grid.shape[0]
    blocks = grid.reshape(fields, N_LAT, BS, NBB, BS).transpose(0, 1, 3, 2, 4)
    blocks = blocks.reshape(fields, N_LAT * NBB, BS, BS)
    bands = jnp.arange(N_LAT, dtype=jnp.int32)[:, None, None]
    index = (bands * NBB + jnp.maximum(slot_col, 0)).reshape(-1)
    taken = jnp.take(blocks, index, axis=1)
    taken = jnp.where((slot_col.reshape(-1) >= 0)[None, :, None, None], taken, jnp.float32(0.0))
    return taken.transpose(0, 2, 1, 3).reshape(fields, BS, SLOTS_ALL * BS)

def east_of(field):
    return jnp.roll(field, -1, axis=-1)

def west_of(field):
    return jnp.roll(field, 1, axis=-1)

def north_of(field):
    return jnp.concatenate([field[..., 1:, :], jnp.zeros_like(field[..., :1, :])], axis=-2)

def south_of(field):
    return jnp.concatenate([jnp.zeros_like(field[..., :1, :]), field[..., :-1, :]], axis=-2)

def update_stress(zonal, merid, zonal_east, merid_east, zonal_north, merid_north, stresses, strength):
    first_inv, second_inv, shear_stress = stresses
    strain_xx = zonal_east - zonal
    strain_yy = merid_north - merid
    strain_xy = 0.5 * (zonal_north - zonal + merid_east - merid)
    divergence = strain_xx + strain_yy
    tension = strain_xx - strain_yy
    shearing = 2.0 * strain_xy
    deformation = jnp.sqrt(divergence * divergence + (tension * tension + shearing * shearing) / ECC_SQ + DMIN_SQ)
    viscous = strength / deformation
    first_inv = (first_inv + KAPPA * (viscous * divergence - strength)) / (1.0 + KAPPA)
    second_inv = (second_inv + KAPPA * viscous * tension / ECC_SQ) / (1.0 + KAPPA)
    shear_stress = (shear_stress + KAPPA * viscous * shearing / (2.0 * ECC_SQ)) / (1.0 + KAPPA)
    return (first_inv, second_inv, shear_stress)

def update_velocity(zonal, merid, stresses, west_stresses, south_stresses, mass, concentration, coriolis, forcing):
    first_inv, second_inv, shear_stress = stresses
    normal_xx = 0.5 * (first_inv + second_inv)
    normal_yy = 0.5 * (first_inv - second_inv)
    west_xx = 0.5 * (west_stresses[0] + west_stresses[1])
    south_yy = 0.5 * (south_stresses[0] - south_stresses[1])
    force_x = normal_xx - west_xx + shear_stress - south_stresses[2]
    force_y = shear_stress - west_stresses[2] + normal_yy - south_yy
    cur_x, cur_y, wind_x, wind_y = (forcing[0], forcing[1], forcing[2], forcing[3])
    drag = concentration * jnp.sqrt((cur_x - zonal) ** 2 + (cur_y - merid) ** 2 + SPEED_SQ)
    diagonal = mass + drag
    turning = coriolis * mass
    rhs_x = mass * zonal + force_x + wind_x + drag * cur_x
    rhs_y = mass * merid + force_y + wind_y + drag * cur_y
    denominator = diagonal * diagonal + turning * turning
    return ((diagonal * rhs_x + turning * rhs_y) / denominator, (diagonal * rhs_y - turning * rhs_x) / denominator)

def surface_stress(zonal, merid, concentration, forcing):
    cur_x, cur_y, wind_x, wind_y = (forcing[0], forcing[1], forcing[2], forcing[3])
    drag = concentration * jnp.sqrt((cur_x - zonal) ** 2 + (cur_y - merid) ** 2 + SPEED_SQ)
    return jnp.stack([(1.0 - concentration) * wind_x + drag * (zonal - cur_x), (1.0 - concentration) * wind_y + drag * (merid - cur_y)])

def reference(ocean_forcing, ice_velocity, ice_stress, cat_area, cat_thick, run_lengths):
    slot_col, grid_slot = ownership(run_lengths)
    forcing = ocean_forcing.astype(jnp.float32)
    velocity = onto_grid(ice_velocity, grid_slot)
    stress = onto_grid(ice_stress, grid_slot)
    area = onto_grid(cat_area, grid_slot)
    thick = onto_grid(cat_thick, grid_slot)
    concentration = lax.optimization_barrier(jnp.sum(area, axis=0))
    mass = lax.optimization_barrier(jnp.sum(area * thick, axis=0))
    strength = PSTAR * mass * jnp.exp(-CSTAR * (1.0 - concentration))
    rows = jnp.arange(NY, dtype=jnp.int32).astype(jnp.float32)
    latitude = -78.0 + 168.0 * (rows + 0.5) / NY
    coriolis = jnp.sin(latitude * (jnp.pi / 180.0))[:, None]
    zonal, merid = (velocity[0], velocity[1])
    stresses = (stress[0], stress[1], stress[2])
    for subcycle in range(ITERS):
        stresses = update_stress(zonal, merid, east_of(zonal), east_of(merid), north_of(zonal), north_of(merid), stresses, strength)
        west_stresses = tuple((west_of(item) for item in stresses))
        south_stresses = tuple((south_of(item) for item in stresses))
        zonal, merid = update_velocity(zonal, merid, stresses, west_stresses, south_stresses, mass, concentration, coriolis, forcing)
    velocity_out = onto_slots(jnp.stack([zonal, merid]), slot_col)
    stress_out = onto_slots(jnp.stack(stresses), slot_col)
    ocean_stress = surface_stress(zonal, merid, concentration, forcing).astype(jnp.bfloat16)
    return (velocity_out, stress_out, ocean_stress)
```

```python
import functools

import jax
import jax.numpy as jnp
from jax import lax
from jax.experimental import pallas as pl
from jax.experimental.pallas import tpu as pltpu
from jax.sharding import PartitionSpec as P

BS = 128
ITERS = 3
NLAT = 8
NLON = 16
SLOTS = 8
NBB = 64
TILE = 4
DEEP = 3
PSTAR = 2.0
CSTAR = 20.0
DMIN_SQ = 0.01
SPEED_SQ = 0.01
ICE = 7
U, V, S1, S2, S12, AREA, MASS, STR, UO, VO, TX, TY = range(12)
STRIP = (SLOTS + 1) * BS
TOP = 8
ROWS = BS + 2 * TOP
SEND_ROWS = 32
M1_ROWS = TILE * 32 + SLOTS * 8
M2_ROWS = (SLOTS + 1) * 32 + 80
M3_ROWS = SLOTS * 16
M4_ROWS = TILE * 16
F32 = jnp.float32
BF16 = jnp.bfloat16


def lanes_of(shape):
    return lax.broadcasted_iota(jnp.int32, shape, len(shape) - 1)


def ice_fields(vel, stress, area, thick):
    conc = area[0] + area[1] + area[2] + area[3] + area[4]
    mass = area[0] * thick[0]
    for n in range(1, 5):
        mass = mass + area[n] * thick[n]
    return [vel[0], vel[1], stress[0], stress[1], stress[2], conc, mass]


def strength_of(conc, mass):
    return (PSTAR / 3.0) * mass * jnp.exp(-CSTAR * (1.0 - conc))


def edges_kernel(lens, place, *refs):
    ice = [refs[4 * i : 4 * i + 4] for i in range(4)]
    f_low, f_high, south, north, prev, nxt = refs[16:]
    odd = lax.rem(place[0], 2) == 1
    for out, which, force, row0, frow0 in (
        (south, 0, f_low, 0, 0),
        (north, 1, f_high, 5, 14),
    ):
        arrays = [ice[i][which] for i in range(4)]
        fields = ice_fields(*[[a[n] for n in range(a.shape[0])] for a in arrays])
        out[...] = jnp.zeros(out.shape, F32)
        for f in range(ICE):
            out[3 * f : 3 * f + 3, :] = fields[f][row0 : row0 + 3, :]
        for f in range(4):
            rows = force[f].astype(F32)
            out[21 + f : 22 + f, 0:512] = rows[frow0 : frow0 + 1, :]
            out[21 + f : 22 + f, 512:1024] = rows[frow0 + 1 : frow0 + 2, :]
    lane = lanes_of((BS, BS))
    for out, which, col_even, col_odd in ((prev, 2, 0, 125), (nxt, 3, 125, 0)):
        arrays = [ice[i][which] for i in range(4)]
        fields = ice_fields(*[[a[n] for n in range(a.shape[0])] for a in arrays])
        packed = jnp.zeros((BS, BS), F32)
        for f in range(ICE):
            shift = jnp.where(odd, (3 * f - col_odd) % BS, (3 * f - col_even) % BS)
            moved = pltpu.roll(fields[f], shift, 1)
            packed = jnp.where((lane >= 3 * f) & (lane < 3 * f + 3), moved, packed)
        out[...] = packed


def make_edges(lens, place, vel, stress, area, thick, forcing):
    width = SLOTS * BS

    def specs(n):
        return [
            pl.BlockSpec((n, 8, width), lambda i, lens, place: (0, 0, 0)),
            pl.BlockSpec((n, 8, width), lambda i, lens, place: (0, BS // 8 - 1, 0)),
            pl.BlockSpec((n, BS, BS), lambda i, lens, place: (0, 0, 0)),
            pl.BlockSpec(
                (n, BS, BS),
                lambda i, lens, place: (0, 0, lens[place[0] * NLON + place[1]] - 1),
            ),
        ]

    in_specs = specs(2) + specs(3) + specs(5) + specs(5)
    in_specs += [
        pl.BlockSpec((4, 16, 512), lambda i, lens, place: (0, 0, 0)),
        pl.BlockSpec((4, 16, 512), lambda i, lens, place: (0, BS // 16 - 1, 0)),
    ]
    whole = lambda i, lens, place: (0, 0)
    return pl.pallas_call(
        edges_kernel,
        grid_spec=pltpu.PrefetchScalarGridSpec(
            num_scalar_prefetch=2,
            grid=(1,),
            in_specs=in_specs,
            out_specs=[
                pl.BlockSpec((SEND_ROWS, width), whole),
                pl.BlockSpec((SEND_ROWS, width), whole),
                pl.BlockSpec((BS, BS), whole),
                pl.BlockSpec((BS, BS), whole),
            ],
        ),
        out_shape=[
            jax.ShapeDtypeStruct((SEND_ROWS, width), F32),
            jax.ShapeDtypeStruct((SEND_ROWS, width), F32),
            jax.ShapeDtypeStruct((BS, BS), F32),
            jax.ShapeDtypeStruct((BS, BS), F32),
        ],
        compiler_params=pltpu.CompilerParams(vmem_limit_bytes=32 * 2**20),
        name="edges",
    )(lens, place, *([vel] * 4), *([stress] * 4), *([area] * 4), *([thick] * 4), forcing, forcing)


def spread_kernel(forcing, north, south, out, hold):
    def rows16(pair, carry):
        base = pl.multiple_of(pair * 16, 16)
        for cb in range(TILE):
            parts = [
                forcing[f, pl.ds(base, 16), cb * BS : (cb + 1) * BS].astype(F32) for f in range(4)
            ]
            low = jnp.concatenate([p[0:8] for p in parts], axis=0)
            high = jnp.concatenate([p[8:16] for p in parts], axis=0)
            out[2 * pair, cb * 32 : (cb + 1) * 32, :] = low.astype(BF16)
            out[2 * pair + 1, cb * 32 : (cb + 1) * 32, :] = high.astype(BF16)
        return carry

    lax.fori_loop(0, BS // 16, rows16, 0)
    for j in range(NLON):
        hold[...] = jnp.zeros(hold.shape, F32)
        source = north if j < 8 else south
        f = j % 8
        if f < ICE:
            rows = source[3 * f : 3 * f + 3, :]
            high = rows.astype(BF16).astype(F32)
            low = rows - high
            for s in range(SLOTS):
                hold[8 * s : 8 * s + 3, :] = high[:, s * BS : (s + 1) * BS]
                hold[8 * s + 3 : 8 * s + 6, :] = low[:, s * BS : (s + 1) * BS]
        field, h = j // 4, j % 4
        source = south if h < 2 else north
        for cb in range(TILE):
            at = (h % 2) * 512 + cb * BS
            hold[8 * cb + 6 : 8 * cb + 7, :] = source[21 + field : 22 + field, at : at + BS]
        out[j, TILE * 32 :, :] = hold[...].astype(BF16)


def spread(forcing, north, south):
    return pl.pallas_call(
        spread_kernel,
        out_shape=jax.ShapeDtypeStruct((NLON, M1_ROWS, BS), BF16),
        in_specs=[pl.BlockSpec(memory_space=pltpu.VMEM)] * 3,
        out_specs=pl.BlockSpec(memory_space=pltpu.VMEM),
        scratch_shapes=[pltpu.VMEM((SLOTS * 8, BS), F32)],
        compiler_params=pltpu.CompilerParams(vmem_limit_bytes=32 * 2**20),
        name="spread",
    )(forcing, north, south)


def deal_kernel(lens, place, got, out, groups, hold, table):
    band, lon = place[0], place[1]
    odd = lax.rem(band, 2) == 1
    other = jnp.where(lon < 8, jnp.minimum(band + 1, NLAT - 1), jnp.maximum(band - 1, 0))
    other_odd = lax.rem(other, 2) == 1

    def fill(l, start):
        groups[pl.ds(pl.multiple_of(l * SLOTS, SLOTS), SLOTS)] = (
            got[l, TILE * 32 :, :].astype(F32).reshape(SLOTS, 8, BS)
        )
        count = lens[other * NLON + l]

        def slot(s, carry):
            at = start + s
            table[jnp.where(other_odd, NBB - 1 - at, at)] = l * SLOTS + s
            return carry

        lax.fori_loop(0, count, slot, 0)
        return start + count

    lax.fori_loop(0, NLON, fill, 0)
    lane32 = lanes_of((32, BS)) < 64
    lane8 = lanes_of((8, BS)) < 64
    row6 = lax.broadcasted_iota(jnp.int32, (8, BS), 0) == 6
    hold[72:80, :] = jnp.zeros((8, BS), F32)

    def block(c):
        tile, cb = c // TILE, lax.rem(c, TILE)
        rows = got[tile, pl.ds(pl.multiple_of(cb * 32, 32), 32), :].astype(F32)
        group = jnp.where(row6, groups[tile * SLOTS + cb], groups[table[c]])
        return rows, group

    def owner(k, start):
        count = lens[band * NLON + k]
        last = start + count - 1
        east = jnp.where(odd, NBB - 1 - start, last) + 1
        west = jnp.where(odd, NBB - 1 - last, start) - 1
        east, west = lax.rem(east, NBB), lax.rem(west + NBB, NBB)
        for e in range(SLOTS + 1):
            mine = e < count
            at = start + e
            column = jnp.where(odd, NBB - 1 - at, at)
            rows_a, group_a = block(jnp.where(mine, column, east))
            rows_b, group_b = block(jnp.where(mine, column, west))
            out[k, e * 32 : (e + 1) * 32, :] = jnp.where(lane32, rows_a, rows_b).astype(BF16)
            hold[e * 8 : (e + 1) * 8, :] = jnp.where(lane8, group_a, group_b)
        out[k, (SLOTS + 1) * 32 :, :] = hold[...].astype(BF16)
        return start + count

    lax.fori_loop(0, NLON, owner, 0)


def deal(lens, place, got):
    return pl.pallas_call(
        deal_kernel,
        out_shape=jax.ShapeDtypeStruct((NLON, M2_ROWS, BS), BF16),
        in_specs=[pl.BlockSpec(memory_space=pltpu.SMEM)] * 2
        + [pl.BlockSpec(memory_space=pltpu.VMEM)],
        out_specs=pl.BlockSpec(memory_space=pltpu.VMEM),
        scratch_shapes=[
            pltpu.VMEM((NLON * SLOTS, 8, BS), F32),
            pltpu.VMEM((80, BS), F32),
            pltpu.SMEM((NBB,), jnp.int32),
        ],
        compiler_params=pltpu.CompilerParams(vmem_limit_bytes=32 * 2**20),
        name="deal",
    )(lens, place, got)


def dynamics_kernel(
    lens, place, vel, stress, area, thick, got, from_prev, from_next, coriolis,
    vel_out, stress_out, handed, st,
):
    s = pl.program_id(0)
    band, lon = place[0], place[1]
    odd = lax.rem(band, 2) == 1
    count = lens[band * NLON + lon]
    own = pl.ds(TOP, BS)

    def lanes_at(slot):
        return pl.ds(pl.multiple_of(jnp.where(odd, SLOTS - 1 - slot, slot) * BS, BS), BS)

    edge_lanes = pl.ds(SLOTS * BS, BS)

    @pl.when(s == 0)
    def _():
        lane = lanes_of((BS, BS)) < 64
        east = jnp.where(odd, from_prev[...], from_next[...])
        west = jnp.where(odd, from_next[...], from_prev[...])
        edge = []
        for f in range(ICE):
            moved = jnp.where(
                lane,
                pltpu.roll(east, (BS - 3 * f) % BS, 1),
                pltpu.roll(west, 125 - 3 * f, 1),
            )
            st[f, own, edge_lanes] = moved
            edge.append(moved)
        st[STR, own, edge_lanes] = strength_of(edge[AREA], edge[MASS])

        def forcing_rows(j, carry):
            at = pl.ds(pl.multiple_of(TOP + j * 8, 8), 8)
            for e in range(SLOTS + 1):
                rows = got[j, e * 32 : (e + 1) * 32, :].astype(F32)
                lanes = lanes_at(e) if e < SLOTS else edge_lanes
                for f in range(4):
                    st[UO + f, at, lanes] = rows[f * 8 : (f + 1) * 8, :]
            return carry

        lax.fori_loop(0, NLON, forcing_rows, 0)
        for j in range(NLON):
            group = got[j, (SLOTS + 1) * 32 :, :].astype(F32)
            f = j % 8
            row0 = TOP + BS if j < 8 else TOP - DEEP
            force_row = (TOP - 2, TOP - 1, TOP + BS, TOP + BS + 1)[j % 4]
            for e in range(SLOTS + 1):
                lanes = lanes_at(e) if e < SLOTS else edge_lanes
                if f < ICE:
                    st[f, row0 : row0 + DEEP, lanes] = (
                        group[8 * e : 8 * e + 3, :] + group[8 * e + 3 : 8 * e + 6, :]
                    )
                st[UO + j // 4, force_row : force_row + 1, lanes] = group[8 * e + 6 : 8 * e + 7, :]
        for row0 in (0, TOP + BS):
            rows = pl.ds(row0, 8)
            st[STR, rows, :] = strength_of(st[AREA, rows, :], st[MASS, rows, :])

    @pl.when(s < count)
    def _():
        fields = ice_fields(
            [vel[0], vel[1]],
            [stress[0], stress[1], stress[2]],
            [area[n] for n in range(5)],
            [thick[n] for n in range(5)],
        )
        lanes = lanes_at(s)
        for f in range(ICE):
            st[f, own, lanes] = fields[f]
        st[STR, own, lanes] = strength_of(fields[AREA], fields[MASS])

    @pl.when(s >= count)
    def _():
        lanes = lanes_at(s)
        for f in range(STR + 1):
            st[f, own, lanes] = st[f, own, edge_lanes]

    @pl.when(s == SLOTS - 1)
    def _():
        cells = (8, STRIP)

        row = lax.broadcasted_iota(jnp.int32, cells, 0)

        def load(f, g):
            return st[f, pl.ds(pl.multiple_of(g * 8, 8), 8), :]

        def north_of(x, above):
            return pltpu.roll(jnp.where(row == 0, above, x), 7, 0)

        def south_of(x, below):
            return pltpu.roll(jnp.where(row == 7, below, x), 1, 0)

        def stress_rows(g):
            u, v = load(U, g), load(V, g)
            exx = pltpu.roll(u, STRIP - 1, 1) - u
            eyy = north_of(v, load(V, g + 1)) - v
            shr = north_of(u, load(U, g + 1)) - u + (pltpu.roll(v, STRIP - 1, 1) - v)
            div = exx + eyy
            ten = exx - eyy
            square = div * div + 0.25 * (ten * ten + shr * shr) + DMIN_SQ
            third = load(STR, g)
            visc = third * lax.rsqrt(square)
            rows = pl.ds(pl.multiple_of(g * 8, 8), 8)
            st[S1, rows, :] = (2.0 / 3.0) * load(S1, g) + (visc * div - third)
            st[S2, rows, :] = (2.0 / 3.0) * load(S2, g) + 0.25 * visc * ten
            st[S12, rows, :] = (2.0 / 3.0) * load(S12, g) + 0.125 * visc * shr

        def velocity_rows(g, beyond=None):
            below = max(g - 1, 0) if isinstance(g, int) else g - 1
            s1, s2, s12 = load(S1, g), load(S2, g), load(S12, g)
            sxx = 0.5 * (s1 + s2)
            syy = 0.5 * (s1 - s2)
            syy_s = south_of(syy, 0.5 * (load(S1, below) - load(S2, below)))
            fx = sxx - pltpu.roll(sxx, 1, 1) + s12 - south_of(s12, load(S12, below))
            fy = s12 - pltpu.roll(s12, 1, 1) + syy - syy_s
            u, v, uo, vo, m = load(U, g), load(V, g), load(UO, g), load(VO, g), load(MASS, g)
            du, dv = uo - u, vo - v
            square = du * du + dv * dv + SPEED_SQ
            drag = load(AREA, g) * (square * lax.rsqrt(square))
            d = m + drag
            turn = jnp.broadcast_to(
                coriolis[pl.ds(pl.multiple_of(g * 8, 8), 8), :], (8, BS)
            )
            q = jnp.concatenate([turn] * (SLOTS + 1), axis=1) * m
            ru = m * u + fx + load(TX, g) + drag * uo
            rv = m * v + fy + load(TY, g) + drag * vo
            inv = 1.0 / (d * d + q * q)
            new_u = (d * ru + q * rv) * inv
            new_v = (d * rv - q * ru) * inv
            if beyond is not None:
                new_u = jnp.where(beyond, 0.0, new_u)
                new_v = jnp.where(beyond, 0.0, new_v)
            rows = pl.ds(pl.multiple_of(g * 8, 8), 8)
            st[U, rows, :] = new_u
            st[V, rows, :] = new_v

        groups = BS // 8
        first = jnp.broadcast_to(band == 0, cells)
        final = jnp.broadcast_to(band == NLAT - 1, cells)
        for it in range(ITERS):
            last = it == ITERS - 1

            def stress_step(g, carry):
                stress_rows(g)
                return carry

            def velocity_step(g, carry):
                velocity_rows(g)
                return carry

            lax.fori_loop(0, groups + (1 if last else 2), stress_step, 0)
            if not last:
                velocity_rows(0, first)
                velocity_rows(groups + 1, final)
            lax.fori_loop(1, groups + 1, velocity_step, 0)

        def finish(j, carry):
            rows = pl.ds(pl.multiple_of(TOP + j * 8, 8), 8)
            out_rows = pl.ds(pl.multiple_of(j * 8, 8), 8)
            for e in range(SLOTS):
                lanes = lanes_at(e)
                out_lanes = slice(e * BS, (e + 1) * BS)
                mine = jnp.broadcast_to(e < count, (8, BS))
                u, v = st[U, rows, lanes], st[V, rows, lanes]
                vel_out[0, out_rows, out_lanes] = jnp.where(mine, u, 0.0)
                vel_out[1, out_rows, out_lanes] = jnp.where(mine, v, 0.0)
                for n in range(3):
                    stress_out[n, out_rows, out_lanes] = jnp.where(
                        mine, st[S1 + n, rows, lanes], 0.0
                    )
                conc = st[AREA, rows, lanes]
                du, dv = u - st[UO, rows, lanes], v - st[VO, rows, lanes]
                square = du * du + dv * dv + SPEED_SQ
                drag = conc * (square * lax.rsqrt(square))
                x = (1.0 - conc) * st[TX, rows, lanes] + drag * du
                y = (1.0 - conc) * st[TY, rows, lanes] + drag * dv
                handed[j, e * 16 : (e + 1) * 16, :] = jnp.concatenate([x, y], axis=0).astype(BF16)
            return carry

        lax.fori_loop(0, groups, finish, 0)


def dynamics(lens, place, vel, stress, area, thick, got, from_prev, from_next, coriolis):
    def slot(n):
        return pl.BlockSpec((n, BS, BS), lambda i, lens, place: (0, 0, i))

    def whole(*shape):
        return pl.BlockSpec(shape, lambda i, lens, place: (0,) * len(shape))

    width = SLOTS * BS
    return pl.pallas_call(
        dynamics_kernel,
        grid_spec=pltpu.PrefetchScalarGridSpec(
            num_scalar_prefetch=2,
            grid=(SLOTS,),
            in_specs=[
                slot(2), slot(3), slot(5), slot(5),
                whole(NLON, M2_ROWS, BS), whole(BS, BS), whole(BS, BS), whole(ROWS, BS),
            ],
            out_specs=[whole(2, BS, width), whole(3, BS, width), whole(NLON, M3_ROWS, BS)],
            scratch_shapes=[pltpu.VMEM((12, ROWS + 8, STRIP), F32)],
        ),
        out_shape=[
            jax.ShapeDtypeStruct((2, BS, width), F32),
            jax.ShapeDtypeStruct((3, BS, width), F32),
            jax.ShapeDtypeStruct((NLON, M3_ROWS, BS), BF16),
        ],
        compiler_params=pltpu.CompilerParams(vmem_limit_bytes=48 * 2**20),
        name="dynamics",
    )(lens, place, vel, stress, area, thick, got, from_prev, from_next, coriolis)


def sort_kernel(lens, place, got, out):
    band = place[0]
    odd = lax.rem(band, 2) == 1

    def owner(k, start):
        count = lens[band * NLON + k]

        def slot(s, carry):
            at = start + s
            out[jnp.where(odd, NBB - 1 - at, at)] = got[k * SLOTS + s]
            return carry

        lax.fori_loop(0, count, slot, 0)
        return start + count

    lax.fori_loop(0, NLON, owner, 0)


def sort_back(lens, place, got):
    return pl.pallas_call(
        sort_kernel,
        out_shape=jax.ShapeDtypeStruct((NBB, 16, BS), BF16),
        in_specs=[pl.BlockSpec(memory_space=pltpu.SMEM)] * 2
        + [pl.BlockSpec(memory_space=pltpu.VMEM)],
        out_specs=pl.BlockSpec(memory_space=pltpu.VMEM),
        name="sort_back",
    )(lens, place, got)


def settle_kernel(got, out):
    def rows16(pair, carry):
        rows = pl.ds(pl.multiple_of(pair * 16, 16), 16)
        for cb in range(TILE):
            a = got[2 * pair, cb * 16 : (cb + 1) * 16, :].astype(F32)
            b = got[2 * pair + 1, cb * 16 : (cb + 1) * 16, :].astype(F32)
            lanes = slice(cb * BS, (cb + 1) * BS)
            out[0, rows, lanes] = jnp.concatenate([a[0:8], b[0:8]], axis=0).astype(BF16)
            out[1, rows, lanes] = jnp.concatenate([a[8:16], b[8:16]], axis=0).astype(BF16)
        return carry

    lax.fori_loop(0, BS // 16, rows16, 0)


def settle(got):
    return pl.pallas_call(
        settle_kernel,
        out_shape=jax.ShapeDtypeStruct((2, BS, TILE * BS), BF16),
        in_specs=[pl.BlockSpec(memory_space=pltpu.VMEM)],
        out_specs=pl.BlockSpec(memory_space=pltpu.VMEM),
        name="settle",
    )(got)


def to_all(block):
    return lax.all_to_all(block, "lon", 0, 0, tiled=True)


def body(ocean_forcing, ice_velocity, ice_stress, cat_area, cat_thick, run_lengths):
    band_idx = lax.axis_index("lat")
    lon_idx = lax.axis_index("lon")
    lens = run_lengths.reshape(-1)
    place = jnp.stack([band_idx, lon_idx]).astype(jnp.int32)
    ice = (ice_velocity, ice_stress, cat_area, cat_thick)
    to_south, to_north, to_prev, to_next = make_edges(lens, place, *ice, ocean_forcing)
    north = lax.ppermute(to_south, "lat", [(b, b - 1) for b in range(1, NLAT)])
    south = lax.ppermute(to_north, "lat", [(b, b + 1) for b in range(NLAT - 1)])
    from_prev = lax.ppermute(to_next, "lon", [(k, (k + 1) % NLON) for k in range(NLON)])
    from_next = lax.ppermute(to_prev, "lon", [(k, (k - 1) % NLON) for k in range(NLON)])
    rows = (band_idx * BS + jnp.arange(-TOP, BS + TOP, dtype=jnp.int32)).astype(F32)
    latitude = -78.0 + 168.0 * (rows + 0.5) / (BS * NLAT)
    coriolis = jnp.broadcast_to(jnp.sin(latitude * (jnp.pi / 180.0))[:, None], (ROWS, BS))
    dealt = to_all(deal(lens, place, to_all(spread(ocean_forcing, north, south))))
    velocity_out, stress_out, handed = dynamics(
        lens, place, *ice, dealt, from_prev, from_next, coriolis
    )
    handed = to_all(handed).reshape(NLON * SLOTS, 16, BS)
    back = sort_back(lens, place, handed).reshape(NLON, M4_ROWS, BS)
    return (velocity_out, stress_out, settle(to_all(back)))


def solution(mesh):
    slots = P(None, None, ("lat", "lon"))
    grid = P(None, "lat", "lon")
    return jax.shard_map(
        body,
        mesh=mesh,
        in_specs=(grid, slots, slots, slots, slots, P()),
        out_specs=(slots, slots, grid),
        check_vma=False,
    )
```

```python
import functools

import jax
import jax.numpy as jnp
from jax import lax
from jax.experimental import pallas as pl
from jax.experimental.pallas import tpu as pltpu
from jax.sharding import PartitionSpec as P

BS = 128
ITERS = 3
NLAT = 8
NLON = 16
SLOTS = 8
NBB = 64
TILE = 4
DEEP = 3
PSTAR = 2.0
CSTAR = 20.0
DMIN_SQ = 0.01
SPEED_SQ = 0.01
ICE = 7
U, V, SXX, SYY, S12, AREA, MASS, STR, UO, VO, TX, TY, TURN, S2_OUT = range(14)
EDGE_LANES = 3 * ICE
STRIP = (SLOTS + 1) * BS
WIDE = 3 * BS
TOP = 8
ROWS = BS + 2 * TOP
SEND_ROWS = 32
M1_ROWS = TILE * 32 + SLOTS * 8
M2_ROWS = (SLOTS + 1) * 32 + 80
M3_ROWS = SLOTS * 16
M4_ROWS = TILE * 16
F32 = jnp.float32
BF16 = jnp.bfloat16


def lanes_of(shape):
    return lax.broadcasted_iota(jnp.int32, shape, len(shape) - 1)


def ice_fields(vel, stress, area, thick):
    conc = area[0] + area[1] + area[2] + area[3] + area[4]
    mass = area[0] * thick[0]
    for n in range(1, 5):
        mass = mass + area[n] * thick[n]
    sxx, syy = 0.5 * (stress[0] + stress[1]), 0.5 * (stress[0] - stress[1])
    return [vel[0], vel[1], sxx, syy, stress[2], conc, mass]


def strength_of(conc, mass):
    return (PSTAR / 6.0) * mass * jnp.exp(-CSTAR * (1.0 - conc))


def edges_kernel(lens, place, *refs):
    ice = [refs[4 * i : 4 * i + 4] for i in range(4)]
    f_low, f_high, south, north, packed_out = refs[16:]
    odd = lax.rem(place[0], 2) == 1
    for out, which, force, row0, frow0 in (
        (south, 0, f_low, 0, 0),
        (north, 1, f_high, 5, 14),
    ):
        arrays = [ice[i][which] for i in range(4)]
        fields = ice_fields(*[[a[n] for n in range(a.shape[0])] for a in arrays])
        out[...] = jnp.zeros(out.shape, F32)
        for f in range(ICE):
            out[3 * f : 3 * f + 3, :] = fields[f][row0 : row0 + 3, :]
        for f in range(4):
            rows = force[f].astype(F32)
            out[21 + f : 22 + f, 0:512] = rows[frow0 : frow0 + 1, :]
            out[21 + f : 22 + f, 512:1024] = rows[frow0 + 1 : frow0 + 2, :]
    lane = lanes_of((BS, BS))
    packed = jnp.zeros((BS, BS), F32)
    for side, which, col_even, col_odd in ((0, 2, 0, 125), (1, 3, 125, 0)):
        arrays = [ice[i][which] for i in range(4)]
        fields = ice_fields(*[[a[n] for n in range(a.shape[0])] for a in arrays])
        for f in range(ICE):
            at = 2 * side * EDGE_LANES + 3 * f
            high = fields[f].astype(BF16).astype(F32)
            for part, there in ((high, at), (fields[f] - high, at + EDGE_LANES)):
                shift = jnp.where(odd, (there - col_odd) % BS, (there - col_even) % BS)
                moved = pltpu.roll(part, shift, 1)
                packed = jnp.where((lane >= there) & (lane < there + 3), moved, packed)
    packed_out[...] = packed


def make_edges(lens, place, vel, stress, area, thick, forcing):
    width = SLOTS * BS

    def specs(n):
        return [
            pl.BlockSpec((n, 8, width), lambda i, lens, place: (0, 0, 0)),
            pl.BlockSpec((n, 8, width), lambda i, lens, place: (0, BS // 8 - 1, 0)),
            pl.BlockSpec((n, BS, BS), lambda i, lens, place: (0, 0, 0)),
            pl.BlockSpec(
                (n, BS, BS),
                lambda i, lens, place: (0, 0, lens[place[0], place[1]] - 1),
            ),
        ]

    in_specs = specs(2) + specs(3) + specs(5) + specs(5)
    in_specs += [
        pl.BlockSpec((4, 16, 512), lambda i, lens, place: (0, 0, 0)),
        pl.BlockSpec((4, 16, 512), lambda i, lens, place: (0, BS // 16 - 1, 0)),
    ]
    whole = lambda i, lens, place: (0, 0)
    return pl.pallas_call(
        edges_kernel,
        grid_spec=pltpu.PrefetchScalarGridSpec(
            num_scalar_prefetch=2,
            grid=(1,),
            in_specs=in_specs,
            out_specs=[
                pl.BlockSpec((SEND_ROWS, width), whole),
                pl.BlockSpec((SEND_ROWS, width), whole),
                pl.BlockSpec((BS, BS), whole),
            ],
        ),
        out_shape=[
            jax.ShapeDtypeStruct((SEND_ROWS, width), F32),
            jax.ShapeDtypeStruct((SEND_ROWS, width), F32),
            jax.ShapeDtypeStruct((BS, BS), F32),
        ],
        compiler_params=pltpu.CompilerParams(vmem_limit_bytes=60 * 2**20),
        name="edges",
    )(lens, place, *([vel] * 4), *([stress] * 4), *([area] * 4), *([thick] * 4), forcing, forcing)


def spread_kernel(forcing, north, south, edges, out, hold):
    def rows16(pair, carry):
        base = pl.multiple_of(pair * 16, 16)
        for cb in range(TILE):
            parts = [
                forcing[f, pl.ds(base, 16), cb * BS : (cb + 1) * BS].astype(F32) for f in range(4)
            ]
            low = jnp.concatenate([p[0:8] for p in parts], axis=0)
            high = jnp.concatenate([p[8:16] for p in parts], axis=0)
            out[2 * pair, cb * 32 : (cb + 1) * 32, :] = low.astype(BF16)
            out[2 * pair + 1, cb * 32 : (cb + 1) * 32, :] = high.astype(BF16)
        return carry

    lax.fori_loop(0, BS // 16, rows16, 0)
    for j in range(NLON):
        hold[...] = jnp.zeros(hold.shape, F32)
        source = north if j < 8 else south
        f = j % 8
        if f < ICE:
            rows = source[3 * f : 3 * f + 3, :]
            high = rows.astype(BF16).astype(F32)
            low = rows - high
            for s in range(SLOTS):
                hold[8 * s : 8 * s + 3, :] = high[:, s * BS : (s + 1) * BS]
                hold[8 * s + 3 : 8 * s + 6, :] = low[:, s * BS : (s + 1) * BS]
        field, h = j // 4, j % 4
        source = south if h < 2 else north
        for cb in range(TILE):
            at = (h % 2) * 512 + cb * BS
            hold[8 * cb + 6 : 8 * cb + 7, :] = source[21 + field : 22 + field, at : at + BS]
        for s in range(SLOTS):
            hold[8 * s + 7 : 8 * s + 8, :] = edges[8 * j + s : 8 * j + s + 1, :]
        out[j, TILE * 32 :, :] = hold[...].astype(BF16)


def spread(forcing, north, south, edges):
    return pl.pallas_call(
        spread_kernel,
        out_shape=jax.ShapeDtypeStruct((NLON, M1_ROWS, BS), BF16),
        in_specs=[pl.BlockSpec(memory_space=pltpu.VMEM)] * 4,
        out_specs=pl.BlockSpec(memory_space=pltpu.VMEM),
        scratch_shapes=[pltpu.VMEM((SLOTS * 8, BS), F32)],
        compiler_params=pltpu.CompilerParams(vmem_limit_bytes=32 * 2**20),
        name="spread",
    )(forcing, north, south, edges)


def deal_kernel(lens, place, got, out, groups, hold, table):
    band, lon = place[0], place[1]
    odd = lax.rem(band, 2) == 1
    other = jnp.where(lon < 8, jnp.minimum(band + 1, NLAT - 1), jnp.maximum(band - 1, 0))
    other_odd = lax.rem(other, 2) == 1

    def fill(l, start):
        groups[pl.ds(pl.multiple_of(l * SLOTS, SLOTS), SLOTS)] = (
            got[l, TILE * 32 :, :].astype(F32).reshape(SLOTS, 8, BS)
        )
        count = lens[other, l]

        def slot(s, carry):
            at = start + s
            table[jnp.where(other_odd, NBB - 1 - at, at)] = l * SLOTS + s
            return carry

        lax.fori_loop(0, count, slot, 0)
        return start + count

    lax.fori_loop(0, NLON, fill, 0)
    lane32 = lanes_of((32, BS)) < 64
    lane8 = lanes_of((8, BS)) < 64
    row6 = lax.broadcasted_iota(jnp.int32, (8, BS), 0) == 6
    from_next = lanes_of((8, BS)) < 2 * EDGE_LANES

    def edges(k):
        at = pl.multiple_of(lax.rem(k, NLON) * SLOTS, SLOTS)
        return groups[pl.ds(at, SLOTS), 7, :]

    def block(c):
        tile, cb = c // TILE, lax.rem(c, TILE)
        rows = got[tile, pl.ds(pl.multiple_of(cb * 32, 32), 32), :].astype(F32)
        group = jnp.where(row6, groups[tile * SLOTS + cb], groups[table[c]])
        return rows, group

    def owner(k, start):
        count = lens[band, k]
        last = start + count - 1
        east = jnp.where(odd, NBB - 1 - start, last) + 1
        west = jnp.where(odd, NBB - 1 - last, start) - 1
        east, west = lax.rem(east, NBB), lax.rem(west + NBB, NBB)
        for e in range(SLOTS + 1):
            mine = e < count
            at = start + e
            column = jnp.where(odd, NBB - 1 - at, at)
            rows_a, group_a = block(jnp.where(mine, column, east))
            rows_b, group_b = block(jnp.where(mine, column, west))
            out[k, e * 32 : (e + 1) * 32, :] = jnp.where(lane32, rows_a, rows_b).astype(BF16)
            hold[e * 8 : (e + 1) * 8, :] = jnp.where(lane8, group_a, group_b)
        hold[72:80, :] = jnp.where(from_next, edges(k + 1), edges(k + NLON - 1))
        out[k, (SLOTS + 1) * 32 :, :] = hold[...].astype(BF16)
        return start + count

    lax.fori_loop(0, NLON, owner, 0)


def deal(lens, place, got):
    return pl.pallas_call(
        deal_kernel,
        out_shape=jax.ShapeDtypeStruct((NLON, M2_ROWS, BS), BF16),
        in_specs=[pl.BlockSpec(memory_space=pltpu.SMEM)] * 2
        + [pl.BlockSpec(memory_space=pltpu.VMEM)],
        out_specs=pl.BlockSpec(memory_space=pltpu.VMEM),
        scratch_shapes=[
            pltpu.VMEM((NLON * SLOTS, 8, BS), F32),
            pltpu.VMEM((80, BS), F32),
            pltpu.SMEM((NBB,), jnp.int32),
        ],
        compiler_params=pltpu.CompilerParams(vmem_limit_bytes=32 * 2**20),
        name="deal",
    )(lens, place, got)


def dynamics_kernel(
    lens, place, vel, stress, area, thick, got, coriolis,
    vel_out, stress_out, handed, st, edge, empty, sems,
):
    band, lon = place[0], place[1]
    odd = lax.rem(band, 2) == 1
    count = lens[band, lon]
    groups = BS // 8

    def rows_at(g):
        return pl.ds(g * 8 if isinstance(g, int) else pl.multiple_of(g * 8, 8), 8)

    def slot_lanes(slot):
        return pl.ds(pl.multiple_of(jnp.where(odd, SLOTS - 1 - slot, slot) * BS, BS), BS)

    edge_lanes = pl.ds(SLOTS * BS, BS)
    empty[...] = jnp.zeros(empty.shape, F32)

    def arrived(j, carry):
        for e in range(SLOTS + 1):
            rows = got[j, e * 32 : (e + 1) * 32, :].astype(F32)
            lanes = slot_lanes(e) if e < SLOTS else edge_lanes
            for f in range(4):
                st[UO + f, rows_at(j + 1), lanes] = rows[f * 8 : (f + 1) * 8, :]
        edge[rows_at(j), :] = got[j, M2_ROWS - 16 :, :].astype(F32)[8:16, :]
        return carry

    lax.fori_loop(0, NLON, arrived, 0)
    for j in range(NLON):
        group = got[j, (SLOTS + 1) * 32 :, :].astype(F32)
        f = j % 8
        row0 = TOP + BS if j < 8 else TOP - DEEP
        force_row = (TOP - 2, TOP - 1, TOP + BS, TOP + BS + 1)[j % 4]
        for e in range(SLOTS + 1):
            lanes = slot_lanes(e) if e < SLOTS else edge_lanes
            if f < ICE:
                st[f, row0 : row0 + DEEP, lanes] = (
                    group[8 * e : 8 * e + 3, :] + group[8 * e + 3 : 8 * e + 6, :]
                )
            st[UO + j // 4, force_row : force_row + 1, lanes] = group[8 * e + 6 : 8 * e + 7, :]

    def derived(conc, mass, g, lanes):
        turn = coriolis[rows_at(g), :]
        if conc.shape[1] > BS:
            turn = jnp.concatenate([turn] * (conc.shape[1] // BS), axis=1)
        st[STR, rows_at(g), lanes] = strength_of(conc, mass)
        st[TURN, rows_at(g), lanes] = turn * mass

    for g in (0, groups + 1):
        derived(st[AREA, rows_at(g), :], st[MASS, rows_at(g), :], g, slice(0, STRIP))

    def own_rows(j, carry):
        packed = edge[rows_at(j), :]
        packed = packed + pltpu.roll(packed, BS - EDGE_LANES, 1)
        at_zero = pltpu.roll(packed, BS - 2 * EDGE_LANES, 1)
        east = jnp.where(odd, at_zero, packed)
        west = jnp.where(odd, packed, at_zero)
        near = lanes_of((8, BS)) < 64
        beside = [
            jnp.where(
                near,
                pltpu.roll(east, (BS - 3 * f) % BS, 1),
                pltpu.roll(west, 125 - 3 * f, 1),
            )
            for f in range(ICE)
        ]
        rows = rows_at(j)
        for e in range(SLOTS + 1):
            if e == SLOTS:
                fields, lanes = beside, edge_lanes
            else:
                lanes = slot_lanes(e)
                at = slice(e * BS, (e + 1) * BS)
                fields = ice_fields(
                    [vel[n, rows, at] for n in range(2)],
                    [stress[n, rows, at] for n in range(3)],
                    [area[n, rows, at] for n in range(5)],
                    [thick[n, rows, at] for n in range(5)],
                )
                mine = jnp.broadcast_to(e < count, (8, BS))
                fields = [jnp.where(mine, fields[f], beside[f]) for f in range(ICE)]
            for f in range(ICE):
                st[f, rows_at(j + 1), lanes] = fields[f]
            derived(fields[AREA], fields[MASS], j + 1, lanes)
        return carry

    lax.fori_loop(0, groups, own_rows, 0)

    cells = (8, WIDE)
    row = lax.broadcasted_iota(jnp.int32, cells, 0)

    def load(f, g, c, width=WIDE):
        return st[f, rows_at(g), c : c + width]

    def north_of(f, x, g, c):
        return pltpu.roll(jnp.where(row == 0, load(f, g + 1, c), x), 7, 0)

    def south_of(f, x, g, c):
        return pltpu.roll(jnp.where(row == 7, load(f, max(g - 1, 0) if isinstance(g, int) else g - 1, c), x), 1, 0)

    def east_of(f, x, g, c):
        if WIDE == STRIP:
            return pltpu.roll(x, STRIP - 1, 1)
        more = load(f, g, (c + WIDE) % STRIP, BS)
        return pltpu.roll(jnp.concatenate([x, more], axis=1), WIDE + BS - 1, 1)[:, :WIDE]

    def west_of(f, x, g, c):
        if WIDE == STRIP:
            return pltpu.roll(x, 1, 1)
        more = load(f, g, (c - BS) % STRIP, BS)
        return pltpu.roll(jnp.concatenate([more, x], axis=1), 1, 1)[:, BS:]

    def stress_rows(g, last):
        for c in range(0, STRIP, WIDE):
            u, v = load(U, g, c), load(V, g, c)
            exx = east_of(U, u, g, c) - u
            eyy = north_of(V, v, g, c) - v
            shr = (north_of(U, u, g, c) - u) + (east_of(V, v, g, c) - v)
            div = exx + eyy
            ten = exx - eyy
            square = div * div + 0.25 * (ten * ten + shr * shr) + DMIN_SQ
            sixth = load(STR, g, c)
            half = sixth * lax.rsqrt(square)
            eighth = 0.25 * half
            both = half * div - sixth
            apart = eighth * ten
            sxx = (2.0 / 3.0) * load(SXX, g, c) + (both + apart)
            syy = (2.0 / 3.0) * load(SYY, g, c) + (both - apart)
            at = slice(c, c + WIDE)
            st[SXX, rows_at(g), at] = sxx
            st[SYY, rows_at(g), at] = syy
            st[S12, rows_at(g), at] = (2.0 / 3.0) * load(S12, g, c) + eighth * shr
            if last:
                st[STR, rows_at(g), at] = sxx + syy
                st[S2_OUT, rows_at(g), at] = sxx - syy

    def velocity_rows(g, beyond=None, last=False):
        for c in range(0, STRIP, WIDE):
            sxx, syy, s12 = load(SXX, g, c), load(SYY, g, c), load(S12, g, c)
            fx = sxx - west_of(SXX, sxx, g, c) + s12 - south_of(S12, s12, g, c)
            fy = s12 - west_of(S12, s12, g, c) + syy - south_of(SYY, syy, g, c)
            u, v, uo, vo = [load(f, g, c) for f in (U, V, UO, VO)]
            m, conc, tx, ty = [load(f, g, c) for f in (MASS, AREA, TX, TY)]
            du, dv = uo - u, vo - v
            square = du * du + dv * dv + SPEED_SQ
            drag = conc * (square * lax.rsqrt(square))
            d = m + drag
            q = load(TURN, g, c)
            ru = m * u + fx + tx + drag * uo
            rv = m * v + fy + ty + drag * vo
            inv = 1.0 / (d * d + q * q)
            u = (d * ru + q * rv) * inv
            v = (d * rv - q * ru) * inv
            if beyond is not None:
                mask = jnp.broadcast_to(beyond, cells)
                u = jnp.where(mask, 0.0, u)
                v = jnp.where(mask, 0.0, v)
            at = slice(c, c + WIDE)
            st[U, rows_at(g), at] = u
            st[V, rows_at(g), at] = v
            if last:
                du, dv = u - uo, v - vo
                square = du * du + dv * dv + SPEED_SQ
                drag = conc * (square * lax.rsqrt(square))
                x = (1.0 - conc) * tx + drag * du
                y = (1.0 - conc) * ty + drag * dv
                for i in range(WIDE // BS):
                    p = c // BS + i
                    if p < SLOTS:
                        slot = jnp.where(odd, SLOTS - 1 - p, p)
                        pair = [x[:, i * BS : (i + 1) * BS], y[:, i * BS : (i + 1) * BS]]
                        handed[g - 1, pl.ds(pl.multiple_of(slot * 16, 16), 16), :] = (
                            jnp.concatenate(pair, axis=0).astype(BF16)
                        )

    def copies(fields, out, row0, rows, sem0):
        made = []
        for n, f in enumerate(fields):
            for e in range(SLOTS):
                to = out.at[n, pl.ds(row0, rows), pl.ds(e * BS, BS)]
                sem = sems.at[sem0 + n * SLOTS + e]
                block = st.at[f, pl.ds(TOP + row0, rows), slot_lanes(e)]
                made.append((e, pltpu.make_async_copy(block, to, sem),
                             pltpu.make_async_copy(empty.at[pl.ds(0, rows), :], to, sem)))
        return made

    def start(made):
        for e, full, none in made:
            @pl.when(e < count)
            def _():
                full.start()

            @pl.when(e >= count)
            def _():
                none.start()

    pending = []
    for it in range(ITERS):
        last = it == ITERS - 1

        def stress_step(g, carry):
            stress_rows(g, last)
            return carry

        lax.fori_loop(0, groups + (1 if last else 2), stress_step, 0)
        if last:
            made = copies((STR, S2_OUT, S12), stress_out, 0, BS, 0)
            start(made)
            pending += made
        else:
            velocity_rows(0, band == 0)
            velocity_rows(groups + 1, band == NLAT - 1)

        def velocity_step(g, carry):
            velocity_rows(g, None, last)
            return carry

        if last:
            for h in range(2):
                lax.fori_loop(1 + h * groups // 2, 1 + (h + 1) * groups // 2, velocity_step, 0)
                made = copies((U, V), vel_out, h * BS // 2, BS // 2, 24 + 16 * h)
                start(made)
                pending += made
        else:
            lax.fori_loop(1, groups + 1, velocity_step, 0)
    for _, full, _ in pending:
        full.wait()


def dynamics(lens, place, vel, stress, area, thick, got, coriolis):
    width = SLOTS * BS
    vmem = pl.BlockSpec(memory_space=pltpu.VMEM)
    smem = pl.BlockSpec(memory_space=pltpu.SMEM)
    return pl.pallas_call(
        dynamics_kernel,
        in_specs=[smem, smem] + [vmem] * 6,
        out_specs=[pl.BlockSpec(memory_space=pl.ANY)] * 2 + [vmem],
        scratch_shapes=[
            pltpu.VMEM((14, ROWS + 8, STRIP), F32),
            pltpu.VMEM((BS, BS), F32),
            pltpu.VMEM((BS, BS), F32),
            pltpu.SemaphoreType.DMA((24 + 32,)),
        ],
        out_shape=[
            jax.ShapeDtypeStruct((2, BS, width), F32),
            jax.ShapeDtypeStruct((3, BS, width), F32),
            jax.ShapeDtypeStruct((NLON, M3_ROWS, BS), BF16),
        ],
        compiler_params=pltpu.CompilerParams(vmem_limit_bytes=32 * 2**20),
        name="dynamics",
    )(lens, place, vel, stress, area, thick, got, coriolis)


def sort_kernel(lens, place, got, out):
    band = place[0]
    odd = lax.rem(band, 2) == 1

    def owner(k, start):
        count = lens[band, k]

        def slot(s, carry):
            at = start + s
            out[jnp.where(odd, NBB - 1 - at, at)] = got[k * SLOTS + s]
            return carry

        lax.fori_loop(0, count, slot, 0)
        return start + count

    lax.fori_loop(0, NLON, owner, 0)


def sort_back(lens, place, got):
    return pl.pallas_call(
        sort_kernel,
        out_shape=jax.ShapeDtypeStruct((NBB, 16, BS), BF16),
        in_specs=[pl.BlockSpec(memory_space=pltpu.SMEM)] * 2
        + [pl.BlockSpec(memory_space=pltpu.VMEM)],
        out_specs=pl.BlockSpec(memory_space=pltpu.VMEM),
        name="sort_back",
    )(lens, place, got)


def settle_kernel(got, out):
    def rows16(pair, carry):
        rows = pl.ds(pl.multiple_of(pair * 16, 16), 16)
        for cb in range(TILE):
            a = got[2 * pair, cb * 16 : (cb + 1) * 16, :].astype(F32)
            b = got[2 * pair + 1, cb * 16 : (cb + 1) * 16, :].astype(F32)
            lanes = slice(cb * BS, (cb + 1) * BS)
            out[0, rows, lanes] = jnp.concatenate([a[0:8], b[0:8]], axis=0).astype(BF16)
            out[1, rows, lanes] = jnp.concatenate([a[8:16], b[8:16]], axis=0).astype(BF16)
        return carry

    lax.fori_loop(0, BS // 16, rows16, 0)


def settle(got):
    return pl.pallas_call(
        settle_kernel,
        out_shape=jax.ShapeDtypeStruct((2, BS, TILE * BS), BF16),
        in_specs=[pl.BlockSpec(memory_space=pltpu.VMEM)],
        out_specs=pl.BlockSpec(memory_space=pltpu.VMEM),
        name="settle",
    )(got)


def to_all(block):
    return lax.all_to_all(block, "lon", 0, 0, tiled=True)


def body(ocean_forcing, ice_velocity, ice_stress, cat_area, cat_thick, run_lengths):
    band_idx = lax.axis_index("lat")
    lon_idx = lax.axis_index("lon")
    lens = run_lengths
    place = jnp.stack([band_idx, lon_idx]).astype(jnp.int32)
    ice = (ice_velocity, ice_stress, cat_area, cat_thick)
    rows = (band_idx * BS + jnp.arange(-TOP, BS + TOP, dtype=jnp.int32)).astype(F32)
    latitude = -78.0 + 168.0 * (rows + 0.5) / (BS * NLAT)
    coriolis = jnp.broadcast_to(jnp.sin(latitude * (jnp.pi / 180.0))[:, None], (ROWS, BS))
    to_south, to_north, edges = make_edges(lens, place, *ice, ocean_forcing)
    north = lax.ppermute(to_south, "lat", [(b, b - 1) for b in range(1, NLAT)])
    south = lax.ppermute(to_north, "lat", [(b, b + 1) for b in range(NLAT - 1)])
    north, south, coriolis = lax.optimization_barrier((north, south, coriolis))
    message = spread(ocean_forcing, north, south, edges)
    dealt = to_all(deal(lens, place, to_all(message)))
    velocity_out, stress_out, handed = dynamics(lens, place, *ice, dealt, coriolis)
    handed = to_all(handed).reshape(NLON * SLOTS, 16, BS)
    back = sort_back(lens, place, handed).reshape(NLON, M4_ROWS, BS)
    return (velocity_out, stress_out, settle(to_all(back)))


def solution(mesh):
    slots = P(None, None, ("lat", "lon"))
    grid = P(None, "lat", "lon")
    return jax.shard_map(
        body,
        mesh=mesh,
        in_specs=(grid, slots, slots, slots, slots, P()),
        out_specs=(slots, slots, grid),
        check_vma=False,
    )
```

```python
import functools

import jax
import jax.numpy as jnp
from jax import lax
from jax.experimental import pallas as pl
from jax.experimental.pallas import tpu as pltpu
from jax.sharding import PartitionSpec as P

BS = 128
ITERS = 3
NLAT = 8
NLON = 16
SLOTS = 8
NBB = 64
TILE = 4
DEEP = 3
PSTAR = 2.0
CSTAR = 20.0
DMIN_SQ = 0.01
SPEED_SQ = 0.01
ICE = 7
U, V, SXX, SYY, S12, AREA, MASS, STR, UO, VO, TX, TY, TURN, S1_OUT, S2_OUT, U_NEW, V_NEW = range(17)
RENEWED = (U, V, SXX, SYY, S12)
EDGE_LANES = 3 * ICE
STRIP = (SLOTS + 1) * BS
UNROLL = 4
WIDE = 3 * BS
TOP = 8
ROWS = BS + 2 * TOP
SEND_ROWS = 32
M1_ROWS = TILE * 32 + SLOTS * 8
M2_ROWS = (SLOTS + 1) * 32 + 80
M3_ROWS = SLOTS * 16
M4_ROWS = TILE * 16
F32 = jnp.float32
BF16 = jnp.bfloat16


def lanes_of(shape):
    return lax.broadcasted_iota(jnp.int32, shape, len(shape) - 1)


def ice_fields(vel, stress, area, thick):
    conc = area[0] + area[1] + area[2] + area[3] + area[4]
    mass = area[0] * thick[0]
    for n in range(1, 5):
        mass = mass + area[n] * thick[n]
    sxx, syy = 0.5 * (stress[0] + stress[1]), 0.5 * (stress[0] - stress[1])
    return [vel[0], vel[1], sxx, syy, stress[2], conc, mass]


def strength_of(conc, mass):
    return (PSTAR / 6.0) * mass * jnp.exp(-CSTAR * (1.0 - conc))


def edges_kernel(lens, band, lon, *refs):
    ice = [refs[4 * i : 4 * i + 4] for i in range(4)]
    f_low, f_high, south, north, packed_out = refs[16:]
    odd = lax.rem(band[0], 2) == 1
    for out, which, force, row0, frow0 in (
        (south, 0, f_low, 0, 0),
        (north, 1, f_high, 5, 14),
    ):
        arrays = [ice[i][which] for i in range(4)]
        fields = ice_fields(*[[a[n] for n in range(a.shape[0])] for a in arrays])
        out[...] = jnp.zeros(out.shape, F32)
        for f in range(ICE):
            out[3 * f : 3 * f + 3, :] = fields[f][row0 : row0 + 3, :]
        for f in range(4):
            rows = force[f].astype(F32)
            out[21 + f : 22 + f, 0:512] = rows[frow0 : frow0 + 1, :]
            out[21 + f : 22 + f, 512:1024] = rows[frow0 + 1 : frow0 + 2, :]
    lane = lanes_of((BS, BS))
    packed = jnp.zeros((BS, BS), F32)
    for side, which, col_even, col_odd in ((0, 2, 0, 125), (1, 3, 125, 0)):
        arrays = [ice[i][which] for i in range(4)]
        fields = ice_fields(*[[a[n] for n in range(a.shape[0])] for a in arrays])
        for f in range(ICE):
            at = 2 * side * EDGE_LANES + 3 * f
            high = fields[f].astype(BF16).astype(F32)
            for part, there in ((high, at), (fields[f] - high, at + EDGE_LANES)):
                shift = jnp.where(odd, (there - col_odd) % BS, (there - col_even) % BS)
                moved = pltpu.roll(part, shift, 1)
                packed = jnp.where((lane >= there) & (lane < there + 3), moved, packed)
    packed_out[...] = packed


def make_edges(lens, band, lon, vel, stress, area, thick, forcing):
    width = SLOTS * BS

    def specs(n):
        return [
            pl.BlockSpec((n, 8, width), lambda i, lens, band, lon: (0, 0, 0)),
            pl.BlockSpec((n, 8, width), lambda i, lens, band, lon: (0, BS // 8 - 1, 0)),
            pl.BlockSpec((n, BS, BS), lambda i, lens, band, lon: (0, 0, 0)),
            pl.BlockSpec(
                (n, BS, BS),
                lambda i, lens, band, lon: (0, 0, lens[band[0], lon[0]] - 1),
            ),
        ]

    in_specs = specs(2) + specs(3) + specs(5) + specs(5)
    in_specs += [
        pl.BlockSpec((4, 16, 512), lambda i, lens, band, lon: (0, 0, 0)),
        pl.BlockSpec((4, 16, 512), lambda i, lens, band, lon: (0, BS // 16 - 1, 0)),
    ]
    whole = lambda i, lens, band, lon: (0, 0)
    return pl.pallas_call(
        edges_kernel,
        grid_spec=pltpu.PrefetchScalarGridSpec(
            num_scalar_prefetch=3,
            grid=(1,),
            in_specs=in_specs,
            out_specs=[
                pl.BlockSpec((SEND_ROWS, width), whole),
                pl.BlockSpec((SEND_ROWS, width), whole),
                pl.BlockSpec((BS, BS), whole),
            ],
        ),
        out_shape=[
            jax.ShapeDtypeStruct((SEND_ROWS, width), F32),
            jax.ShapeDtypeStruct((SEND_ROWS, width), F32),
            jax.ShapeDtypeStruct((BS, BS), F32),
        ],
        compiler_params=pltpu.CompilerParams(vmem_limit_bytes=60 * 2**20),
        name="edges",
    )(lens, band, lon, *([vel] * 4), *([stress] * 4), *([area] * 4), *([thick] * 4), forcing, forcing)


def spread_kernel(forcing, north, south, edges, out, hold):
    def rows16(pair, carry):
        base = pl.multiple_of(pair * 16, 16)
        for cb in range(TILE):
            parts = [
                forcing[f, pl.ds(base, 16), cb * BS : (cb + 1) * BS].astype(F32) for f in range(4)
            ]
            low = jnp.concatenate([p[0:8] for p in parts], axis=0)
            high = jnp.concatenate([p[8:16] for p in parts], axis=0)
            out[2 * pair, cb * 32 : (cb + 1) * 32, :] = low.astype(BF16)
            out[2 * pair + 1, cb * 32 : (cb + 1) * 32, :] = high.astype(BF16)
        return carry

    lax.fori_loop(0, BS // 16, rows16, 0)
    for j in range(NLON):
        hold[...] = jnp.zeros(hold.shape, F32)
        source = north if j < 8 else south
        f = j % 8
        if f < ICE:
            rows = source[3 * f : 3 * f + 3, :]
            high = rows.astype(BF16).astype(F32)
            low = rows - high
            for s in range(SLOTS):
                hold[8 * s : 8 * s + 3, :] = high[:, s * BS : (s + 1) * BS]
                hold[8 * s + 3 : 8 * s + 6, :] = low[:, s * BS : (s + 1) * BS]
        field, h = j // 4, j % 4
        source = south if h < 2 else north
        for cb in range(TILE):
            at = (h % 2) * 512 + cb * BS
            hold[8 * cb + 6 : 8 * cb + 7, :] = source[21 + field : 22 + field, at : at + BS]
        for s in range(SLOTS):
            hold[8 * s + 7 : 8 * s + 8, :] = edges[8 * j + s : 8 * j + s + 1, :]
        out[j, TILE * 32 :, :] = hold[...].astype(BF16)


def spread(forcing, north, south, edges):
    return pl.pallas_call(
        spread_kernel,
        out_shape=jax.ShapeDtypeStruct((NLON, M1_ROWS, BS), BF16),
        in_specs=[pl.BlockSpec(memory_space=pltpu.VMEM)] * 4,
        out_specs=pl.BlockSpec(memory_space=pltpu.VMEM),
        scratch_shapes=[pltpu.VMEM((SLOTS * 8, BS), F32)],
        compiler_params=pltpu.CompilerParams(vmem_limit_bytes=32 * 2**20),
        name="spread",
    )(forcing, north, south, edges)


def note_slots(table, k, count, start, odd):
    for s in range(SLOTS):
        at = start + s
        column = jnp.where(odd, NBB - 1 - at, at)
        table[jnp.where(s < count, column, NBB)] = k * SLOTS + s


def deal_kernel(lens, band, lon, got, out, groups, hold, table):
    band, lon = band[0], lon[0]
    odd = lax.rem(band, 2) == 1
    other = jnp.where(lon < 8, jnp.minimum(band + 1, NLAT - 1), jnp.maximum(band - 1, 0))
    other_odd = lax.rem(other, 2) == 1

    def fill(l, start):
        groups[pl.ds(pl.multiple_of(l * SLOTS, SLOTS), SLOTS)] = (
            got[l, TILE * 32 :, :].astype(F32).reshape(SLOTS, 8, BS)
        )
        note_slots(table, l, lens[other, l], start, other_odd)
        return start + lens[other, l]

    lax.fori_loop(0, NLON, fill, 0, unroll=UNROLL)
    lane32 = lanes_of((32, BS)) < 64
    lane8 = lanes_of((8, BS)) < 64
    row6 = lax.broadcasted_iota(jnp.int32, (8, BS), 0) == 6
    from_next = lanes_of((8, BS)) < 2 * EDGE_LANES

    def edges(k):
        at = pl.multiple_of(lax.rem(k, NLON) * SLOTS, SLOTS)
        return groups[pl.ds(at, SLOTS), 7, :]

    def block(c):
        tile, cb = c // TILE, lax.rem(c, TILE)
        rows = got[tile, pl.ds(pl.multiple_of(cb * 32, 32), 32), :].astype(F32)
        group = jnp.where(row6, groups[tile * SLOTS + cb], groups[table[c]])
        return rows, group

    def owner(k, start):
        count = lens[band, k]
        last = start + count - 1
        east = jnp.where(odd, NBB - 1 - start, last) + 1
        west = jnp.where(odd, NBB - 1 - last, start) - 1
        east, west = lax.rem(east, NBB), lax.rem(west + NBB, NBB)
        for e in range(SLOTS + 1):
            mine = e < count
            at = start + e
            column = jnp.where(odd, NBB - 1 - at, at)
            rows_a, group_a = block(jnp.where(mine, column, east))
            rows_b, group_b = block(jnp.where(mine, column, west))
            out[k, e * 32 : (e + 1) * 32, :] = jnp.where(lane32, rows_a, rows_b).astype(BF16)
            hold[e * 8 : (e + 1) * 8, :] = jnp.where(lane8, group_a, group_b)
        hold[72:80, :] = jnp.where(from_next, edges(k + 1), edges(k + NLON - 1))
        out[k, (SLOTS + 1) * 32 :, :] = hold[...].astype(BF16)
        return start + count

    lax.fori_loop(0, NLON, owner, 0, unroll=2)


def deal(lens, band, lon, got):
    return pl.pallas_call(
        deal_kernel,
        out_shape=jax.ShapeDtypeStruct((NLON, M2_ROWS, BS), BF16),
        in_specs=[pl.BlockSpec(memory_space=pltpu.SMEM)] * 3
        + [pl.BlockSpec(memory_space=pltpu.VMEM)],
        out_specs=pl.BlockSpec(memory_space=pltpu.VMEM),
        scratch_shapes=[
            pltpu.VMEM((NLON * SLOTS, 8, BS), F32),
            pltpu.VMEM((80, BS), F32),
            pltpu.SMEM((NBB + 1,), jnp.int32),
        ],
        compiler_params=pltpu.CompilerParams(vmem_limit_bytes=32 * 2**20),
        name="deal",
    )(lens, band, lon, got)


def dynamics_kernel(
    lens, band, lon, vel, stress, area, thick, got, coriolis,
    vel_out, stress_out, handed, *scratch,
):
    fields_at, (edge, empty, sems) = list(scratch[:-3]), scratch[-3:]
    band, lon = band[0], lon[0]
    odd = lax.rem(band, 2) == 1
    count = lens[band, lon]
    groups = BS // 8

    def rows_at(g):
        return pl.ds(g * 8 if isinstance(g, int) else pl.multiple_of(g * 8, 8), 8)

    def slot_lanes(slot):
        return pl.ds(pl.multiple_of(jnp.where(odd, SLOTS - 1 - slot, slot) * BS, BS), BS)

    edge_lanes = pl.ds(SLOTS * BS, BS)
    empty[...] = jnp.zeros(empty.shape, F32)

    def arrived(j, carry):
        for e in range(SLOTS + 1):
            rows = got[j, e * 32 : (e + 1) * 32, :].astype(F32)
            lanes = slot_lanes(e) if e < SLOTS else edge_lanes
            for f in range(4):
                fields_at[UO + f][rows_at(j + 1), lanes] = rows[f * 8 : (f + 1) * 8, :]
        edge[rows_at(j), :] = got[j, M2_ROWS - 16 :, :].astype(F32)[8:16, :]
        return carry

    lax.fori_loop(0, NLON, arrived, 0)
    for j in range(NLON):
        group = got[j, (SLOTS + 1) * 32 :, :].astype(F32)[0 : 8 * (SLOTS + 1), :]
        group = group.reshape(SLOTS + 1, 8, BS)
        whole = group + pltpu.roll(group, 5, 1)
        if j >= 8:
            whole = pltpu.roll(whole, 5, 1)
        f = j % 8
        g = groups + 1 if j < 8 else 0
        force_row = (TOP - 2, TOP - 1, TOP + BS, TOP + BS + 1)[j % 4]
        for e in range(SLOTS + 1):
            lanes = slot_lanes(e) if e < SLOTS else edge_lanes
            if f < ICE:
                fields_at[f][rows_at(g), lanes] = whole[e]
            fields_at[UO + j // 4][force_row : force_row + 1, lanes] = group[e, 6:7, :]

    def derived(conc, mass, g, lanes):
        turn = coriolis[rows_at(g), :]
        if conc.shape[1] > BS:
            turn = jnp.concatenate([turn] * (conc.shape[1] // BS), axis=1)
        fields_at[STR][rows_at(g), lanes] = strength_of(conc, mass)
        fields_at[TURN][rows_at(g), lanes] = turn * mass

    for g in (0, groups + 1):
        derived(fields_at[AREA][rows_at(g), :], fields_at[MASS][rows_at(g), :], g, slice(0, STRIP))

    def own_rows(j, carry):
        packed = edge[rows_at(j), :]
        packed = packed + pltpu.roll(packed, BS - EDGE_LANES, 1)
        at_zero = pltpu.roll(packed, BS - 2 * EDGE_LANES, 1)
        east = jnp.where(odd, at_zero, packed)
        west = jnp.where(odd, packed, at_zero)
        near = lanes_of((8, BS)) < 64
        beside = [
            jnp.where(
                near,
                pltpu.roll(east, (BS - 3 * f) % BS, 1),
                pltpu.roll(west, 125 - 3 * f, 1),
            )
            for f in range(ICE)
        ]
        rows = rows_at(j)
        for e in range(SLOTS + 1):
            if e == SLOTS:
                fields, lanes = beside, edge_lanes
            else:
                lanes = slot_lanes(e)
                at = slice(e * BS, (e + 1) * BS)
                fields = ice_fields(
                    [vel[n, rows, at] for n in range(2)],
                    [stress[n, rows, at] for n in range(3)],
                    [area[n, rows, at] for n in range(5)],
                    [thick[n, rows, at] for n in range(5)],
                )
                mine = jnp.broadcast_to(e < count, (8, BS))
                fields = [jnp.where(mine, fields[f], beside[f]) for f in range(ICE)]
            for f in range(ICE):
                fields_at[f][rows_at(j + 1), lanes] = fields[f]
            derived(fields[AREA], fields[MASS], j + 1, lanes)
        return carry

    lax.fori_loop(0, groups, own_rows, 0, unroll=UNROLL)

    cells = (8, WIDE)
    row = lax.broadcasted_iota(jnp.int32, cells, 0)

    def load(f, g, c, width=WIDE):
        return fields_at[f][rows_at(g), c : c + width]

    def north_of(f, x, g, c):
        return pltpu.roll(jnp.where(row == 0, load(f, g + 1, c), x), 7, 0)

    def south_of(f, x, g, c):
        return pltpu.roll(jnp.where(row == 7, load(f, max(g - 1, 0) if isinstance(g, int) else g - 1, c), x), 1, 0)

    def east_of(f, x, g, c):
        if WIDE == STRIP:
            return pltpu.roll(x, STRIP - 1, 1)
        more = load(f, g, (c + WIDE) % STRIP, BS)
        return pltpu.roll(jnp.concatenate([x, more], axis=1), WIDE + BS - 1, 1)[:, :WIDE]

    def west_of(f, x, g, c):
        if WIDE == STRIP:
            return pltpu.roll(x, 1, 1)
        more = load(f, g, (c - BS) % STRIP, BS)
        return pltpu.roll(jnp.concatenate([more, x], axis=1), 1, 1)[:, BS:]

    def stress_rows(g, new, last):
        for c in range(0, STRIP, WIDE):
            u, v = load(U, g, c), load(V, g, c)
            exx = east_of(U, u, g, c) - u
            eyy = north_of(V, v, g, c) - v
            shr = (north_of(U, u, g, c) - u) + (east_of(V, v, g, c) - v)
            div = exx + eyy
            ten = exx - eyy
            square = div * div + 0.25 * (ten * ten + shr * shr) + DMIN_SQ
            sixth = load(STR, g, c)
            half = sixth * lax.rsqrt(square)
            eighth = 0.25 * half
            both = half * div - sixth
            apart = eighth * ten
            sxx = (2.0 / 3.0) * load(SXX, g, c) + (both + apart)
            syy = (2.0 / 3.0) * load(SYY, g, c) + (both - apart)
            at = slice(c, c + WIDE)
            new[SXX][rows_at(g), at] = sxx
            new[SYY][rows_at(g), at] = syy
            new[S12][rows_at(g), at] = (2.0 / 3.0) * load(S12, g, c) + eighth * shr
            if last:
                new[S1_OUT][rows_at(g), at] = sxx + syy
                new[S2_OUT][rows_at(g), at] = sxx - syy

    def velocity_rows(g, new, beyond=None, last=False):
        for c in range(0, STRIP, WIDE):
            sxx, syy, s12 = load(SXX, g, c), load(SYY, g, c), load(S12, g, c)
            fx = sxx - west_of(SXX, sxx, g, c) + s12 - south_of(S12, s12, g, c)
            fy = s12 - west_of(S12, s12, g, c) + syy - south_of(SYY, syy, g, c)
            u, v, uo, vo = [load(f, g, c) for f in (U, V, UO, VO)]
            m, conc, tx, ty = [load(f, g, c) for f in (MASS, AREA, TX, TY)]
            du, dv = uo - u, vo - v
            square = du * du + dv * dv + SPEED_SQ
            drag = conc * (square * lax.rsqrt(square))
            d = m + drag
            q = load(TURN, g, c)
            ru = m * u + fx + tx + drag * uo
            rv = m * v + fy + ty + drag * vo
            inv = 1.0 / (d * d + q * q)
            u = (d * ru + q * rv) * inv
            v = (d * rv - q * ru) * inv
            if beyond is not None:
                mask = jnp.broadcast_to(beyond, cells)
                u = jnp.where(mask, 0.0, u)
                v = jnp.where(mask, 0.0, v)
            at = slice(c, c + WIDE)
            new[U][rows_at(g), at] = u
            new[V][rows_at(g), at] = v
            if last:
                du, dv = u - uo, v - vo
                square = du * du + dv * dv + SPEED_SQ
                drag = conc * (square * lax.rsqrt(square))
                x = (1.0 - conc) * tx + drag * du
                y = (1.0 - conc) * ty + drag * dv
                for i in range(WIDE // BS):
                    p = c // BS + i
                    if p < SLOTS:
                        slot = jnp.where(odd, SLOTS - 1 - p, p)
                        pair = [x[:, i * BS : (i + 1) * BS], y[:, i * BS : (i + 1) * BS]]
                        handed[g - 1, pl.ds(pl.multiple_of(slot * 16, 16), 16), :] = (
                            jnp.concatenate(pair, axis=0).astype(BF16)
                        )

    def copies(fields, out, row0, rows, sem0):
        made = []
        for n, f in enumerate(fields):
            for e in range(SLOTS):
                to = out.at[n, pl.ds(row0, rows), pl.ds(e * BS, BS)]
                sem = sems.at[sem0 + n * SLOTS + e]
                block = fields_at[f].at[pl.ds(TOP + row0, rows), slot_lanes(e)]
                made.append((e, pltpu.make_async_copy(block, to, sem),
                             pltpu.make_async_copy(empty.at[pl.ds(0, rows), :], to, sem)))
        return made

    def start(made):
        for e, full, none in made:
            @pl.when(e < count)
            def _():
                full.start()

            @pl.when(e >= count)
            def _():
                none.start()

    pending = []
    for it in range(ITERS):
        last = it == ITERS - 1
        new = {f: fields_at[n] for f, n in zip(RENEWED, range(S2_OUT + 1, S2_OUT + 6))}
        new[S1_OUT], new[S2_OUT] = fields_at[S1_OUT], fields_at[S2_OUT]

        def stress_step(g, carry):
            stress_rows(g, new, last)
            return carry

        lax.fori_loop(0, groups + (1 if last else 2), stress_step, 0, unroll=UNROLL)
        for f in (SXX, SYY, S12):
            n = S2_OUT + 1 + RENEWED.index(f)
            fields_at[f], fields_at[n] = fields_at[n], fields_at[f]
        if last:
            made = copies((S1_OUT, S2_OUT, S12), stress_out, 0, BS, 0)
            start(made)
            pending += made
        else:
            velocity_rows(0, new, band == 0)
            velocity_rows(groups + 1, new, band == NLAT - 1)

        def velocity_step(g, carry):
            velocity_rows(g, new, None, last)
            return carry

        if last:
            for h in range(2):
                half = groups // 2
                lax.fori_loop(1 + h * half, 1 + (h + 1) * half, velocity_step, 0, unroll=UNROLL)
                made = copies((U_NEW, V_NEW), vel_out, h * BS // 2, BS // 2, 24 + 16 * h)
                start(made)
                pending += made
        else:
            lax.fori_loop(1, groups + 1, velocity_step, 0, unroll=UNROLL)
            for f in (U, V):
                n = S2_OUT + 1 + RENEWED.index(f)
                fields_at[f], fields_at[n] = fields_at[n], fields_at[f]
    for _, full, _ in pending:
        full.wait()


def dynamics(lens, band, lon, vel, stress, area, thick, got, coriolis):
    width = SLOTS * BS
    vmem = pl.BlockSpec(memory_space=pltpu.VMEM)
    smem = pl.BlockSpec(memory_space=pltpu.SMEM)
    return pl.pallas_call(
        dynamics_kernel,
        in_specs=[smem] * 3 + [vmem] * 6,
        out_specs=[pl.BlockSpec(memory_space=pl.ANY)] * 2 + [vmem],
        scratch_shapes=[
            *[pltpu.VMEM((ROWS + 8, STRIP), F32) for _ in range(S2_OUT + 6)],
            pltpu.VMEM((BS, BS), F32),
            pltpu.VMEM((BS, BS), F32),
            pltpu.SemaphoreType.DMA((24 + 32,)),
        ],
        out_shape=[
            jax.ShapeDtypeStruct((2, BS, width), F32),
            jax.ShapeDtypeStruct((3, BS, width), F32),
            jax.ShapeDtypeStruct((NLON, M3_ROWS, BS), BF16),
        ],
        compiler_params=pltpu.CompilerParams(vmem_limit_bytes=32 * 2**20),
        name="dynamics",
    )(lens, band, lon, vel, stress, area, thick, got, coriolis)


def sort_kernel(lens, band, got, out, table):
    odd = lax.rem(band[0], 2) == 1

    def owner(k, start):
        note_slots(table, k, lens[band[0], k], start, odd)
        return start + lens[band[0], k]

    lax.fori_loop(0, NLON, owner, 0, unroll=UNROLL)

    def block(c, carry):
        out[c] = got[table[c]]
        return carry

    lax.fori_loop(0, NBB, block, 0, unroll=8)


def sort_back(lens, band, got):
    return pl.pallas_call(
        sort_kernel,
        out_shape=jax.ShapeDtypeStruct((NBB, 16, BS), BF16),
        in_specs=[pl.BlockSpec(memory_space=pltpu.SMEM)] * 2
        + [pl.BlockSpec(memory_space=pltpu.VMEM)],
        out_specs=pl.BlockSpec(memory_space=pltpu.VMEM),
        scratch_shapes=[pltpu.SMEM((NBB + 1,), jnp.int32)],
        compiler_params=pltpu.CompilerParams(vmem_limit_bytes=16 * 2**20),
        name="sort_back",
    )(lens, band, got)


def settle_kernel(got, out):
    def rows16(pair, carry):
        rows = pl.ds(pl.multiple_of(pair * 16, 16), 16)
        for cb in range(TILE):
            a = got[2 * pair, cb * 16 : (cb + 1) * 16, :].astype(F32)
            b = got[2 * pair + 1, cb * 16 : (cb + 1) * 16, :].astype(F32)
            lanes = slice(cb * BS, (cb + 1) * BS)
            out[0, rows, lanes] = jnp.concatenate([a[0:8], b[0:8]], axis=0).astype(BF16)
            out[1, rows, lanes] = jnp.concatenate([a[8:16], b[8:16]], axis=0).astype(BF16)
        return carry

    lax.fori_loop(0, BS // 16, rows16, 0, unroll=UNROLL)


def settle(got):
    return pl.pallas_call(
        settle_kernel,
        out_shape=jax.ShapeDtypeStruct((2, BS, TILE * BS), BF16),
        in_specs=[pl.BlockSpec(memory_space=pltpu.VMEM)],
        out_specs=pl.BlockSpec(memory_space=pltpu.VMEM),
        compiler_params=pltpu.CompilerParams(vmem_limit_bytes=16 * 2**20),
        name="settle",
    )(got)


def to_all(block):
    return lax.all_to_all(block, "lon", 0, 0, tiled=True)


def body(ocean_forcing, ice_velocity, ice_stress, cat_area, cat_thick, run_lengths):
    band_idx = lax.axis_index("lat")
    lon_idx = lax.axis_index("lon")
    lens = run_lengths
    place = (jnp.reshape(band_idx, (1,)), jnp.reshape(lon_idx, (1,)))
    ice = (ice_velocity, ice_stress, cat_area, cat_thick)
    rows = (band_idx * BS + jnp.arange(-TOP, BS + TOP, dtype=jnp.int32)).astype(F32)
    latitude = -78.0 + 168.0 * (rows + 0.5) / (BS * NLAT)
    coriolis = jnp.broadcast_to(jnp.sin(latitude * (jnp.pi / 180.0))[:, None], (ROWS, BS))
    to_south, to_north, edges = make_edges(lens, *place, *ice, ocean_forcing)
    north = lax.ppermute(to_south, "lat", [(b, b - 1) for b in range(1, NLAT)])
    south = lax.ppermute(to_north, "lat", [(b, b + 1) for b in range(NLAT - 1)])
    north, south, coriolis = lax.optimization_barrier((north, south, coriolis))
    message = spread(ocean_forcing, north, south, edges)
    dealt = to_all(deal(lens, *place, to_all(message)))
    velocity_out, stress_out, handed = dynamics(lens, *place, *ice, dealt, coriolis)
    handed = to_all(handed).reshape(NLON * SLOTS, 16, BS)
    back = sort_back(lens, place[0], handed).reshape(NLON, M4_ROWS, BS)
    return (velocity_out, stress_out, settle(to_all(back)))


def solution(mesh):
    slots = P(None, None, ("lat", "lon"))
    grid = P(None, "lat", "lon")
    return jax.shard_map(
        body,
        mesh=mesh,
        in_specs=(grid, slots, slots, slots, slots, P()),
        out_specs=(slots, slots, grid),
        check_vma=False,
    )
```

```python
import functools

import jax
import jax.numpy as jnp
from jax import lax
from jax.experimental import pallas as pl
from jax.experimental.pallas import tpu as pltpu
from jax.sharding import PartitionSpec as P

BS = 128
ITERS = 3
NLAT = 8
NLON = 16
SLOTS = 8
NBB = 64
TILE = 4
DEEP = 3
PSTAR = 2.0
CSTAR = 20.0
DMIN_SQ = 0.01
SPEED_SQ = 0.01
ICE = 7
U, V, SXX, SYY, S12, AREA, MASS, STR, UO, VO, TX, TY, TURN, S1_OUT, S2_OUT, U_NEW, V_NEW = range(17)
RENEWED = (U, V, SXX, SYY, S12)
EDGE_LANES = 3 * ICE
EAST_AT = 4 * EDGE_LANES
WEST_AT = EAST_AT + 12
STRIP = (SLOTS + 1) * BS
UNROLL = 4
UNROLL_OWN = 8
UNROLL_STRESS = 9
UNROLL_VELOCITY = 8
WIDE = 3 * BS
TOP = 8
ROWS = BS + 2 * TOP
SEND_ROWS = 32
M1_ROWS = TILE * 32 + SLOTS * 8
M2_ROWS = SLOTS * 32 + (SLOTS + 1) * 8 + 8
M3_ROWS = SLOTS * 16
M4_ROWS = TILE * 16
F32 = jnp.float32
BF16 = jnp.bfloat16


def lanes_of(shape):
    return lax.broadcasted_iota(jnp.int32, shape, len(shape) - 1)


def ice_fields(vel, stress, area, thick):
    conc = area[0] + area[1] + area[2] + area[3] + area[4]
    mass = area[0] * thick[0]
    for n in range(1, 5):
        mass = mass + area[n] * thick[n]
    sxx, syy = 0.5 * (stress[0] + stress[1]), 0.5 * (stress[0] - stress[1])
    return [vel[0], vel[1], sxx, syy, stress[2], conc, mass]


def strength_of(conc, mass):
    return (PSTAR / 6.0) * mass * jnp.exp(-CSTAR * (1.0 - conc))


def rows_kernel(*refs):
    ice = [refs[2 * i : 2 * i + 2] for i in range(4)]
    f_low, f_high, south, north = refs[8:]
    for out, which, force, row0, frow0 in (
        (south, 0, f_low, 0, 0),
        (north, 1, f_high, 5, 14),
    ):
        arrays = [ice[i][which] for i in range(4)]
        fields = ice_fields(*[[a[n] for n in range(a.shape[0])] for a in arrays])
        out[...] = jnp.zeros(out.shape, F32)
        for f in range(ICE):
            out[3 * f : 3 * f + 3, :] = fields[f][row0 : row0 + 3, :]
        for f in range(4):
            rows = force[f].astype(F32)
            out[21 + f : 22 + f, 0:512] = rows[frow0 : frow0 + 1, :]
            out[21 + f : 22 + f, 512:1024] = rows[frow0 + 1 : frow0 + 2, :]


def edge_rows(vel, stress, area, thick, forcing):
    width = SLOTS * BS

    def specs(n):
        return [
            pl.BlockSpec((n, 8, width), lambda i: (0, 0, 0)),
            pl.BlockSpec((n, 8, width), lambda i: (0, BS // 8 - 1, 0)),
        ]

    in_specs = specs(2) + specs(3) + specs(5) + specs(5)
    in_specs += [
        pl.BlockSpec((4, 16, 512), lambda i: (0, 0, 0)),
        pl.BlockSpec((4, 16, 512), lambda i: (0, BS // 16 - 1, 0)),
    ]
    return pl.pallas_call(
        rows_kernel,
        grid=(1,),
        in_specs=in_specs,
        out_specs=[pl.BlockSpec((SEND_ROWS, width), lambda i: (0, 0))] * 2,
        out_shape=[jax.ShapeDtypeStruct((SEND_ROWS, width), F32)] * 2,
        compiler_params=pltpu.CompilerParams(vmem_limit_bytes=60 * 2**20),
        name="edge_rows",
    )(*([vel] * 2), *([stress] * 2), *([area] * 2), *([thick] * 2), forcing, forcing)


def columns_kernel(lens, band, lon, vel, stress, area, thick, packed_out, blocks, sems):
    odd = lax.rem(band[0], 2) == 1
    last = pl.multiple_of((lens[band[0], lon[0]] - 1) * BS, BS)
    made = []
    for side, at in ((0, 0), (1, last)):
        n = 0
        for ref in (vel, stress, area, thick):
            for m in range(ref.shape[0]):
                made.append(
                    pltpu.make_async_copy(
                        ref.at[m, :, pl.ds(at, BS)], blocks.at[side, n], sems.at[side, n]
                    )
                )
                n += 1
    for copy in made:
        copy.start()
    lane = lanes_of((BS, BS))
    total = jnp.zeros((BS, BS), F32)
    for side in range(2):
        for copy in made[15 * side : 15 * side + 15]:
            copy.wait()
        held = [blocks[side, n] for n in range(15)]
        fields = ice_fields(held[0:2], held[2:5], held[5:10], held[10:15])
        first_columns = jnp.broadcast_to(odd if side else jnp.logical_not(odd), (BS, BS))
        packed = jnp.zeros((BS, BS), F32)
        for f in range(ICE):
            at_zero = jnp.where(first_columns, fields[f], pltpu.roll(fields[f], 3, 1))
            moved = pltpu.roll(at_zero, 3 * f, 1) if f else at_zero
            packed = jnp.where((lane >= 3 * f) & (lane < 3 * f + 3), moved, packed)
        high = packed.astype(BF16).astype(F32)
        both = high + pltpu.roll(packed - high, EDGE_LANES, 1)
        total = total + (pltpu.roll(both, 2 * EDGE_LANES, 1) if side else both)
    packed_out[...] = total


def edge_columns(lens, band, lon, vel, stress, area, thick):
    return pl.pallas_call(
        columns_kernel,
        in_specs=[pl.BlockSpec(memory_space=pltpu.SMEM)] * 3
        + [pl.BlockSpec(memory_space=pl.ANY)] * 4,
        out_specs=pl.BlockSpec(memory_space=pltpu.VMEM),
        out_shape=jax.ShapeDtypeStruct((BS, BS), F32),
        scratch_shapes=[pltpu.VMEM((2, 15, BS, BS), F32), pltpu.SemaphoreType.DMA((2, 15))],
        compiler_params=pltpu.CompilerParams(vmem_limit_bytes=60 * 2**20),
        name="edge_columns",
    )(lens, band, lon, vel, stress, area, thick)


def spread_kernel(forcing, north, south, edges_in, out, hold, edges, sem):
    fetch = pltpu.make_async_copy(edges_in, edges, sem)
    fetch.start()

    def rows16(pair, carry):
        base = pl.multiple_of(pair * 16, 16)
        for cb in range(TILE):
            parts = [
                forcing[f, pl.ds(base, 16), cb * BS : (cb + 1) * BS].astype(F32) for f in range(4)
            ]
            low = jnp.concatenate([p[0:8] for p in parts], axis=0)
            high = jnp.concatenate([p[8:16] for p in parts], axis=0)
            out[2 * pair, cb * 32 : (cb + 1) * 32, :] = low.astype(BF16)
            out[2 * pair + 1, cb * 32 : (cb + 1) * 32, :] = high.astype(BF16)
        return carry

    lax.fori_loop(0, BS // 16, rows16, 0, unroll=2)
    fetch.wait()
    for j in range(NLON):
        hold[...] = jnp.zeros(hold.shape, F32)
        source = north if j < 8 else south
        f = j % 8
        if f < ICE:
            rows = source[3 * f : 3 * f + 3, :]
            high = rows.astype(BF16).astype(F32)
            low = rows - high
            for s in range(SLOTS):
                hold[8 * s : 8 * s + 3, :] = high[:, s * BS : (s + 1) * BS]
                hold[8 * s + 3 : 8 * s + 6, :] = low[:, s * BS : (s + 1) * BS]
        field, h = j // 4, j % 4
        source = south if h < 2 else north
        for cb in range(TILE):
            at = (h % 2) * 512 + cb * BS
            hold[8 * cb + 6 : 8 * cb + 7, :] = source[21 + field : 22 + field, at : at + BS]
        for s in range(SLOTS):
            hold[8 * s + 7 : 8 * s + 8, :] = edges[8 * j + s : 8 * j + s + 1, :]
        out[j, TILE * 32 :, :] = hold[...].astype(BF16)


def spread(forcing, north, south, edges):
    return pl.pallas_call(
        spread_kernel,
        out_shape=jax.ShapeDtypeStruct((NLON, M1_ROWS, BS), BF16),
        in_specs=[pl.BlockSpec(memory_space=pltpu.VMEM)] * 3
        + [pl.BlockSpec(memory_space=pl.ANY)],
        out_specs=pl.BlockSpec(memory_space=pltpu.VMEM),
        scratch_shapes=[
            pltpu.VMEM((SLOTS * 8, BS), F32),
            pltpu.VMEM((BS, BS), F32),
            pltpu.SemaphoreType.DMA,
        ],
        compiler_params=pltpu.CompilerParams(vmem_limit_bytes=32 * 2**20),
        name="spread",
    )(forcing, north, south, edges)


def note_slots(table, k, count, start, odd):
    for s in range(SLOTS):
        at = start + s
        column = jnp.where(odd, NBB - 1 - at, at)
        table[jnp.where(s < count, column, NBB)] = k * SLOTS + s


def deal_kernel(lens, band, lon, got, out, groups, halos, table):
    band, lon = band[0], lon[0]
    odd = lax.rem(band, 2) == 1
    other = jnp.where(lon < 8, jnp.minimum(band + 1, NLAT - 1), jnp.maximum(band - 1, 0))
    other_odd = lax.rem(other, 2) == 1

    def fill(l, start):
        groups[pl.ds(pl.multiple_of(l * SLOTS, SLOTS), SLOTS)] = (
            got[l, TILE * 32 :, :].astype(F32).reshape(SLOTS, 8, BS)
        )
        note_slots(table, l, lens[other, l], start, other_odd)
        return start + lens[other, l]

    lax.fori_loop(0, NLON, fill, 0, unroll=UNROLL)
    row6 = lax.broadcasted_iota(jnp.int32, (8, BS), 0) == 6

    def halo(c, carry):
        own = (c // TILE) * SLOTS + lax.rem(c, TILE)
        halos[c] = jnp.where(row6, groups[own], groups[table[c]])
        return carry

    lax.fori_loop(0, NBB, halo, 0, unroll=8)
    lane = lanes_of((8, BS))

    def column_at(p):
        p = jnp.minimum(p, NBB - 1)
        return jnp.where(odd, NBB - 1 - p, p)

    def forcing(c):
        at = pl.multiple_of(lax.rem(c, TILE) * 32, 32)
        return got[c // TILE, pl.ds(at, 32), :]

    def edges(k):
        at = pl.multiple_of(lax.rem(k, NLON) * SLOTS, SLOTS)
        return groups[pl.ds(at, SLOTS), 7, :]

    def owner(k, start):
        count = lens[band, k]
        last = start + count - 1
        east = jnp.where(odd, NBB - 1 - start, last) + 1
        west = jnp.where(odd, NBB - 1 - last, start) - 1
        east, west = lax.rem(east, NBB), lax.rem(west + NBB, NBB)
        parts = []
        for e in range(SLOTS):
            c = column_at(start + e)
            out[k, e * 32 : (e + 1) * 32, :] = forcing(c)
            parts.append(halos[c])
        parts.append(jnp.where(lane < 64, halos[east], halos[west]))
        side = jnp.where(lane < 2 * EDGE_LANES, edges(k + 1), edges(k + NLON - 1))
        by_east, by_west = forcing(east).astype(F32), forcing(west).astype(F32)
        for f in range(4):
            for rows, at, col in ((by_east, EAST_AT, 0), (by_west, WEST_AT, 125)):
                there = at + 3 * f
                moved = pltpu.roll(rows[8 * f : 8 * f + 8, :], (there - col) % BS, 1)
                side = jnp.where((lane >= there) & (lane < there + 3), moved, side)
        parts.append(side)
        out[k, SLOTS * 32 :, :] = jnp.concatenate(parts, axis=0).astype(BF16)
        return start + count

    lax.fori_loop(0, NLON, owner, 0, unroll=4)


def deal(lens, band, lon, got):
    return pl.pallas_call(
        deal_kernel,
        out_shape=jax.ShapeDtypeStruct((NLON, M2_ROWS, BS), BF16),
        in_specs=[pl.BlockSpec(memory_space=pltpu.SMEM)] * 3
        + [pl.BlockSpec(memory_space=pltpu.VMEM)],
        out_specs=pl.BlockSpec(memory_space=pltpu.VMEM),
        scratch_shapes=[
            pltpu.VMEM((NLON * SLOTS, 8, BS), F32),
            pltpu.VMEM((NBB, 8, BS), F32),
            pltpu.SMEM((NBB + 1,), jnp.int32),
        ],
        compiler_params=pltpu.CompilerParams(vmem_limit_bytes=32 * 2**20),
        name="deal",
    )(lens, band, lon, got)


def dynamics_kernel(
    lens, band, lon, vel, stress, area, thick, got, coriolis,
    vel_out, stress_out, handed, *scratch,
):
    fields_at, (empty, sems) = list(scratch[:-2]), scratch[-2:]
    band, lon = band[0], lon[0]
    odd = lax.rem(band, 2) == 1
    count = lens[band, lon]
    groups = BS // 8

    def rows_at(g):
        return pl.ds(g * 8 if isinstance(g, int) else pl.multiple_of(g * 8, 8), 8)

    def slot_lanes(slot):
        return pl.ds(pl.multiple_of(jnp.where(odd, SLOTS - 1 - slot, slot) * BS, BS), BS)

    edge_lanes = pl.ds(SLOTS * BS, BS)
    empty[...] = jnp.zeros(empty.shape, F32)

    for j in range(NLON):
        group = got[j, SLOTS * 32 : SLOTS * 32 + 8 * (SLOTS + 1), :].astype(F32)
        group = group.reshape(SLOTS + 1, 8, BS)
        whole = group + pltpu.roll(group, 5, 1)
        if j >= 8:
            whole = pltpu.roll(whole, 5, 1)
        f = j % 8
        g = groups + 1 if j < 8 else 0
        force_row = (TOP - 2, TOP - 1, TOP + BS, TOP + BS + 1)[j % 4]
        for e in range(SLOTS + 1):
            lanes = slot_lanes(e) if e < SLOTS else edge_lanes
            mine = jnp.broadcast_to(e < count, (8, BS))
            if f < ICE:
                fields_at[f][rows_at(g), lanes] = jnp.where(mine, whole[e], whole[SLOTS])
            rows = jnp.where(mine, group[e], group[SLOTS])
            fields_at[UO + j // 4][force_row : force_row + 1, lanes] = rows[6:7, :]

    def derived(conc, mass, g, lanes):
        turn = coriolis[rows_at(g), :]
        if conc.shape[1] > BS:
            turn = jnp.concatenate([turn] * (conc.shape[1] // BS), axis=1)
        fields_at[STR][rows_at(g), lanes] = strength_of(conc, mass)
        fields_at[TURN][rows_at(g), lanes] = turn * mass

    for g in (0, groups + 1):
        derived(fields_at[AREA][rows_at(g), :], fields_at[MASS][rows_at(g), :], g, slice(0, STRIP))

    def own_rows(j, carry):
        packed = got[j, M2_ROWS - 16 :, :].astype(F32)[8:16, :]
        near = lanes_of((8, BS)) < 64

        def joined(east, east_lane, west, west_lane):
            return jnp.where(
                near,
                pltpu.roll(east, (BS - east_lane) % BS, 1),
                pltpu.roll(west, (125 - west_lane) % BS, 1),
            )

        forced = [joined(packed, EAST_AT + 3 * f, packed, WEST_AT + 3 * f) for f in range(4)]
        packed = packed + pltpu.roll(packed, BS - EDGE_LANES, 1)
        at_zero = pltpu.roll(packed, BS - 2 * EDGE_LANES, 1)
        east = jnp.where(odd, at_zero, packed)
        west = jnp.where(odd, packed, at_zero)
        beside = [joined(east, 3 * f, west, 3 * f) for f in range(ICE)]
        rows = rows_at(j)
        for e in range(SLOTS + 1):
            if e == SLOTS:
                fields, lanes = beside, edge_lanes
            else:
                lanes = slot_lanes(e)
                at = slice(e * BS, (e + 1) * BS)
                fields = ice_fields(
                    [vel[n, rows, at] for n in range(2)],
                    [stress[n, rows, at] for n in range(3)],
                    [area[n, rows, at] for n in range(5)],
                    [thick[n, rows, at] for n in range(5)],
                )
                mine = jnp.broadcast_to(e < count, (8, BS))
                fields = [jnp.where(mine, fields[f], beside[f]) for f in range(ICE)]
            force = forced
            if e < SLOTS:
                force = got[j, e * 32 : (e + 1) * 32, :].astype(F32)
                force = [jnp.where(mine, force[8 * f : 8 * f + 8], forced[f]) for f in range(4)]
            for f in range(4):
                fields_at[UO + f][rows_at(j + 1), lanes] = force[f]
            for f in range(ICE):
                fields_at[f][rows_at(j + 1), lanes] = fields[f]
            derived(fields[AREA], fields[MASS], j + 1, lanes)
        return carry

    lax.fori_loop(0, groups, own_rows, 0, unroll=UNROLL_OWN)

    cells = (8, WIDE)
    row = lax.broadcasted_iota(jnp.int32, cells, 0)

    def load(f, g, c, width=WIDE):
        return fields_at[f][rows_at(g), c : c + width]

    def north_of(f, x, g, c):
        return pltpu.roll(jnp.where(row == 0, load(f, g + 1, c), x), 7, 0)

    def south_of(f, x, g, c):
        return pltpu.roll(jnp.where(row == 7, load(f, max(g - 1, 0) if isinstance(g, int) else g - 1, c), x), 1, 0)

    def east_of(f, x, g, c):
        if WIDE == STRIP:
            return pltpu.roll(x, STRIP - 1, 1)
        more = load(f, g, (c + WIDE) % STRIP, BS)
        return pltpu.roll(jnp.concatenate([x, more], axis=1), WIDE + BS - 1, 1)[:, :WIDE]

    def west_of(f, x, g, c):
        if WIDE == STRIP:
            return pltpu.roll(x, 1, 1)
        more = load(f, g, (c - BS) % STRIP, BS)
        return pltpu.roll(jnp.concatenate([more, x], axis=1), 1, 1)[:, BS:]

    def stress_rows(g, new, last):
        for c in range(0, STRIP, WIDE):
            u, v = load(U, g, c), load(V, g, c)
            exx = east_of(U, u, g, c) - u
            eyy = north_of(V, v, g, c) - v
            shr = (north_of(U, u, g, c) - u) + (east_of(V, v, g, c) - v)
            div = exx + eyy
            ten = exx - eyy
            square = div * div + 0.25 * (ten * ten + shr * shr) + DMIN_SQ
            sixth = load(STR, g, c)
            half = sixth * lax.rsqrt(square)
            eighth = 0.25 * half
            both = half * div - sixth
            apart = eighth * ten
            sxx = (2.0 / 3.0) * load(SXX, g, c) + (both + apart)
            syy = (2.0 / 3.0) * load(SYY, g, c) + (both - apart)
            at = slice(c, c + WIDE)
            new[SXX][rows_at(g), at] = sxx
            new[SYY][rows_at(g), at] = syy
            new[S12][rows_at(g), at] = (2.0 / 3.0) * load(S12, g, c) + eighth * shr
            if last:
                new[S1_OUT][rows_at(g), at] = sxx + syy
                new[S2_OUT][rows_at(g), at] = sxx - syy

    def velocity_rows(g, new, beyond=None, last=False):
        for c in range(0, STRIP, WIDE):
            sxx, syy, s12 = load(SXX, g, c), load(SYY, g, c), load(S12, g, c)
            fx = sxx - west_of(SXX, sxx, g, c) + s12 - south_of(S12, s12, g, c)
            fy = s12 - west_of(S12, s12, g, c) + syy - south_of(SYY, syy, g, c)
            u, v, uo, vo = [load(f, g, c) for f in (U, V, UO, VO)]
            m, conc, tx, ty = [load(f, g, c) for f in (MASS, AREA, TX, TY)]
            du, dv = uo - u, vo - v
            square = du * du + dv * dv + SPEED_SQ
            drag = conc * (square * lax.rsqrt(square))
            d = m + drag
            q = load(TURN, g, c)
            ru = m * u + fx + tx + drag * uo
            rv = m * v + fy + ty + drag * vo
            inv = 1.0 / (d * d + q * q)
            u = (d * ru + q * rv) * inv
            v = (d * rv - q * ru) * inv
            if beyond is not None:
                mask = jnp.broadcast_to(beyond, cells)
                u = jnp.where(mask, 0.0, u)
                v = jnp.where(mask, 0.0, v)
            at = slice(c, c + WIDE)
            new[U][rows_at(g), at] = u
            new[V][rows_at(g), at] = v
            if last:
                du, dv = u - uo, v - vo
                square = du * du + dv * dv + SPEED_SQ
                drag = conc * (square * lax.rsqrt(square))
                x = (1.0 - conc) * tx + drag * du
                y = (1.0 - conc) * ty + drag * dv
                for i in range(WIDE // BS):
                    p = c // BS + i
                    if p < SLOTS:
                        slot = jnp.where(odd, SLOTS - 1 - p, p)
                        pair = [x[:, i * BS : (i + 1) * BS], y[:, i * BS : (i + 1) * BS]]
                        handed[g - 1, pl.ds(pl.multiple_of(slot * 16, 16), 16), :] = (
                            jnp.concatenate(pair, axis=0).astype(BF16)
                        )

    def copies(fields, out, row0, rows, sem0):
        made = []
        for n, f in enumerate(fields):
            for e in range(SLOTS):
                to = out.at[n, pl.ds(row0, rows), pl.ds(e * BS, BS)]
                sem = sems.at[sem0 + n * SLOTS + e]
                block = fields_at[f].at[pl.ds(TOP + row0, rows), slot_lanes(e)]
                made.append((e, pltpu.make_async_copy(block, to, sem),
                             pltpu.make_async_copy(empty.at[pl.ds(0, rows), :], to, sem)))
        return made

    def start(made):
        for e, full, none in made:
            @pl.when(e < count)
            def _():
                full.start()

            @pl.when(e >= count)
            def _():
                none.start()

    pending = []
    for it in range(ITERS):
        last = it == ITERS - 1
        new = {f: fields_at[n] for f, n in zip(RENEWED, range(S2_OUT + 1, S2_OUT + 6))}
        new[S1_OUT], new[S2_OUT] = fields_at[S1_OUT], fields_at[S2_OUT]

        def stress_step(g, carry):
            stress_rows(g, new, last)
            return carry

        lax.fori_loop(0, groups + (1 if last else 2), stress_step, 0, unroll=UNROLL_STRESS)
        for f in (SXX, SYY, S12):
            n = S2_OUT + 1 + RENEWED.index(f)
            fields_at[f], fields_at[n] = fields_at[n], fields_at[f]
        if last:
            made = copies((S1_OUT, S2_OUT, S12), stress_out, 0, BS, 0)
            start(made)
            pending += made
        else:
            velocity_rows(0, new, band == 0)
            velocity_rows(groups + 1, new, band == NLAT - 1)

        def velocity_step(g, carry):
            velocity_rows(g, new, None, last)
            return carry

        if last:
            for h in range(2):
                half = groups // 2
                lax.fori_loop(1 + h * half, 1 + (h + 1) * half, velocity_step, 0, unroll=UNROLL_VELOCITY)
                made = copies((U_NEW, V_NEW), vel_out, h * BS // 2, BS // 2, 24 + 16 * h)
                start(made)
                pending += made
        else:
            lax.fori_loop(1, groups + 1, velocity_step, 0, unroll=UNROLL_VELOCITY)
            for f in (U, V):
                n = S2_OUT + 1 + RENEWED.index(f)
                fields_at[f], fields_at[n] = fields_at[n], fields_at[f]
    for _, full, _ in pending:
        full.wait()


def dynamics(lens, band, lon, vel, stress, area, thick, got, coriolis):
    width = SLOTS * BS
    vmem = pl.BlockSpec(memory_space=pltpu.VMEM)
    smem = pl.BlockSpec(memory_space=pltpu.SMEM)
    return pl.pallas_call(
        dynamics_kernel,
        in_specs=[smem] * 3 + [vmem] * 6,
        out_specs=[pl.BlockSpec(memory_space=pl.ANY)] * 2 + [vmem],
        scratch_shapes=[
            *[pltpu.VMEM((ROWS + 8, STRIP), F32) for _ in range(S2_OUT + 6)],
            pltpu.VMEM((BS, BS), F32),
            pltpu.SemaphoreType.DMA((24 + 32,)),
        ],
        out_shape=[
            jax.ShapeDtypeStruct((2, BS, width), F32),
            jax.ShapeDtypeStruct((3, BS, width), F32),
            jax.ShapeDtypeStruct((NLON, M3_ROWS, BS), BF16),
        ],
        compiler_params=pltpu.CompilerParams(vmem_limit_bytes=32 * 2**20),
        name="dynamics",
    )(lens, band, lon, vel, stress, area, thick, got, coriolis)


def sort_kernel(lens, band, got, out, table):
    odd = lax.rem(band[0], 2) == 1

    def owner(k, start):
        note_slots(table, k, lens[band[0], k], start, odd)
        return start + lens[band[0], k]

    lax.fori_loop(0, NLON, owner, 0, unroll=UNROLL)

    def block(c, carry):
        out[c] = got[table[c]]
        return carry

    lax.fori_loop(0, NBB, block, 0, unroll=8)


def sort_back(lens, band, got):
    return pl.pallas_call(
        sort_kernel,
        out_shape=jax.ShapeDtypeStruct((NBB, 16, BS), BF16),
        in_specs=[pl.BlockSpec(memory_space=pltpu.SMEM)] * 2
        + [pl.BlockSpec(memory_space=pltpu.VMEM)],
        out_specs=pl.BlockSpec(memory_space=pltpu.VMEM),
        scratch_shapes=[pltpu.SMEM((NBB + 1,), jnp.int32)],
        compiler_params=pltpu.CompilerParams(vmem_limit_bytes=16 * 2**20),
        name="sort_back",
    )(lens, band, got)


def settle_kernel(got, out):
    def rows16(pair, carry):
        rows = pl.ds(pl.multiple_of(pair * 16, 16), 16)
        for cb in range(TILE):
            a = got[2 * pair, cb * 16 : (cb + 1) * 16, :].astype(F32)
            b = got[2 * pair + 1, cb * 16 : (cb + 1) * 16, :].astype(F32)
            lanes = slice(cb * BS, (cb + 1) * BS)
            out[0, rows, lanes] = jnp.concatenate([a[0:8], b[0:8]], axis=0).astype(BF16)
            out[1, rows, lanes] = jnp.concatenate([a[8:16], b[8:16]], axis=0).astype(BF16)
        return carry

    lax.fori_loop(0, BS // 16, rows16, 0, unroll=UNROLL)


def settle(got):
    return pl.pallas_call(
        settle_kernel,
        out_shape=jax.ShapeDtypeStruct((2, BS, TILE * BS), BF16),
        in_specs=[pl.BlockSpec(memory_space=pltpu.VMEM)],
        out_specs=pl.BlockSpec(memory_space=pltpu.VMEM),
        compiler_params=pltpu.CompilerParams(vmem_limit_bytes=16 * 2**20),
        name="settle",
    )(got)


def to_all(block):
    return lax.all_to_all(block, "lon", 0, 0, tiled=True)


def body(ocean_forcing, ice_velocity, ice_stress, cat_area, cat_thick, run_lengths):
    band_idx = lax.axis_index("lat")
    lon_idx = lax.axis_index("lon")
    lens = run_lengths
    place = (jnp.reshape(band_idx, (1,)), jnp.reshape(lon_idx, (1,)))
    ice = (ice_velocity, ice_stress, cat_area, cat_thick)
    rows = (band_idx * BS + jnp.arange(-TOP, BS + TOP, dtype=jnp.int32)).astype(F32)
    latitude = -78.0 + 168.0 * (rows + 0.5) / (BS * NLAT)
    coriolis = jnp.broadcast_to(jnp.sin(latitude * (jnp.pi / 180.0))[:, None], (ROWS, BS))
    to_south, to_north = edge_rows(*ice, ocean_forcing)
    north = lax.ppermute(to_south, "lat", [(b, b - 1) for b in range(1, NLAT)])
    south = lax.ppermute(to_north, "lat", [(b, b + 1) for b in range(NLAT - 1)])
    north, south, coriolis = lax.optimization_barrier((north, south, coriolis))
    edges = edge_columns(lens, *place, *ice)
    message = spread(ocean_forcing, north, south, edges)
    dealt = to_all(deal(lens, *place, to_all(message)))
    velocity_out, stress_out, handed = dynamics(lens, *place, *ice, dealt, coriolis)
    handed = to_all(handed).reshape(NLON * SLOTS, 16, BS)
    back = sort_back(lens, place[0], handed).reshape(NLON, M4_ROWS, BS)
    return (velocity_out, stress_out, settle(to_all(back)))


def solution(mesh):
    slots = P(None, None, ("lat", "lon"))
    grid = P(None, "lat", "lon")
    return jax.shard_map(
        body,
        mesh=mesh,
        in_specs=(grid, slots, slots, slots, slots, P()),
        out_specs=(slots, slots, grid),
        check_vma=False,
    )
```

```python
import functools

import jax
import jax.numpy as jnp
from jax import lax
from jax.experimental import pallas as pl
from jax.experimental.pallas import tpu as pltpu
from jax.sharding import PartitionSpec as P

BS = 128
ITERS = 3
NLAT = 8
NLON = 16
SLOTS = 8
NBB = 64
TILE = 4
DEEP = 3
PSTAR = 2.0
CSTAR = 20.0
DMIN_SQ = 0.01
SPEED_SQ = 0.01
ICE = 7
U, V, SXX, SYY, S12, AREA, MASS, STR, UO, VO, TX, TY, TURN, S1_OUT, S2_OUT, U_NEW, V_NEW = range(17)
RENEWED = (U, V, SXX, SYY, S12)
EDGE_LANES = 3 * ICE
EAST_AT = 4 * EDGE_LANES
WEST_AT = EAST_AT + 12
STRIP = (SLOTS + 1) * BS
UNROLL = 4
UNROLL_OWN = 8
UNROLL_STRESS = 9
UNROLL_VELOCITY = 8
WIDE = 3 * BS
TOP = 8
ROWS = BS + 2 * TOP
SEND_ROWS = 24
MASS_AT, FORCE_AT = 18, 20
M1_ROWS = TILE * 32 + SLOTS * 8
M2_ROWS = SLOTS * 32 + (SLOTS + 1) * 8 + 8
M3_ROWS = SLOTS * 16
M4_ROWS = TILE * 16
F32 = jnp.float32
BF16 = jnp.bfloat16


def lanes_of(shape):
    return lax.broadcasted_iota(jnp.int32, shape, len(shape) - 1)


def ice_fields(vel, stress, area, thick):
    conc = area[0] + area[1] + area[2] + area[3] + area[4]
    mass = area[0] * thick[0]
    for n in range(1, 5):
        mass = mass + area[n] * thick[n]
    sxx, syy = 0.5 * (stress[0] + stress[1]), 0.5 * (stress[0] - stress[1])
    return [vel[0], vel[1], sxx, syy, stress[2], conc, mass]


def strength_of(conc, mass):
    return (PSTAR / 6.0) * mass * jnp.exp(-CSTAR * (1.0 - conc))


def edges_kernel(lens, band, lon, *refs):
    ice = [refs[4 * i : 4 * i + 4] for i in range(4)]
    f_low, f_high, to_mate, to_other, packed_out = refs[16:]
    odd = lax.rem(band[0], 2) == 1

    def strips(out, which, force, row0, frow0):
        arrays = [ice[i][which] for i in range(4)]
        fields = ice_fields(*[[a[n] for n in range(a.shape[0])] for a in arrays])
        for f in range(MASS):
            out[3 * f : 3 * f + 3, :] = fields[f][row0 : row0 + 3, :]
        near = row0 if row0 == 0 else row0 + 1
        out[MASS_AT : MASS_AT + 2, :] = fields[MASS][near : near + 2, :]
        if row0:
            strength = strength_of(fields[AREA], fields[MASS])
            out[3 * AREA : 3 * AREA + 1, :] = strength[row0 : row0 + 1, :]
        for f in range(4):
            rows = force[f].astype(F32)
            at = FORCE_AT + f
            out[at : at + 1, 0:512] = rows[frow0 : frow0 + 1, :]
            out[at : at + 1, 512:1024] = rows[frow0 + 1 : frow0 + 2, :]

    low, high = (0, f_low, 0, 0), (1, f_high, 5, 14)

    @pl.when(odd)
    def _():
        strips(to_mate, *low)
        strips(to_other, *high)

    @pl.when(jnp.logical_not(odd))
    def _():
        strips(to_mate, *high)
        strips(to_other, *low)

    lane = lanes_of((BS, BS))
    total = jnp.zeros((BS, BS), F32)
    for side in range(2):
        arrays = [ice[i][2 + side] for i in range(4)]
        fields = ice_fields(*[[a[n] for n in range(a.shape[0])] for a in arrays])
        first_columns = jnp.broadcast_to(odd if side else jnp.logical_not(odd), (BS, BS))
        packed = jnp.zeros((BS, BS), F32)
        for f in range(ICE):
            at_zero = jnp.where(first_columns, fields[f], pltpu.roll(fields[f], 3, 1))
            moved = pltpu.roll(at_zero, 3 * f, 1) if f else at_zero
            packed = jnp.where((lane >= 3 * f) & (lane < 3 * f + 3), moved, packed)
        high = packed.astype(BF16).astype(F32)
        both = high + pltpu.roll(packed - high, EDGE_LANES, 1)
        total = total + (pltpu.roll(both, 2 * EDGE_LANES, 1) if side else both)
    packed_out[...] = total


def make_edges(lens, band, lon, vel, stress, area, thick, forcing):
    width = SLOTS * BS

    def at(*index):
        return lambda i, lens, band, lon: index

    def specs(n):
        return [
            pl.BlockSpec((n, 8, width), at(0, 0, 0)),
            pl.BlockSpec((n, 8, width), at(0, BS // 8 - 1, 0)),
            pl.BlockSpec((n, BS, BS), at(0, 0, 0)),
            pl.BlockSpec(
                (n, BS, BS), lambda i, lens, band, lon: (0, 0, lens[band[0], lon[0]] - 1)
            ),
        ]

    in_specs = specs(2) + specs(3) + specs(5) + specs(5)
    in_specs += [
        pl.BlockSpec((4, 16, 512), at(0, 0, 0)),
        pl.BlockSpec((4, 16, 512), at(0, BS // 16 - 1, 0)),
    ]
    return pl.pallas_call(
        edges_kernel,
        grid_spec=pltpu.PrefetchScalarGridSpec(
            num_scalar_prefetch=3,
            grid=(1,),
            in_specs=in_specs,
            out_specs=[pl.BlockSpec((SEND_ROWS, width), at(0, 0))] * 2
            + [pl.BlockSpec((BS, BS), at(0, 0))],
        ),
        out_shape=[jax.ShapeDtypeStruct((SEND_ROWS, width), F32)] * 2
        + [jax.ShapeDtypeStruct((BS, BS), F32)],
        compiler_params=pltpu.CompilerParams(vmem_limit_bytes=60 * 2**20),
        name="edges",
    )(lens, band, lon, *([vel] * 4), *([stress] * 4), *([area] * 4), *([thick] * 4), forcing, forcing)


def spread_kernel(forcing, edges, out):
    def rows16(pair, carry):
        base = pl.multiple_of(pair * 16, 16)
        for cb in range(TILE):
            parts = [
                forcing[f, pl.ds(base, 16), cb * BS : (cb + 1) * BS].astype(F32) for f in range(4)
            ]
            low = jnp.concatenate([p[0:8] for p in parts], axis=0)
            high = jnp.concatenate([p[8:16] for p in parts], axis=0)
            out[2 * pair, cb * 32 : (cb + 1) * 32, :] = low.astype(BF16)
            out[2 * pair + 1, cb * 32 : (cb + 1) * 32, :] = high.astype(BF16)
        return carry

    lax.fori_loop(0, BS // 16, rows16, 0, unroll=2)
    row = lax.broadcasted_iota(jnp.int32, (SLOTS, 8, BS), 1)
    for j in range(NLON):
        rows = edges[8 * j : 8 * j + 8, :].reshape(SLOTS, 1, BS)
        rows = jnp.where(row == 7, jnp.broadcast_to(rows, (SLOTS, 8, BS)), 0.0)
        out[j, TILE * 32 :, :] = rows.reshape(SLOTS * 8, BS).astype(BF16)


def spread(forcing, edges):
    return pl.pallas_call(
        spread_kernel,
        out_shape=jax.ShapeDtypeStruct((NLON, M1_ROWS, BS), BF16),
        in_specs=[pl.BlockSpec(memory_space=pltpu.VMEM)] * 2,
        out_specs=pl.BlockSpec(memory_space=pltpu.VMEM),
        compiler_params=pltpu.CompilerParams(vmem_limit_bytes=16 * 2**20),
        name="spread",
    )(forcing, edges)


def spread_strips_kernel(band, message, from_mate, from_other, out, hold):
    odd = lax.rem(band[0], 2) == 1

    def beside(is_north, row, rows, at, width):
        from_chip, from_next = (
            ref[row : row + rows, at : at + width] for ref in (from_mate, from_other)
        )
        use_chip = jnp.logical_not(odd) if is_north else odd
        return jnp.where(jnp.broadcast_to(use_chip, from_chip.shape), from_chip, from_next)

    for j in range(NLON):
        hold[...] = jnp.zeros(hold.shape, F32)
        f = j % 8
        if f < ICE:
            if f < MASS:
                rows = beside(j < 8, 3 * f, 3, 0, SLOTS * BS)
            else:
                rows = beside(j < 8, MASS_AT, 2, 0, SLOTS * BS)
                spare = jnp.zeros((1, SLOTS * BS), F32)
                rows = jnp.concatenate([rows, spare] if j < 8 else [spare, rows], axis=0)
            high = rows.astype(BF16).astype(F32)
            low = rows - high
            for s in range(SLOTS):
                hold[8 * s : 8 * s + 3, :] = high[:, s * BS : (s + 1) * BS]
                hold[8 * s + 3 : 8 * s + 6, :] = low[:, s * BS : (s + 1) * BS]
        field, h = j // 4, j % 4
        for cb in range(TILE):
            at = (h % 2) * 512 + cb * BS
            hold[8 * cb + 6 : 8 * cb + 7, :] = beside(h >= 2, FORCE_AT + field, 1, at, BS)
        edges = message[j, TILE * 32 :, :].astype(F32)
        out[j, TILE * 32 :, :] = (hold[...] + edges).astype(BF16)


def spread_strips(band, message, from_mate, from_other):
    return pl.pallas_call(
        spread_strips_kernel,
        out_shape=jax.ShapeDtypeStruct((NLON, M1_ROWS, BS), BF16),
        in_specs=[pl.BlockSpec(memory_space=pltpu.SMEM)]
        + [pl.BlockSpec(memory_space=pltpu.VMEM)] * 3,
        out_specs=pl.BlockSpec(memory_space=pltpu.VMEM),
        scratch_shapes=[pltpu.VMEM((SLOTS * 8, BS), F32)],
        input_output_aliases={1: 0},
        compiler_params=pltpu.CompilerParams(vmem_limit_bytes=16 * 2**20),
        name="spread_strips",
    )(band, message, from_mate, from_other)


def note_slots(table, k, count, start, odd):
    for s in range(SLOTS):
        at = start + s
        column = jnp.where(odd, NBB - 1 - at, at)
        table[jnp.where(s < count, column, NBB)] = k * SLOTS + s


def deal_kernel(lens, band, lon, got, out, groups, halos, table):
    band, lon = band[0], lon[0]
    odd = lax.rem(band, 2) == 1
    other = jnp.where(lon < 8, jnp.minimum(band + 1, NLAT - 1), jnp.maximum(band - 1, 0))
    other_odd = lax.rem(other, 2) == 1

    def fill(l, start):
        groups[pl.ds(pl.multiple_of(l * SLOTS, SLOTS), SLOTS)] = (
            got[l, TILE * 32 :, :].astype(F32).reshape(SLOTS, 8, BS)
        )
        note_slots(table, l, lens[other, l], start, other_odd)
        return start + lens[other, l]

    lax.fori_loop(0, NLON, fill, 0, unroll=UNROLL)
    row6 = lax.broadcasted_iota(jnp.int32, (8, BS), 0) == 6

    def halo(c, carry):
        own = (c // TILE) * SLOTS + lax.rem(c, TILE)
        halos[c] = jnp.where(row6, groups[own], groups[table[c]])
        return carry

    lax.fori_loop(0, NBB, halo, 0, unroll=8)
    lane = lanes_of((8, BS))

    def column_at(p):
        p = jnp.minimum(p, NBB - 1)
        return jnp.where(odd, NBB - 1 - p, p)

    def forcing(c):
        at = pl.multiple_of(lax.rem(c, TILE) * 32, 32)
        return got[c // TILE, pl.ds(at, 32), :]

    def edges(k):
        at = pl.multiple_of(lax.rem(k, NLON) * SLOTS, SLOTS)
        return groups[pl.ds(at, SLOTS), 7, :]

    def owner(k, start):
        count = lens[band, k]
        last = start + count - 1
        east = jnp.where(odd, NBB - 1 - start, last) + 1
        west = jnp.where(odd, NBB - 1 - last, start) - 1
        east, west = lax.rem(east, NBB), lax.rem(west + NBB, NBB)
        parts = []
        for e in range(SLOTS):
            c = column_at(start + e)
            out[k, e * 32 : (e + 1) * 32, :] = forcing(c)
            parts.append(halos[c])
        parts.append(jnp.where(lane < 64, halos[east], halos[west]))
        side = jnp.where(lane < 2 * EDGE_LANES, edges(k + 1), edges(k + NLON - 1))
        by_east, by_west = forcing(east).astype(F32), forcing(west).astype(F32)
        for f in range(4):
            for rows, at, col in ((by_east, EAST_AT, 0), (by_west, WEST_AT, 125)):
                there = at + 3 * f
                moved = pltpu.roll(rows[8 * f : 8 * f + 8, :], (there - col) % BS, 1)
                side = jnp.where((lane >= there) & (lane < there + 3), moved, side)
        parts.append(side)
        out[k, SLOTS * 32 :, :] = jnp.concatenate(parts, axis=0).astype(BF16)
        return start + count

    lax.fori_loop(0, NLON, owner, 0, unroll=4)


def deal(lens, band, lon, got):
    return pl.pallas_call(
        deal_kernel,
        out_shape=jax.ShapeDtypeStruct((NLON, M2_ROWS, BS), BF16),
        in_specs=[pl.BlockSpec(memory_space=pltpu.SMEM)] * 3
        + [pl.BlockSpec(memory_space=pltpu.VMEM)],
        out_specs=pl.BlockSpec(memory_space=pltpu.VMEM),
        scratch_shapes=[
            pltpu.VMEM((NLON * SLOTS, 8, BS), F32),
            pltpu.VMEM((NBB, 8, BS), F32),
            pltpu.SMEM((NBB + 1,), jnp.int32),
        ],
        compiler_params=pltpu.CompilerParams(vmem_limit_bytes=32 * 2**20),
        name="deal",
    )(lens, band, lon, got)


def dynamics_kernel(
    lens, band, lon, vel, stress, area, thick, got, coriolis,
    vel_out, stress_out, handed, *scratch,
):
    fields_at, (empty, sems) = list(scratch[:-2]), scratch[-2:]
    band, lon = band[0], lon[0]
    odd = lax.rem(band, 2) == 1
    count = lens[band, lon]
    groups = BS // 8

    def rows_at(g):
        return pl.ds(g * 8 if isinstance(g, int) else pl.multiple_of(g * 8, 8), 8)

    def slot_lanes(slot):
        return pl.ds(pl.multiple_of(jnp.where(odd, SLOTS - 1 - slot, slot) * BS, BS), BS)

    edge_lanes = pl.ds(SLOTS * BS, BS)
    empty[...] = jnp.zeros(empty.shape, F32)

    for j in range(NLON):
        group = got[j, SLOTS * 32 : SLOTS * 32 + 8 * (SLOTS + 1), :].astype(F32)
        group = group.reshape(SLOTS + 1, 8, BS)
        whole = group + pltpu.roll(group, 5, 1)
        if j >= 8:
            whole = pltpu.roll(whole, 5, 1)
        f = j % 8
        g = groups + 1 if j < 8 else 0
        force_row = (TOP - 2, TOP - 1, TOP + BS, TOP + BS + 1)[j % 4]
        for e in range(SLOTS + 1):
            lanes = slot_lanes(e) if e < SLOTS else edge_lanes
            mine = jnp.broadcast_to(e < count, (8, BS))
            if f < ICE:
                fields_at[f][rows_at(g), lanes] = jnp.where(mine, whole[e], whole[SLOTS])
            rows = jnp.where(mine, group[e], group[SLOTS])
            fields_at[UO + j // 4][force_row : force_row + 1, lanes] = rows[6:7, :]

    def derived(conc, mass, g, lanes):
        turn = coriolis[rows_at(g), :]
        if conc.shape[1] > BS:
            turn = jnp.concatenate([turn] * (conc.shape[1] // BS), axis=1)
        fields_at[STR][rows_at(g), lanes] = strength_of(conc, mass)
        fields_at[TURN][rows_at(g), lanes] = turn * mass

    for g in (0, groups + 1):
        derived(fields_at[AREA][rows_at(g), :], fields_at[MASS][rows_at(g), :], g, slice(0, STRIP))
    far = TOP - DEEP
    fields_at[STR][far : far + 1, :] = fields_at[AREA][far : far + 1, :]

    def own_rows(j, carry):
        packed = got[j, M2_ROWS - 16 :, :].astype(F32)[8:16, :]
        near = lanes_of((8, BS)) < 64

        def joined(east, east_lane, west, west_lane):
            return jnp.where(
                near,
                pltpu.roll(east, (BS - east_lane) % BS, 1),
                pltpu.roll(west, (125 - west_lane) % BS, 1),
            )

        forced = [joined(packed, EAST_AT + 3 * f, packed, WEST_AT + 3 * f) for f in range(4)]
        packed = packed + pltpu.roll(packed, BS - EDGE_LANES, 1)
        at_zero = pltpu.roll(packed, BS - 2 * EDGE_LANES, 1)
        east = jnp.where(odd, at_zero, packed)
        west = jnp.where(odd, packed, at_zero)
        beside = [joined(east, 3 * f, west, 3 * f) for f in range(ICE)]
        rows = rows_at(j)
        for e in range(SLOTS + 1):
            if e == SLOTS:
                fields, lanes = beside, edge_lanes
            else:
                lanes = slot_lanes(e)
                at = slice(e * BS, (e + 1) * BS)
                fields = ice_fields(
                    [vel[n, rows, at] for n in range(2)],
                    [stress[n, rows, at] for n in range(3)],
                    [area[n, rows, at] for n in range(5)],
                    [thick[n, rows, at] for n in range(5)],
                )
                mine = jnp.broadcast_to(e < count, (8, BS))
                fields = [jnp.where(mine, fields[f], beside[f]) for f in range(ICE)]
            force = forced
            if e < SLOTS:
                force = got[j, e * 32 : (e + 1) * 32, :].astype(F32)
                force = [jnp.where(mine, force[8 * f : 8 * f + 8], forced[f]) for f in range(4)]
            for f in range(4):
                fields_at[UO + f][rows_at(j + 1), lanes] = force[f]
            for f in range(ICE):
                fields_at[f][rows_at(j + 1), lanes] = fields[f]
            derived(fields[AREA], fields[MASS], j + 1, lanes)
        return carry

    lax.fori_loop(0, groups, own_rows, 0, unroll=UNROLL_OWN)

    cells = (8, WIDE)
    row = lax.broadcasted_iota(jnp.int32, cells, 0)

    def load(f, g, c, width=WIDE):
        return fields_at[f][rows_at(g), c : c + width]

    def north_of(f, x, g, c):
        return pltpu.roll(jnp.where(row == 0, load(f, g + 1, c), x), 7, 0)

    def south_of(f, x, g, c):
        return pltpu.roll(jnp.where(row == 7, load(f, max(g - 1, 0) if isinstance(g, int) else g - 1, c), x), 1, 0)

    def east_of(f, x, g, c):
        if WIDE == STRIP:
            return pltpu.roll(x, STRIP - 1, 1)
        more = load(f, g, (c + WIDE) % STRIP, BS)
        return pltpu.roll(jnp.concatenate([x, more], axis=1), WIDE + BS - 1, 1)[:, :WIDE]

    def west_of(f, x, g, c):
        if WIDE == STRIP:
            return pltpu.roll(x, 1, 1)
        more = load(f, g, (c - BS) % STRIP, BS)
        return pltpu.roll(jnp.concatenate([more, x], axis=1), 1, 1)[:, BS:]

    def stress_rows(g, new, last):
        for c in range(0, STRIP, WIDE):
            u, v = load(U, g, c), load(V, g, c)
            exx = east_of(U, u, g, c) - u
            eyy = north_of(V, v, g, c) - v
            shr = (north_of(U, u, g, c) - u) + (east_of(V, v, g, c) - v)
            div = exx + eyy
            ten = exx - eyy
            square = div * div + 0.25 * (ten * ten + shr * shr) + DMIN_SQ
            sixth = load(STR, g, c)
            half = sixth * lax.rsqrt(square)
            eighth = 0.25 * half
            both = half * div - sixth
            apart = eighth * ten
            sxx = (2.0 / 3.0) * load(SXX, g, c) + (both + apart)
            syy = (2.0 / 3.0) * load(SYY, g, c) + (both - apart)
            at = slice(c, c + WIDE)
            new[SXX][rows_at(g), at] = sxx
            new[SYY][rows_at(g), at] = syy
            new[S12][rows_at(g), at] = (2.0 / 3.0) * load(S12, g, c) + eighth * shr
            if last:
                new[S1_OUT][rows_at(g), at] = sxx + syy
                new[S2_OUT][rows_at(g), at] = sxx - syy

    def velocity_rows(g, new, beyond=None, last=False):
        for c in range(0, STRIP, WIDE):
            sxx, syy, s12 = load(SXX, g, c), load(SYY, g, c), load(S12, g, c)
            fx = sxx - west_of(SXX, sxx, g, c) + s12 - south_of(S12, s12, g, c)
            fy = s12 - west_of(S12, s12, g, c) + syy - south_of(SYY, syy, g, c)
            u, v, uo, vo = [load(f, g, c) for f in (U, V, UO, VO)]
            m, conc, tx, ty = [load(f, g, c) for f in (MASS, AREA, TX, TY)]
            du, dv = uo - u, vo - v
            square = du * du + dv * dv + SPEED_SQ
            drag = conc * (square * lax.rsqrt(square))
            d = m + drag
            q = load(TURN, g, c)
            ru = m * u + fx + tx + drag * uo
            rv = m * v + fy + ty + drag * vo
            inv = 1.0 / (d * d + q * q)
            u = (d * ru + q * rv) * inv
            v = (d * rv - q * ru) * inv
            if beyond is not None:
                mask = jnp.broadcast_to(beyond, cells)
                u = jnp.where(mask, 0.0, u)
                v = jnp.where(mask, 0.0, v)
            at = slice(c, c + WIDE)
            new[U][rows_at(g), at] = u
            new[V][rows_at(g), at] = v
            if last:
                du, dv = u - uo, v - vo
                square = du * du + dv * dv + SPEED_SQ
                drag = conc * (square * lax.rsqrt(square))
                x = (1.0 - conc) * tx + drag * du
                y = (1.0 - conc) * ty + drag * dv
                for i in range(WIDE // BS):
                    p = c // BS + i
                    if p < SLOTS:
                        slot = jnp.where(odd, SLOTS - 1 - p, p)
                        pair = [x[:, i * BS : (i + 1) * BS], y[:, i * BS : (i + 1) * BS]]
                        handed[g - 1, pl.ds(pl.multiple_of(slot * 16, 16), 16), :] = (
                            jnp.concatenate(pair, axis=0).astype(BF16)
                        )

    def copies(fields, out, row0, rows, sem0):
        made = []
        for n, f in enumerate(fields):
            for e in range(SLOTS):
                to = out.at[n, pl.ds(row0, rows), pl.ds(e * BS, BS)]
                sem = sems.at[sem0 + n * SLOTS + e]
                block = fields_at[f].at[pl.ds(TOP + row0, rows), slot_lanes(e)]
                made.append((e, pltpu.make_async_copy(block, to, sem),
                             pltpu.make_async_copy(empty.at[pl.ds(0, rows), :], to, sem)))
        return made

    def start(made):
        for e, full, none in made:
            @pl.when(e < count)
            def _():
                full.start()

            @pl.when(e >= count)
            def _():
                none.start()

    pending = []
    for it in range(ITERS):
        last = it == ITERS - 1
        new = {f: fields_at[n] for f, n in zip(RENEWED, range(S2_OUT + 1, S2_OUT + 6))}
        new[S1_OUT], new[S2_OUT] = fields_at[S1_OUT], fields_at[S2_OUT]

        def stress_step(g, carry):
            stress_rows(g, new, last)
            return carry

        lax.fori_loop(0, groups + (1 if last else 2), stress_step, 0, unroll=UNROLL_STRESS)
        for f in (SXX, SYY, S12):
            n = S2_OUT + 1 + RENEWED.index(f)
            fields_at[f], fields_at[n] = fields_at[n], fields_at[f]
        if last:
            made = copies((S1_OUT, S2_OUT, S12), stress_out, 0, BS, 0)
            start(made)
            pending += made
        else:
            velocity_rows(0, new, band == 0)
            velocity_rows(groups + 1, new, band == NLAT - 1)

        def velocity_step(g, carry):
            velocity_rows(g, new, None, last)
            return carry

        if last:
            for h in range(2):
                half = groups // 2
                lax.fori_loop(1 + h * half, 1 + (h + 1) * half, velocity_step, 0, unroll=UNROLL_VELOCITY)
                made = copies((U_NEW, V_NEW), vel_out, h * BS // 2, BS // 2, 24 + 16 * h)
                start(made)
                pending += made
        else:
            lax.fori_loop(1, groups + 1, velocity_step, 0, unroll=UNROLL_VELOCITY)
            for f in (U, V):
                n = S2_OUT + 1 + RENEWED.index(f)
                fields_at[f], fields_at[n] = fields_at[n], fields_at[f]
    for _, full, _ in pending:
        full.wait()


def dynamics(lens, band, lon, vel, stress, area, thick, got, coriolis):
    width = SLOTS * BS
    vmem = pl.BlockSpec(memory_space=pltpu.VMEM)
    smem = pl.BlockSpec(memory_space=pltpu.SMEM)
    return pl.pallas_call(
        dynamics_kernel,
        in_specs=[smem] * 3 + [vmem] * 6,
        out_specs=[pl.BlockSpec(memory_space=pl.ANY)] * 2 + [vmem],
        scratch_shapes=[
            *[pltpu.VMEM((ROWS + 8, STRIP), F32) for _ in range(S2_OUT + 6)],
            pltpu.VMEM((BS, BS), F32),
            pltpu.SemaphoreType.DMA((24 + 32,)),
        ],
        out_shape=[
            jax.ShapeDtypeStruct((2, BS, width), F32),
            jax.ShapeDtypeStruct((3, BS, width), F32),
            jax.ShapeDtypeStruct((NLON, M3_ROWS, BS), BF16),
        ],
        compiler_params=pltpu.CompilerParams(vmem_limit_bytes=32 * 2**20),
        name="dynamics",
    )(lens, band, lon, vel, stress, area, thick, got, coriolis)


def sort_kernel(lens, band, got, out, table):
    odd = lax.rem(band[0], 2) == 1

    def owner(k, start):
        note_slots(table, k, lens[band[0], k], start, odd)
        return start + lens[band[0], k]

    lax.fori_loop(0, NLON, owner, 0, unroll=UNROLL)

    def block(c, carry):
        out[c] = got[table[c]]
        return carry

    lax.fori_loop(0, NBB, block, 0, unroll=8)


def sort_back(lens, band, got):
    return pl.pallas_call(
        sort_kernel,
        out_shape=jax.ShapeDtypeStruct((NBB, 16, BS), BF16),
        in_specs=[pl.BlockSpec(memory_space=pltpu.SMEM)] * 2
        + [pl.BlockSpec(memory_space=pltpu.VMEM)],
        out_specs=pl.BlockSpec(memory_space=pltpu.VMEM),
        scratch_shapes=[pltpu.SMEM((NBB + 1,), jnp.int32)],
        compiler_params=pltpu.CompilerParams(vmem_limit_bytes=16 * 2**20),
        name="sort_back",
    )(lens, band, got)


def settle_kernel(got, out):
    def rows16(pair, carry):
        rows = pl.ds(pl.multiple_of(pair * 16, 16), 16)
        for cb in range(TILE):
            a = got[2 * pair, cb * 16 : (cb + 1) * 16, :].astype(F32)
            b = got[2 * pair + 1, cb * 16 : (cb + 1) * 16, :].astype(F32)
            lanes = slice(cb * BS, (cb + 1) * BS)
            out[0, rows, lanes] = jnp.concatenate([a[0:8], b[0:8]], axis=0).astype(BF16)
            out[1, rows, lanes] = jnp.concatenate([a[8:16], b[8:16]], axis=0).astype(BF16)
        return carry

    lax.fori_loop(0, BS // 16, rows16, 0, unroll=UNROLL)


def settle(got):
    return pl.pallas_call(
        settle_kernel,
        out_shape=jax.ShapeDtypeStruct((2, BS, TILE * BS), BF16),
        in_specs=[pl.BlockSpec(memory_space=pltpu.VMEM)],
        out_specs=pl.BlockSpec(memory_space=pltpu.VMEM),
        compiler_params=pltpu.CompilerParams(vmem_limit_bytes=16 * 2**20),
        name="settle",
    )(got)


def to_all(block):
    return lax.all_to_all(block, "lon", 0, 0, tiled=True)


def body(ocean_forcing, ice_velocity, ice_stress, cat_area, cat_thick, run_lengths):
    band_idx = lax.axis_index("lat")
    lon_idx = lax.axis_index("lon")
    lens = run_lengths
    place = (jnp.reshape(band_idx, (1,)), jnp.reshape(lon_idx, (1,)))
    ice = (ice_velocity, ice_stress, cat_area, cat_thick)
    rows = (band_idx * BS + jnp.arange(-TOP, BS + TOP, dtype=jnp.int32)).astype(F32)
    latitude = -78.0 + 168.0 * (rows + 0.5) / (BS * NLAT)
    coriolis = jnp.broadcast_to(jnp.sin(latitude * (jnp.pi / 180.0))[:, None], (ROWS, BS))
    to_mate, to_other, edges = make_edges(lens, *place, *ice, ocean_forcing)
    message = spread(ocean_forcing, edges)
    pairs = [(b, b ^ 1) for b in range(NLAT)]
    from_mate = lax.ppermute(to_mate, "lat", pairs)
    pairs = [(b, b + 1 if b % 2 else b - 1) for b in range(1, NLAT - 1)]
    from_other = lax.ppermute(to_other, "lat", pairs)
    from_mate, from_other, coriolis = lax.optimization_barrier((from_mate, from_other, coriolis))
    message = spread_strips(place[0], message, from_mate, from_other)
    dealt = to_all(deal(lens, *place, to_all(message)))
    velocity_out, stress_out, handed = dynamics(lens, *place, *ice, dealt, coriolis)
    handed = to_all(handed).reshape(NLON * SLOTS, 16, BS)
    back = sort_back(lens, place[0], handed).reshape(NLON, M4_ROWS, BS)
    return (velocity_out, stress_out, settle(to_all(back)))


def solution(mesh):
    slots = P(None, None, ("lat", "lon"))
    grid = P(None, "lat", "lon")
    return jax.shard_map(
        body,
        mesh=mesh,
        in_specs=(grid, slots, slots, slots, slots, P()),
        out_specs=(slots, slots, grid),
        check_vma=False,
    )
```

```python
import functools

import jax
import jax.numpy as jnp
from jax import lax
from jax.experimental import pallas as pl
from jax.experimental.pallas import tpu as pltpu
from jax.sharding import PartitionSpec as P

BS = 128
ITERS = 3
NLAT = 8
NLON = 16
SLOTS = 8
NBB = 64
TILE = 4
DEEP = 3
PSTAR = 2.0
CSTAR = 20.0
DMIN_SQ = 0.01
SPEED_SQ = 0.01
ICE = 7
U, V, SXX, SYY, S12, AREA, MASS, STR, UO, VO, TX, TY, TURN, S1_OUT, S2_OUT, U_NEW, V_NEW = range(17)
RENEWED = (U, V, SXX, SYY, S12)
EDGE_LANES = 3 * ICE
EAST_AT = 4 * EDGE_LANES
WEST_AT = EAST_AT + 12
STRIP = (SLOTS + 1) * BS
UNROLL = 4
UNROLL_OWN = 8
UNROLL_STRESS = 8
UNROLL_VELOCITY = 8
WIDE = 3 * BS
ROWS = BS + 8
SEND_ROWS = 24
MASS_AT, FORCE_AT = 18, 20
M1_ROWS = TILE * 32 + SLOTS * 8
M2_ROWS = SLOTS * 32 + (SLOTS + 1) * 8 + 8
M3_ROWS = SLOTS * 16
M4_ROWS = TILE * 16
F32 = jnp.float32
BF16 = jnp.bfloat16


def lanes_of(shape):
    return lax.broadcasted_iota(jnp.int32, shape, len(shape) - 1)


def ice_fields(vel, stress, area, thick):
    conc = area[0] + area[1] + area[2] + area[3] + area[4]
    mass = area[0] * thick[0]
    for n in range(1, 5):
        mass = mass + area[n] * thick[n]
    sxx, syy = 0.5 * (stress[0] + stress[1]), 0.5 * (stress[0] - stress[1])
    return [vel[0], vel[1], sxx, syy, stress[2], conc, mass]


def strength_of(conc, mass):
    return (PSTAR / 6.0) * mass * jnp.exp(-CSTAR * (1.0 - conc))


def edges_kernel(lens, band, lon, *refs):
    ice = [refs[4 * i : 4 * i + 4] for i in range(4)]
    f_low, f_high, to_mate, to_other, packed_out = refs[16:]
    odd = lax.rem(band[0], 2) == 1

    def strips(out, which, force, row0, frow0):
        arrays = [ice[i][which] for i in range(4)]
        fields = ice_fields(*[[a[n] for n in range(a.shape[0])] for a in arrays])
        for f in range(MASS):
            out[3 * f : 3 * f + 3, :] = fields[f][row0 : row0 + 3, :]
        near = row0 if row0 == 0 else row0 + 1
        out[MASS_AT : MASS_AT + 2, :] = fields[MASS][near : near + 2, :]
        if row0:
            strength = strength_of(fields[AREA], fields[MASS])
            out[3 * AREA : 3 * AREA + 1, :] = strength[row0 : row0 + 1, :]
        for f in range(4):
            rows = force[f].astype(F32)
            at = FORCE_AT + f
            out[at : at + 1, 0:512] = rows[frow0 : frow0 + 1, :]
            out[at : at + 1, 512:1024] = rows[frow0 + 1 : frow0 + 2, :]

    low, high = (0, f_low, 0, 0), (1, f_high, 5, 14)

    @pl.when(odd)
    def _():
        strips(to_mate, *low)
        strips(to_other, *high)

    @pl.when(jnp.logical_not(odd))
    def _():
        strips(to_mate, *high)
        strips(to_other, *low)

    lane = lanes_of((BS, BS))
    total = jnp.zeros((BS, BS), F32)
    for side in range(2):
        arrays = [ice[i][2 + side] for i in range(4)]
        fields = ice_fields(*[[a[n] for n in range(a.shape[0])] for a in arrays])
        first_columns = jnp.broadcast_to(odd if side else jnp.logical_not(odd), (BS, BS))
        packed = jnp.zeros((BS, BS), F32)
        for f in range(ICE):
            at_zero = jnp.where(first_columns, fields[f], pltpu.roll(fields[f], 3, 1))
            moved = pltpu.roll(at_zero, 3 * f, 1) if f else at_zero
            packed = jnp.where((lane >= 3 * f) & (lane < 3 * f + 3), moved, packed)
        high = packed.astype(BF16).astype(F32)
        both = high + pltpu.roll(packed - high, EDGE_LANES, 1)
        total = total + (pltpu.roll(both, 2 * EDGE_LANES, 1) if side else both)
    packed_out[...] = total


def make_edges(lens, band, lon, vel, stress, area, thick, forcing):
    width = SLOTS * BS

    def at(*index):
        return lambda i, lens, band, lon: index

    def specs(n):
        return [
            pl.BlockSpec((n, 8, width), at(0, 0, 0)),
            pl.BlockSpec((n, 8, width), at(0, BS // 8 - 1, 0)),
            pl.BlockSpec((n, BS, BS), at(0, 0, 0)),
            pl.BlockSpec(
                (n, BS, BS), lambda i, lens, band, lon: (0, 0, lens[band[0], lon[0]] - 1)
            ),
        ]

    in_specs = specs(2) + specs(3) + specs(5) + specs(5)
    in_specs += [
        pl.BlockSpec((4, 16, 512), at(0, 0, 0)),
        pl.BlockSpec((4, 16, 512), at(0, BS // 16 - 1, 0)),
    ]
    return pl.pallas_call(
        edges_kernel,
        grid_spec=pltpu.PrefetchScalarGridSpec(
            num_scalar_prefetch=3,
            grid=(1,),
            in_specs=in_specs,
            out_specs=[pl.BlockSpec((SEND_ROWS, width), at(0, 0))] * 2
            + [pl.BlockSpec((BS, BS), at(0, 0))],
        ),
        out_shape=[jax.ShapeDtypeStruct((SEND_ROWS, width), F32)] * 2
        + [jax.ShapeDtypeStruct((BS, BS), F32)],
        compiler_params=pltpu.CompilerParams(vmem_limit_bytes=60 * 2**20),
        name="edges",
    )(lens, band, lon, *([vel] * 4), *([stress] * 4), *([area] * 4), *([thick] * 4), forcing, forcing)


def spread_kernel(forcing, edges, out):
    def rows16(pair, carry):
        base = pl.multiple_of(pair * 16, 16)
        for cb in range(TILE):
            parts = [
                forcing[f, pl.ds(base, 16), cb * BS : (cb + 1) * BS].astype(F32) for f in range(4)
            ]
            low = jnp.concatenate([p[0:8] for p in parts], axis=0)
            high = jnp.concatenate([p[8:16] for p in parts], axis=0)
            out[2 * pair, cb * 32 : (cb + 1) * 32, :] = low.astype(BF16)
            out[2 * pair + 1, cb * 32 : (cb + 1) * 32, :] = high.astype(BF16)
        return carry

    lax.fori_loop(0, BS // 16, rows16, 0, unroll=2)
    row = lax.broadcasted_iota(jnp.int32, (SLOTS, 8, BS), 1)
    for j in range(NLON):
        rows = edges[8 * j : 8 * j + 8, :].reshape(SLOTS, 1, BS)
        rows = jnp.where(row == 7, jnp.broadcast_to(rows, (SLOTS, 8, BS)), 0.0)
        out[j, TILE * 32 :, :] = rows.reshape(SLOTS * 8, BS).astype(BF16)


def spread(forcing, edges):
    return pl.pallas_call(
        spread_kernel,
        out_shape=jax.ShapeDtypeStruct((NLON, M1_ROWS, BS), BF16),
        in_specs=[pl.BlockSpec(memory_space=pltpu.VMEM)] * 2,
        out_specs=pl.BlockSpec(memory_space=pltpu.VMEM),
        compiler_params=pltpu.CompilerParams(vmem_limit_bytes=16 * 2**20),
        name="spread",
    )(forcing, edges)


def spread_strips_kernel(band, message, from_mate, from_other, out, hold):
    odd = lax.rem(band[0], 2) == 1

    def beside(is_north, row, rows, at, width):
        from_chip, from_next = (
            ref[row : row + rows, at : at + width] for ref in (from_mate, from_other)
        )
        use_chip = jnp.logical_not(odd) if is_north else odd
        return jnp.where(jnp.broadcast_to(use_chip, from_chip.shape), from_chip, from_next)

    for j in range(NLON):
        hold[...] = jnp.zeros(hold.shape, F32)
        f = j % 8
        if f < ICE:
            if f < MASS:
                rows = beside(j < 8, 3 * f, 3, 0, SLOTS * BS)
            else:
                rows = beside(j < 8, MASS_AT, 2, 0, SLOTS * BS)
                spare = jnp.zeros((1, SLOTS * BS), F32)
                rows = jnp.concatenate([rows, spare] if j < 8 else [spare, rows], axis=0)
            high = rows.astype(BF16).astype(F32)
            low = rows - high
            for s in range(SLOTS):
                hold[8 * s : 8 * s + 3, :] = high[:, s * BS : (s + 1) * BS]
                hold[8 * s + 3 : 8 * s + 6, :] = low[:, s * BS : (s + 1) * BS]
        field, h = j // 4, j % 4
        for cb in range(TILE):
            at = (h % 2) * 512 + cb * BS
            hold[8 * cb + 6 : 8 * cb + 7, :] = beside(h >= 2, FORCE_AT + field, 1, at, BS)
        edges = message[j, TILE * 32 :, :].astype(F32)
        out[j, TILE * 32 :, :] = (hold[...] + edges).astype(BF16)


def spread_strips(band, message, from_mate, from_other):
    return pl.pallas_call(
        spread_strips_kernel,
        out_shape=jax.ShapeDtypeStruct((NLON, M1_ROWS, BS), BF16),
        in_specs=[pl.BlockSpec(memory_space=pltpu.SMEM)]
        + [pl.BlockSpec(memory_space=pltpu.VMEM)] * 3,
        out_specs=pl.BlockSpec(memory_space=pltpu.VMEM),
        scratch_shapes=[pltpu.VMEM((SLOTS * 8, BS), F32)],
        input_output_aliases={1: 0},
        compiler_params=pltpu.CompilerParams(vmem_limit_bytes=16 * 2**20),
        name="spread_strips",
    )(band, message, from_mate, from_other)


def note_slots(table, k, count, start, odd):
    for s in range(SLOTS):
        at = start + s
        column = jnp.where(odd, NBB - 1 - at, at)
        table[jnp.where(s < count, column, NBB)] = k * SLOTS + s


def deal_kernel(lens, band, lon, got, out, groups, halos, table):
    band, lon = band[0], lon[0]
    odd = lax.rem(band, 2) == 1
    other = jnp.where(lon < 8, jnp.minimum(band + 1, NLAT - 1), jnp.maximum(band - 1, 0))
    other_odd = lax.rem(other, 2) == 1

    def fill(l, start):
        groups[pl.ds(pl.multiple_of(l * SLOTS, SLOTS), SLOTS)] = (
            got[l, TILE * 32 :, :].astype(F32).reshape(SLOTS, 8, BS)
        )
        note_slots(table, l, lens[other, l], start, other_odd)
        return start + lens[other, l]

    lax.fori_loop(0, NLON, fill, 0, unroll=UNROLL)
    row6 = lax.broadcasted_iota(jnp.int32, (8, BS), 0) == 6

    def halo(c, carry):
        own = (c // TILE) * SLOTS + lax.rem(c, TILE)
        halos[c] = jnp.where(row6, groups[own], groups[table[c]])
        return carry

    lax.fori_loop(0, NBB, halo, 0, unroll=8)
    lane = lanes_of((8, BS))

    def column_at(p):
        p = jnp.minimum(p, NBB - 1)
        return jnp.where(odd, NBB - 1 - p, p)

    def forcing(c):
        at = pl.multiple_of(lax.rem(c, TILE) * 32, 32)
        return got[c // TILE, pl.ds(at, 32), :]

    def edges(k):
        at = pl.multiple_of(lax.rem(k, NLON) * SLOTS, SLOTS)
        return groups[pl.ds(at, SLOTS), 7, :]

    def owner(k, start):
        count = lens[band, k]
        last = start + count - 1
        east = jnp.where(odd, NBB - 1 - start, last) + 1
        west = jnp.where(odd, NBB - 1 - last, start) - 1
        east, west = lax.rem(east, NBB), lax.rem(west + NBB, NBB)
        parts = []
        for e in range(SLOTS):
            c = column_at(start + e)
            out[k, e * 32 : (e + 1) * 32, :] = forcing(c)
            parts.append(halos[c])
        parts.append(jnp.where(lane < 64, halos[east], halos[west]))
        side = jnp.where(lane < 2 * EDGE_LANES, edges(k + 1), edges(k + NLON - 1))
        by_east, by_west = forcing(east).astype(F32), forcing(west).astype(F32)
        for f in range(4):
            for rows, at, col in ((by_east, EAST_AT, 0), (by_west, WEST_AT, 125)):
                there = at + 3 * f
                moved = pltpu.roll(rows[8 * f : 8 * f + 8, :], (there - col) % BS, 1)
                side = jnp.where((lane >= there) & (lane < there + 3), moved, side)
        parts.append(side)
        out[k, SLOTS * 32 :, :] = jnp.concatenate(parts, axis=0).astype(BF16)
        return start + count

    lax.fori_loop(0, NLON, owner, 0, unroll=NLON)


def deal(lens, band, lon, got):
    return pl.pallas_call(
        deal_kernel,
        out_shape=jax.ShapeDtypeStruct((NLON, M2_ROWS, BS), BF16),
        in_specs=[pl.BlockSpec(memory_space=pltpu.SMEM)] * 3
        + [pl.BlockSpec(memory_space=pltpu.VMEM)],
        out_specs=pl.BlockSpec(memory_space=pltpu.VMEM),
        scratch_shapes=[
            pltpu.VMEM((NLON * SLOTS, 8, BS), F32),
            pltpu.VMEM((NBB, 8, BS), F32),
            pltpu.SMEM((NBB + 1,), jnp.int32),
        ],
        compiler_params=pltpu.CompilerParams(vmem_limit_bytes=32 * 2**20),
        name="deal",
    )(lens, band, lon, got)


def dynamics_kernel(
    lens, band, lon, vel, stress, area, thick, got, coriolis,
    vel_out, stress_out, handed, *scratch,
):
    fields_at, (empty, sems) = list(scratch[:-2]), scratch[-2:]
    band, lon = band[0], lon[0]
    odd = lax.rem(band, 2) == 1
    count = lens[band, lon]
    groups = BS // 8

    def rows_at(g):
        return pl.ds(g * 8 if isinstance(g, int) else pl.multiple_of(g * 8, 8), 8)

    def slot_lanes(slot):
        return pl.ds(pl.multiple_of(jnp.where(odd, SLOTS - 1 - slot, slot) * BS, BS), BS)

    edge_lanes = pl.ds(SLOTS * BS, BS)

    def strips_of(j):
        group = got[j, SLOTS * 32 : SLOTS * 32 + 8 * (SLOTS + 1), :].astype(F32)
        return group.reshape(SLOTS + 1, 8, BS)

    empty[...] = jnp.zeros(empty.shape, F32)

    below4 = lax.broadcasted_iota(jnp.int32, (SLOTS + 1, 8, BS), 1) < 4
    groups_of = []
    for j in range(NLON):
        group = strips_of(j)
        groups_of.append(group)
        force_row = (BS + 6, BS + 7, BS, BS + 1)[j % 4]
        for e in range(SLOTS + 1):
            lanes = slot_lanes(e) if e < SLOTS else edge_lanes
            mine = jnp.broadcast_to(e < count, (8, BS))
            rows = jnp.where(mine, group[e], group[SLOTS])
            fields_at[UO + j // 4][force_row : force_row + 1, lanes] = rows[6:7, :]
    for f in range(ICE):
        north, south = groups_of[f], groups_of[f + 8]
        north = north + pltpu.roll(north, 5, 1)
        south = pltpu.roll(south + pltpu.roll(south, 5, 1), 5, 1)
        both = jnp.where(below4, north, south)
        for e in range(SLOTS + 1):
            lanes = slot_lanes(e) if e < SLOTS else edge_lanes
            mine = jnp.broadcast_to(e < count, (8, BS))
            fields_at[f][rows_at(groups), lanes] = jnp.where(mine, both[e], both[SLOTS])

    def derived(conc, mass, g, lanes):
        turn = coriolis[rows_at(g), :]
        if conc.shape[1] > BS:
            turn = jnp.concatenate([turn] * (conc.shape[1] // BS), axis=1)
        fields_at[STR][rows_at(g), lanes] = strength_of(conc, mass)
        fields_at[TURN][rows_at(g), lanes] = turn * mass

    derived(fields_at[AREA][rows_at(groups), :], fields_at[MASS][rows_at(groups), :], groups, slice(0, STRIP))
    far = ROWS - DEEP
    fields_at[STR][far : far + 1, :] = fields_at[AREA][far : far + 1, :]

    def own_rows(j, carry):
        packed = got[j, M2_ROWS - 16 :, :].astype(F32)[8:16, :]
        near = lanes_of((8, BS)) < 64

        def joined(east, east_lane, west, west_lane):
            return jnp.where(
                near,
                pltpu.roll(east, (BS - east_lane) % BS, 1),
                pltpu.roll(west, (125 - west_lane) % BS, 1),
            )

        forced = [joined(packed, EAST_AT + 3 * f, packed, WEST_AT + 3 * f) for f in range(4)]
        packed = packed + pltpu.roll(packed, BS - EDGE_LANES, 1)
        at_zero = pltpu.roll(packed, BS - 2 * EDGE_LANES, 1)
        east = jnp.where(odd, at_zero, packed)
        west = jnp.where(odd, packed, at_zero)
        beside = [joined(east, 3 * f, west, 3 * f) for f in range(ICE)]
        rows = rows_at(j)
        for e in range(SLOTS + 1):
            if e == SLOTS:
                fields, lanes = beside, edge_lanes
            else:
                lanes = slot_lanes(e)
                at = slice(e * BS, (e + 1) * BS)
                fields = ice_fields(
                    [vel[n, rows, at] for n in range(2)],
                    [stress[n, rows, at] for n in range(3)],
                    [area[n, rows, at] for n in range(5)],
                    [thick[n, rows, at] for n in range(5)],
                )
                mine = jnp.broadcast_to(e < count, (8, BS))
                fields = [jnp.where(mine, fields[f], beside[f]) for f in range(ICE)]
            force = forced
            if e < SLOTS:
                force = got[j, e * 32 : (e + 1) * 32, :].astype(F32)
                force = [jnp.where(mine, force[8 * f : 8 * f + 8], forced[f]) for f in range(4)]
            for f in range(4):
                fields_at[UO + f][rows_at(j), lanes] = force[f]
            for f in range(ICE):
                fields_at[f][rows_at(j), lanes] = fields[f]
            derived(fields[AREA], fields[MASS], j, lanes)
        return carry

    lax.fori_loop(0, groups, own_rows, 0, unroll=UNROLL_OWN)

    cells = (8, WIDE)
    row = lax.broadcasted_iota(jnp.int32, cells, 0)

    def load(f, g, c, width=WIDE):
        return fields_at[f][rows_at(g), c : c + width]

    def north_of(f, x, g, c):
        above = 0 if isinstance(g, int) and g == groups else g + 1
        return pltpu.roll(jnp.where(row == 0, load(f, above, c), x), 7, 0)

    def south_of(f, x, g, c):
        below = lax.rem(g + groups, groups + 1)
        return pltpu.roll(jnp.where(row == 7, load(f, below, c), x), 1, 0)

    def east_of(f, x, g, c):
        if WIDE == STRIP:
            return pltpu.roll(x, STRIP - 1, 1)
        more = load(f, g, (c + WIDE) % STRIP, BS)
        return pltpu.roll(jnp.concatenate([x, more], axis=1), WIDE + BS - 1, 1)[:, :WIDE]

    def west_of(f, x, g, c):
        if WIDE == STRIP:
            return pltpu.roll(x, 1, 1)
        more = load(f, g, (c - BS) % STRIP, BS)
        return pltpu.roll(jnp.concatenate([more, x], axis=1), 1, 1)[:, BS:]

    def stress_rows(g, new, last):
        for c in range(0, STRIP, WIDE):
            u, v = load(U, g, c), load(V, g, c)
            exx = east_of(U, u, g, c) - u
            eyy = north_of(V, v, g, c) - v
            shr = (north_of(U, u, g, c) - u) + (east_of(V, v, g, c) - v)
            div = exx + eyy
            ten = exx - eyy
            square = div * div + 0.25 * (ten * ten + shr * shr) + DMIN_SQ
            sixth = load(STR, g, c)
            half = sixth * lax.rsqrt(square)
            eighth = 0.25 * half
            both = half * div - sixth
            apart = eighth * ten
            sxx = (2.0 / 3.0) * load(SXX, g, c) + (both + apart)
            syy = (2.0 / 3.0) * load(SYY, g, c) + (both - apart)
            at = slice(c, c + WIDE)
            new[SXX][rows_at(g), at] = sxx
            new[SYY][rows_at(g), at] = syy
            new[S12][rows_at(g), at] = (2.0 / 3.0) * load(S12, g, c) + eighth * shr
            if last:
                new[S1_OUT][rows_at(g), at] = sxx + syy
                new[S2_OUT][rows_at(g), at] = sxx - syy

    def velocity_rows(g, new, beyond=None, last=False):
        for c in range(0, STRIP, WIDE):
            sxx, syy, s12 = load(SXX, g, c), load(SYY, g, c), load(S12, g, c)
            fx = sxx - west_of(SXX, sxx, g, c) + s12 - south_of(S12, s12, g, c)
            fy = s12 - west_of(S12, s12, g, c) + syy - south_of(SYY, syy, g, c)
            u, v, uo, vo = [load(f, g, c) for f in (U, V, UO, VO)]
            m, conc, tx, ty = [load(f, g, c) for f in (MASS, AREA, TX, TY)]
            du, dv = uo - u, vo - v
            square = du * du + dv * dv + SPEED_SQ
            drag = conc * (square * lax.rsqrt(square))
            d = m + drag
            q = load(TURN, g, c)
            ru = m * u + fx + tx + drag * uo
            rv = m * v + fy + ty + drag * vo
            inv = 1.0 / (d * d + q * q)
            u = (d * ru + q * rv) * inv
            v = (d * rv - q * ru) * inv
            if beyond is not None:
                u = jnp.where(beyond, 0.0, u)
                v = jnp.where(beyond, 0.0, v)
            at = slice(c, c + WIDE)
            new[U][rows_at(g), at] = u
            new[V][rows_at(g), at] = v
            if last:
                du, dv = u - uo, v - vo
                square = du * du + dv * dv + SPEED_SQ
                drag = conc * (square * lax.rsqrt(square))
                x = (1.0 - conc) * tx + drag * du
                y = (1.0 - conc) * ty + drag * dv
                for i in range(WIDE // BS):
                    p = c // BS + i
                    if p < SLOTS:
                        slot = jnp.where(odd, SLOTS - 1 - p, p)
                        pair = [x[:, i * BS : (i + 1) * BS], y[:, i * BS : (i + 1) * BS]]
                        handed[g, pl.ds(pl.multiple_of(slot * 16, 16), 16), :] = (
                            jnp.concatenate(pair, axis=0).astype(BF16)
                        )

    def copies(fields, out, row0, rows, sem0):
        made = []
        for n, f in enumerate(fields):
            for e in range(SLOTS):
                to = out.at[n, pl.ds(row0, rows), pl.ds(e * BS, BS)]
                sem = sems.at[sem0 + n * SLOTS + e]
                block = fields_at[f].at[pl.ds(row0, rows), slot_lanes(e)]
                made.append((e, pltpu.make_async_copy(block, to, sem),
                             pltpu.make_async_copy(empty.at[pl.ds(0, rows), :], to, sem)))
        return made

    def start(made):
        for e, full, none in made:
            @pl.when(e < count)
            def _():
                full.start()

            @pl.when(e >= count)
            def _():
                none.start()

    pending = []
    for it in range(ITERS):
        last = it == ITERS - 1
        new = {f: fields_at[n] for f, n in zip(RENEWED, range(S2_OUT + 1, S2_OUT + 6))}
        new[S1_OUT], new[S2_OUT] = fields_at[S1_OUT], fields_at[S2_OUT]

        def stress_step(g, carry):
            stress_rows(g, new, last)
            return carry

        lax.fori_loop(0, groups, stress_step, 0, unroll=UNROLL_STRESS)
        stress_rows(groups, new, last)
        for f in (SXX, SYY, S12):
            n = S2_OUT + 1 + RENEWED.index(f)
            fields_at[f], fields_at[n] = fields_at[n], fields_at[f]
        if last:
            made = copies((S1_OUT, S2_OUT, S12), stress_out, 0, BS, 0)
            start(made)
            pending += made
        else:
            beyond = (row < 4) & (band == NLAT - 1) | (row >= 4) & (band == 0)
            velocity_rows(groups, new, beyond)

        def velocity_step(g, carry):
            velocity_rows(g, new, None, last)
            return carry

        if last:
            for h in range(2):
                half = groups // 2
                lax.fori_loop(h * half, (h + 1) * half, velocity_step, 0, unroll=UNROLL_VELOCITY)
                made = copies((U_NEW, V_NEW), vel_out, h * BS // 2, BS // 2, 24 + 16 * h)
                start(made)
                pending += made
        else:
            lax.fori_loop(0, groups, velocity_step, 0, unroll=UNROLL_VELOCITY)
            for f in (U, V):
                n = S2_OUT + 1 + RENEWED.index(f)
                fields_at[f], fields_at[n] = fields_at[n], fields_at[f]
    for _, full, _ in pending:
        full.wait()


def dynamics(lens, band, lon, vel, stress, area, thick, got, coriolis):
    width = SLOTS * BS
    vmem = pl.BlockSpec(memory_space=pltpu.VMEM)
    smem = pl.BlockSpec(memory_space=pltpu.SMEM)
    return pl.pallas_call(
        dynamics_kernel,
        in_specs=[smem] * 3 + [vmem] * 6,
        out_specs=[pl.BlockSpec(memory_space=pl.ANY)] * 2 + [vmem],
        scratch_shapes=[
            *[pltpu.VMEM((ROWS, STRIP), F32) for _ in range(S2_OUT + 6)],
            pltpu.VMEM((BS, BS), F32),
            pltpu.SemaphoreType.DMA((24 + 32,)),
        ],
        out_shape=[
            jax.ShapeDtypeStruct((2, BS, width), F32),
            jax.ShapeDtypeStruct((3, BS, width), F32),
            jax.ShapeDtypeStruct((NLON, M3_ROWS, BS), BF16),
        ],
        compiler_params=pltpu.CompilerParams(vmem_limit_bytes=32 * 2**20),
        name="dynamics",
    )(lens, band, lon, vel, stress, area, thick, got, coriolis)


def sort_kernel(lens, band, got, out, table):
    odd = lax.rem(band[0], 2) == 1

    def owner(k, start):
        note_slots(table, k, lens[band[0], k], start, odd)
        return start + lens[band[0], k]

    lax.fori_loop(0, NLON, owner, 0, unroll=NLON)

    def block(c, carry):
        out[c] = got[table[c]]
        return carry

    lax.fori_loop(0, NBB, block, 0, unroll=16)


def sort_back(lens, band, got):
    return pl.pallas_call(
        sort_kernel,
        out_shape=jax.ShapeDtypeStruct((NBB, 16, BS), BF16),
        in_specs=[pl.BlockSpec(memory_space=pltpu.SMEM)] * 2
        + [pl.BlockSpec(memory_space=pltpu.VMEM)],
        out_specs=pl.BlockSpec(memory_space=pltpu.VMEM),
        scratch_shapes=[pltpu.SMEM((NBB + 1,), jnp.int32)],
        compiler_params=pltpu.CompilerParams(vmem_limit_bytes=16 * 2**20),
        name="sort_back",
    )(lens, band, got)


def settle_kernel(got, out):
    def rows16(pair, carry):
        rows = pl.ds(pl.multiple_of(pair * 16, 16), 16)
        for cb in range(TILE):
            a = got[2 * pair, cb * 16 : (cb + 1) * 16, :].astype(F32)
            b = got[2 * pair + 1, cb * 16 : (cb + 1) * 16, :].astype(F32)
            lanes = slice(cb * BS, (cb + 1) * BS)
            out[0, rows, lanes] = jnp.concatenate([a[0:8], b[0:8]], axis=0).astype(BF16)
            out[1, rows, lanes] = jnp.concatenate([a[8:16], b[8:16]], axis=0).astype(BF16)
        return carry

    lax.fori_loop(0, BS // 16, rows16, 0, unroll=8)


def settle(got):
    return pl.pallas_call(
        settle_kernel,
        out_shape=jax.ShapeDtypeStruct((2, BS, TILE * BS), BF16),
        in_specs=[pl.BlockSpec(memory_space=pltpu.VMEM)],
        out_specs=pl.BlockSpec(memory_space=pltpu.VMEM),
        compiler_params=pltpu.CompilerParams(vmem_limit_bytes=16 * 2**20),
        name="settle",
    )(got)


def to_all(block):
    return lax.all_to_all(block, "lon", 0, 0, tiled=True)


def body(ocean_forcing, ice_velocity, ice_stress, cat_area, cat_thick, run_lengths):
    band_idx = lax.axis_index("lat")
    lon_idx = lax.axis_index("lon")
    lens = run_lengths
    place = (jnp.reshape(band_idx, (1,)), jnp.reshape(lon_idx, (1,)))
    ice = (ice_velocity, ice_stress, cat_area, cat_thick)
    place_of = jnp.arange(ROWS, dtype=jnp.int32)
    place_of = jnp.where(place_of < BS + 4, place_of, place_of - ROWS)
    rows = (band_idx * BS + place_of).astype(F32)
    latitude = -78.0 + 168.0 * (rows + 0.5) / (BS * NLAT)
    coriolis = jnp.broadcast_to(jnp.sin(latitude * (jnp.pi / 180.0))[:, None], (ROWS, BS))
    to_mate, to_other, edges = make_edges(lens, *place, *ice, ocean_forcing)
    message = spread(ocean_forcing, edges)
    pairs = [(b, b ^ 1) for b in range(NLAT)]
    from_mate = lax.ppermute(to_mate, "lat", pairs)
    pairs = [(b, b + 1 if b % 2 else b - 1) for b in range(1, NLAT - 1)]
    from_other = lax.ppermute(to_other, "lat", pairs)
    from_mate, from_other, coriolis = lax.optimization_barrier((from_mate, from_other, coriolis))
    message = spread_strips(place[0], message, from_mate, from_other)
    dealt = to_all(deal(lens, *place, to_all(message)))
    velocity_out, stress_out, handed = dynamics(lens, *place, *ice, dealt, coriolis)
    handed = to_all(handed).reshape(NLON * SLOTS, 16, BS)
    back = sort_back(lens, place[0], handed).reshape(NLON, M4_ROWS, BS)
    return (velocity_out, stress_out, settle(to_all(back)))


def solution(mesh):
    slots = P(None, None, ("lat", "lon"))
    grid = P(None, "lat", "lon")
    return jax.shard_map(
        body,
        mesh=mesh,
        in_specs=(grid, slots, slots, slots, slots, P()),
        out_specs=(slots, slots, grid),
        check_vma=False,
    )
```

```python
import functools

import jax
import jax.numpy as jnp
from jax import lax
from jax.experimental import pallas as pl
from jax.experimental.pallas import tpu as pltpu
from jax.sharding import PartitionSpec as P

BS = 128
ITERS = 3
NLAT = 8
NLON = 16
SLOTS = 8
NBB = 64
TILE = 4
DEEP = 3
PSTAR = 2.0
CSTAR = 20.0
DMIN_SQ = 0.01
SPEED_SQ = 0.01
ICE = 7
U, V, SXX, SYY, S12, AREA, MASS, STR, UO, VO, TX, TY, TURN, S1_OUT, S2_OUT, U_NEW, V_NEW = range(17)
RENEWED = (U, V, SXX, SYY, S12)
EDGE_LANES = 3 * ICE
EAST_AT = 4 * EDGE_LANES
WEST_AT = EAST_AT + 12
STRIP = (SLOTS + 1) * BS
UNROLL = 4
UNROLL_OWN = 8
UNROLL_STRESS = 16
UNROLL_VELOCITY = 8
WIDE = 3 * BS
ROWS = BS + 8
SEND_ROWS = 24
MASS_AT, FORCE_AT = 18, 20
M1_ROWS = TILE * 32 + SLOTS * 8
M2_ROWS = SLOTS * 32 + (SLOTS + 1) * 8 + 8
M3_ROWS = SLOTS * 16
M4_ROWS = TILE * 16
F32 = jnp.float32
BF16 = jnp.bfloat16


def lanes_of(shape):
    return lax.broadcasted_iota(jnp.int32, shape, len(shape) - 1)


def ice_fields(vel, stress, area, thick):
    conc = area[0] + area[1] + area[2] + area[3] + area[4]
    mass = area[0] * thick[0]
    for n in range(1, 5):
        mass = mass + area[n] * thick[n]
    sxx, syy = 0.5 * (stress[0] + stress[1]), 0.5 * (stress[0] - stress[1])
    return [vel[0], vel[1], sxx, syy, stress[2], conc, mass]


def strength_of(conc, mass):
    return (PSTAR / 6.0) * mass * jnp.exp(-CSTAR * (1.0 - conc))


def edges_kernel(lens, band, lon, *refs):
    ice = [refs[4 * i : 4 * i + 4] for i in range(4)]
    f_low, f_high, to_mate, to_other, packed_out = refs[16:]
    odd = lax.rem(band[0], 2) == 1

    def strips(out, which, force, row0, frow0):
        arrays = [ice[i][which] for i in range(4)]
        fields = ice_fields(*[[a[n] for n in range(a.shape[0])] for a in arrays])
        for f in range(MASS):
            out[3 * f : 3 * f + 3, :] = fields[f][row0 : row0 + 3, :]
        near = row0 if row0 == 0 else row0 + 1
        out[MASS_AT : MASS_AT + 2, :] = fields[MASS][near : near + 2, :]
        if row0:
            strength = strength_of(fields[AREA], fields[MASS])
            out[3 * AREA : 3 * AREA + 1, :] = strength[row0 : row0 + 1, :]
        for f in range(4):
            rows = force[f].astype(F32)
            at = FORCE_AT + f
            out[at : at + 1, 0:512] = rows[frow0 : frow0 + 1, :]
            out[at : at + 1, 512:1024] = rows[frow0 + 1 : frow0 + 2, :]

    low, high = (0, f_low, 0, 0), (1, f_high, 5, 14)

    @pl.when(odd)
    def _():
        strips(to_mate, *low)
        strips(to_other, *high)

    @pl.when(jnp.logical_not(odd))
    def _():
        strips(to_mate, *high)
        strips(to_other, *low)

    lane = lanes_of((BS, BS))
    total = jnp.zeros((BS, BS), F32)
    for side in range(2):
        arrays = [ice[i][2 + side] for i in range(4)]
        fields = ice_fields(*[[a[n] for n in range(a.shape[0])] for a in arrays])
        first_columns = jnp.broadcast_to(odd if side else jnp.logical_not(odd), (BS, BS))
        packed = jnp.zeros((BS, BS), F32)
        for f in range(ICE):
            at_zero = jnp.where(first_columns, fields[f], pltpu.roll(fields[f], 3, 1))
            moved = pltpu.roll(at_zero, 3 * f, 1) if f else at_zero
            packed = jnp.where((lane >= 3 * f) & (lane < 3 * f + 3), moved, packed)
        high = packed.astype(BF16).astype(F32)
        both = high + pltpu.roll(packed - high, EDGE_LANES, 1)
        total = total + (pltpu.roll(both, 2 * EDGE_LANES, 1) if side else both)
    packed_out[...] = total


def make_edges(lens, band, lon, vel, stress, area, thick, forcing):
    width = SLOTS * BS

    def at(*index):
        return lambda i, lens, band, lon: index

    def specs(n):
        return [
            pl.BlockSpec((n, 8, width), at(0, 0, 0)),
            pl.BlockSpec((n, 8, width), at(0, BS // 8 - 1, 0)),
            pl.BlockSpec((n, BS, BS), at(0, 0, 0)),
            pl.BlockSpec(
                (n, BS, BS), lambda i, lens, band, lon: (0, 0, lens[band[0], lon[0]] - 1)
            ),
        ]

    in_specs = specs(2) + specs(3) + specs(5) + specs(5)
    in_specs += [
        pl.BlockSpec((4, 16, 512), at(0, 0, 0)),
        pl.BlockSpec((4, 16, 512), at(0, BS // 16 - 1, 0)),
    ]
    return pl.pallas_call(
        edges_kernel,
        grid_spec=pltpu.PrefetchScalarGridSpec(
            num_scalar_prefetch=3,
            grid=(1,),
            in_specs=in_specs,
            out_specs=[pl.BlockSpec((SEND_ROWS, width), at(0, 0))] * 2
            + [pl.BlockSpec((BS, BS), at(0, 0))],
        ),
        out_shape=[jax.ShapeDtypeStruct((SEND_ROWS, width), F32)] * 2
        + [jax.ShapeDtypeStruct((BS, BS), F32)],
        compiler_params=pltpu.CompilerParams(vmem_limit_bytes=60 * 2**20),
        name="edges",
    )(lens, band, lon, *([vel] * 4), *([stress] * 4), *([area] * 4), *([thick] * 4), forcing, forcing)


def spread_kernel(forcing, edges, out):
    def rows16(pair, carry):
        base = pl.multiple_of(pair * 16, 16)
        for cb in range(TILE):
            parts = [
                forcing[f, pl.ds(base, 16), cb * BS : (cb + 1) * BS].astype(F32) for f in range(4)
            ]
            low = jnp.concatenate([p[0:8] for p in parts], axis=0)
            high = jnp.concatenate([p[8:16] for p in parts], axis=0)
            out[2 * pair, cb * 32 : (cb + 1) * 32, :] = low.astype(BF16)
            out[2 * pair + 1, cb * 32 : (cb + 1) * 32, :] = high.astype(BF16)
        return carry

    lax.fori_loop(0, BS // 16, rows16, 0, unroll=2)
    row = lax.broadcasted_iota(jnp.int32, (SLOTS, 8, BS), 1)
    for j in range(NLON):
        rows = edges[8 * j : 8 * j + 8, :].reshape(SLOTS, 1, BS)
        rows = jnp.where(row == 7, jnp.broadcast_to(rows, (SLOTS, 8, BS)), 0.0)
        out[j, TILE * 32 :, :] = rows.reshape(SLOTS * 8, BS).astype(BF16)


def spread(forcing, edges):
    return pl.pallas_call(
        spread_kernel,
        out_shape=jax.ShapeDtypeStruct((NLON, M1_ROWS, BS), BF16),
        in_specs=[pl.BlockSpec(memory_space=pltpu.VMEM)] * 2,
        out_specs=pl.BlockSpec(memory_space=pltpu.VMEM),
        compiler_params=pltpu.CompilerParams(vmem_limit_bytes=16 * 2**20),
        name="spread",
    )(forcing, edges)


def spread_strips_kernel(band, message, from_mate, from_other, out, hold):
    odd = lax.rem(band[0], 2) == 1

    def beside(is_north, row, rows, at, width):
        from_chip, from_next = (
            ref[row : row + rows, at : at + width] for ref in (from_mate, from_other)
        )
        use_chip = jnp.logical_not(odd) if is_north else odd
        return jnp.where(jnp.broadcast_to(use_chip, from_chip.shape), from_chip, from_next)

    for j in range(NLON):
        hold[...] = jnp.zeros(hold.shape, F32)
        f = j % 8
        if f < ICE:
            if f < MASS:
                rows = beside(j < 8, 3 * f, 3, 0, SLOTS * BS)
            else:
                rows = beside(j < 8, MASS_AT, 2, 0, SLOTS * BS)
                spare = jnp.zeros((1, SLOTS * BS), F32)
                rows = jnp.concatenate([rows, spare] if j < 8 else [spare, rows], axis=0)
            high = rows.astype(BF16).astype(F32)
            low = rows - high
            for s in range(SLOTS):
                hold[8 * s : 8 * s + 3, :] = high[:, s * BS : (s + 1) * BS]
                hold[8 * s + 3 : 8 * s + 6, :] = low[:, s * BS : (s + 1) * BS]
        field, h = j // 4, j % 4
        for cb in range(TILE):
            at = (h % 2) * 512 + cb * BS
            hold[8 * cb + 6 : 8 * cb + 7, :] = beside(h >= 2, FORCE_AT + field, 1, at, BS)
        edges = message[j, TILE * 32 :, :].astype(F32)
        out[j, TILE * 32 :, :] = (hold[...] + edges).astype(BF16)


def spread_strips(band, message, from_mate, from_other):
    return pl.pallas_call(
        spread_strips_kernel,
        out_shape=jax.ShapeDtypeStruct((NLON, M1_ROWS, BS), BF16),
        in_specs=[pl.BlockSpec(memory_space=pltpu.SMEM)]
        + [pl.BlockSpec(memory_space=pltpu.VMEM)] * 3,
        out_specs=pl.BlockSpec(memory_space=pltpu.VMEM),
        scratch_shapes=[pltpu.VMEM((SLOTS * 8, BS), F32)],
        input_output_aliases={1: 0},
        compiler_params=pltpu.CompilerParams(vmem_limit_bytes=16 * 2**20),
        name="spread_strips",
    )(band, message, from_mate, from_other)


def note_slots(table, k, count, start, odd):
    for s in range(SLOTS):
        at = start + s
        column = jnp.where(odd, NBB - 1 - at, at)
        table[jnp.where(s < count, column, NBB)] = k * SLOTS + s


def deal_kernel(lens, band, lon, got, out, groups, halos, table):
    band, lon = band[0], lon[0]
    odd = lax.rem(band, 2) == 1
    other = jnp.where(lon < 8, jnp.minimum(band + 1, NLAT - 1), jnp.maximum(band - 1, 0))
    other_odd = lax.rem(other, 2) == 1

    def fill(l, start):
        groups[pl.ds(pl.multiple_of(l * SLOTS, SLOTS), SLOTS)] = (
            got[l, TILE * 32 :, :].astype(F32).reshape(SLOTS, 8, BS)
        )
        note_slots(table, l, lens[other, l], start, other_odd)
        return start + lens[other, l]

    lax.fori_loop(0, NLON, fill, 0, unroll=UNROLL)
    row6 = lax.broadcasted_iota(jnp.int32, (8, BS), 0) == 6

    def halo(c, carry):
        own = (c // TILE) * SLOTS + lax.rem(c, TILE)
        halos[c] = jnp.where(row6, groups[own], groups[table[c]])
        return carry

    lax.fori_loop(0, NBB, halo, 0, unroll=8)
    lane = lanes_of((8, BS))

    def column_at(p):
        p = jnp.minimum(p, NBB - 1)
        return jnp.where(odd, NBB - 1 - p, p)

    def forcing(c):
        at = pl.multiple_of(lax.rem(c, TILE) * 32, 32)
        return got[c // TILE, pl.ds(at, 32), :]

    def edges(k):
        at = pl.multiple_of(lax.rem(k, NLON) * SLOTS, SLOTS)
        return groups[pl.ds(at, SLOTS), 7, :]

    def owner(k, start):
        count = lens[band, k]
        last = start + count - 1
        east = jnp.where(odd, NBB - 1 - start, last) + 1
        west = jnp.where(odd, NBB - 1 - last, start) - 1
        east, west = lax.rem(east, NBB), lax.rem(west + NBB, NBB)
        parts = []
        for e in range(SLOTS):
            c = column_at(start + e)
            out[k, e * 32 : (e + 1) * 32, :] = forcing(c)
            parts.append(halos[c])
        parts.append(jnp.where(lane < 64, halos[east], halos[west]))
        side = jnp.where(lane < 2 * EDGE_LANES, edges(k + 1), edges(k + NLON - 1))
        by_east, by_west = forcing(east).astype(F32), forcing(west).astype(F32)
        for f in range(4):
            for rows, at, col in ((by_east, EAST_AT, 0), (by_west, WEST_AT, 125)):
                there = at + 3 * f
                moved = pltpu.roll(rows[8 * f : 8 * f + 8, :], (there - col) % BS, 1)
                side = jnp.where((lane >= there) & (lane < there + 3), moved, side)
        parts.append(side)
        out[k, SLOTS * 32 :, :] = jnp.concatenate(parts, axis=0).astype(BF16)
        return start + count

    lax.fori_loop(0, NLON, owner, 0, unroll=NLON)


def deal(lens, band, lon, got):
    return pl.pallas_call(
        deal_kernel,
        out_shape=jax.ShapeDtypeStruct((NLON, M2_ROWS, BS), BF16),
        in_specs=[pl.BlockSpec(memory_space=pltpu.SMEM)] * 3
        + [pl.BlockSpec(memory_space=pltpu.VMEM)],
        out_specs=pl.BlockSpec(memory_space=pltpu.VMEM),
        scratch_shapes=[
            pltpu.VMEM((NLON * SLOTS, 8, BS), F32),
            pltpu.VMEM((NBB, 8, BS), F32),
            pltpu.SMEM((NBB + 1,), jnp.int32),
        ],
        compiler_params=pltpu.CompilerParams(vmem_limit_bytes=32 * 2**20),
        name="deal",
    )(lens, band, lon, got)


def dynamics_kernel(
    lens, band, lon, vel, stress, area, thick, got, coriolis,
    vel_out, stress_out, handed, *scratch,
):
    fields_at, (empty, sems) = list(scratch[:-2]), scratch[-2:]
    band, lon = band[0], lon[0]
    odd = lax.rem(band, 2) == 1
    count = lens[band, lon]
    groups = BS // 8

    def rows_at(g):
        return pl.ds(g * 8 if isinstance(g, int) else pl.multiple_of(g * 8, 8), 8)

    def slot_lanes(slot):
        return pl.ds(pl.multiple_of(jnp.where(odd, SLOTS - 1 - slot, slot) * BS, BS), BS)

    edge_lanes = pl.ds(SLOTS * BS, BS)

    def strips_of(j):
        group = got[j, SLOTS * 32 : SLOTS * 32 + 8 * (SLOTS + 1), :].astype(F32)
        return group.reshape(SLOTS + 1, 8, BS)

    empty[...] = jnp.zeros(empty.shape, F32)

    below4 = lax.broadcasted_iota(jnp.int32, (SLOTS + 1, 8, BS), 1) < 4
    groups_of = []
    for j in range(NLON):
        group = strips_of(j)
        groups_of.append(group)
        force_row = (BS + 6, BS + 7, BS, BS + 1)[j % 4]
        for e in range(SLOTS + 1):
            lanes = slot_lanes(e) if e < SLOTS else edge_lanes
            mine = jnp.broadcast_to(e < count, (8, BS))
            rows = jnp.where(mine, group[e], group[SLOTS])
            fields_at[UO + j // 4][force_row : force_row + 1, lanes] = rows[6:7, :]
    for f in range(ICE):
        north, south = groups_of[f], groups_of[f + 8]
        north = north + pltpu.roll(north, 5, 1)
        south = pltpu.roll(south + pltpu.roll(south, 5, 1), 5, 1)
        both = jnp.where(below4, north, south)
        for e in range(SLOTS + 1):
            lanes = slot_lanes(e) if e < SLOTS else edge_lanes
            mine = jnp.broadcast_to(e < count, (8, BS))
            fields_at[f][rows_at(groups), lanes] = jnp.where(mine, both[e], both[SLOTS])

    def derived(conc, mass, g, lanes):
        turn = coriolis[rows_at(g), :]
        if conc.shape[1] > BS:
            turn = jnp.concatenate([turn] * (conc.shape[1] // BS), axis=1)
        fields_at[STR][rows_at(g), lanes] = strength_of(conc, mass)
        fields_at[TURN][rows_at(g), lanes] = turn * mass

    derived(fields_at[AREA][rows_at(groups), :], fields_at[MASS][rows_at(groups), :], groups, slice(0, STRIP))
    far = ROWS - DEEP
    fields_at[STR][far : far + 1, :] = fields_at[AREA][far : far + 1, :]

    def own_rows(j, carry):
        packed = got[j, M2_ROWS - 16 :, :].astype(F32)[8:16, :]
        near = lanes_of((8, BS)) < 64

        def joined(east, east_lane, west, west_lane):
            return jnp.where(
                near,
                pltpu.roll(east, (BS - east_lane) % BS, 1),
                pltpu.roll(west, (125 - west_lane) % BS, 1),
            )

        forced = [joined(packed, EAST_AT + 3 * f, packed, WEST_AT + 3 * f) for f in range(4)]
        packed = packed + pltpu.roll(packed, BS - EDGE_LANES, 1)
        at_zero = pltpu.roll(packed, BS - 2 * EDGE_LANES, 1)
        east = jnp.where(odd, at_zero, packed)
        west = jnp.where(odd, packed, at_zero)
        beside = [joined(east, 3 * f, west, 3 * f) for f in range(ICE)]
        rows = rows_at(j)
        for e in range(SLOTS + 1):
            if e == SLOTS:
                fields, lanes = beside, edge_lanes
            else:
                lanes = slot_lanes(e)
                at = slice(e * BS, (e + 1) * BS)
                fields = ice_fields(
                    [vel[n, rows, at] for n in range(2)],
                    [stress[n, rows, at] for n in range(3)],
                    [area[n, rows, at] for n in range(5)],
                    [thick[n, rows, at] for n in range(5)],
                )
                mine = jnp.broadcast_to(e < count, (8, BS))
                fields = [jnp.where(mine, fields[f], beside[f]) for f in range(ICE)]
            force = forced
            if e < SLOTS:
                force = got[j, e * 32 : (e + 1) * 32, :].astype(F32)
                force = [jnp.where(mine, force[8 * f : 8 * f + 8], forced[f]) for f in range(4)]
            for f in range(4):
                fields_at[UO + f][rows_at(j), lanes] = force[f]
            for f in range(ICE):
                fields_at[f][rows_at(j), lanes] = fields[f]
            derived(fields[AREA], fields[MASS], j, lanes)
        return carry

    lax.fori_loop(0, groups, own_rows, 0, unroll=UNROLL_OWN)

    cells = (8, WIDE)
    row = lax.broadcasted_iota(jnp.int32, cells, 0)

    def load(f, g, c, width=WIDE):
        return fields_at[f][rows_at(g), c : c + width]

    def north_of(f, x, g, c):
        above = 0 if isinstance(g, int) and g == groups else g + 1
        return pltpu.roll(jnp.where(row == 0, load(f, above, c), x), 7, 0)

    def south_of(f, x, g, c):
        below = lax.rem(g + groups, groups + 1)
        return pltpu.roll(jnp.where(row == 7, load(f, below, c), x), 1, 0)

    def east_of(f, x, g, c):
        if WIDE == STRIP:
            return pltpu.roll(x, STRIP - 1, 1)
        more = load(f, g, (c + WIDE) % STRIP, BS)
        return pltpu.roll(jnp.concatenate([x, more], axis=1), WIDE + BS - 1, 1)[:, :WIDE]

    def west_of(f, x, g, c):
        if WIDE == STRIP:
            return pltpu.roll(x, 1, 1)
        more = load(f, g, (c - BS) % STRIP, BS)
        return pltpu.roll(jnp.concatenate([more, x], axis=1), 1, 1)[:, BS:]

    def stress_rows(g, new, last):
        for c in range(0, STRIP, WIDE):
            u, v = load(U, g, c), load(V, g, c)
            exx = east_of(U, u, g, c) - u
            eyy = north_of(V, v, g, c) - v
            shr = (north_of(U, u, g, c) - u) + (east_of(V, v, g, c) - v)
            div = exx + eyy
            ten = exx - eyy
            square = div * div + 0.25 * (ten * ten + shr * shr) + DMIN_SQ
            sixth = load(STR, g, c)
            half = sixth * lax.rsqrt(square)
            eighth = 0.25 * half
            both = half * div - sixth
            apart = eighth * ten
            sxx = (2.0 / 3.0) * load(SXX, g, c) + (both + apart)
            syy = (2.0 / 3.0) * load(SYY, g, c) + (both - apart)
            at = slice(c, c + WIDE)
            new[SXX][rows_at(g), at] = sxx
            new[SYY][rows_at(g), at] = syy
            new[S12][rows_at(g), at] = (2.0 / 3.0) * load(S12, g, c) + eighth * shr
            if last:
                new[S1_OUT][rows_at(g), at] = sxx + syy
                new[S2_OUT][rows_at(g), at] = sxx - syy

    def velocity_rows(g, new, beyond=None, last=False):
        for c in range(0, STRIP, WIDE):
            sxx, syy, s12 = load(SXX, g, c), load(SYY, g, c), load(S12, g, c)
            fx = sxx - west_of(SXX, sxx, g, c) + s12 - south_of(S12, s12, g, c)
            fy = s12 - west_of(S12, s12, g, c) + syy - south_of(SYY, syy, g, c)
            u, v, uo, vo = [load(f, g, c) for f in (U, V, UO, VO)]
            m, conc, tx, ty = [load(f, g, c) for f in (MASS, AREA, TX, TY)]
            du, dv = uo - u, vo - v
            square = du * du + dv * dv + SPEED_SQ
            drag = conc * (square * lax.rsqrt(square))
            d = m + drag
            q = load(TURN, g, c)
            ru = m * u + fx + tx + drag * uo
            rv = m * v + fy + ty + drag * vo
            inv = 1.0 / (d * d + q * q)
            u = (d * ru + q * rv) * inv
            v = (d * rv - q * ru) * inv
            if beyond is not None:
                u = jnp.where(beyond, 0.0, u)
                v = jnp.where(beyond, 0.0, v)
            at = slice(c, c + WIDE)
            new[U][rows_at(g), at] = u
            new[V][rows_at(g), at] = v
            if last:
                du, dv = u - uo, v - vo
                square = du * du + dv * dv + SPEED_SQ
                drag = conc * (square * lax.rsqrt(square))
                x = (1.0 - conc) * tx + drag * du
                y = (1.0 - conc) * ty + drag * dv
                for i in range(WIDE // BS):
                    p = c // BS + i
                    if p < SLOTS:
                        slot = jnp.where(odd, SLOTS - 1 - p, p)
                        pair = [x[:, i * BS : (i + 1) * BS], y[:, i * BS : (i + 1) * BS]]
                        handed[g, pl.ds(pl.multiple_of(slot * 16, 16), 16), :] = (
                            jnp.concatenate(pair, axis=0).astype(BF16)
                        )

    def copies(fields, out, row0, rows, sem0):
        made = []
        for n, f in enumerate(fields):
            for e in range(SLOTS):
                to = out.at[n, pl.ds(row0, rows), pl.ds(e * BS, BS)]
                sem = sems.at[sem0 + n * SLOTS + e]
                block = fields_at[f].at[pl.ds(row0, rows), slot_lanes(e)]
                made.append((e, pltpu.make_async_copy(block, to, sem),
                             pltpu.make_async_copy(empty.at[pl.ds(0, rows), :], to, sem)))
        return made

    def start(made):
        for e, full, none in made:
            @pl.when(e < count)
            def _():
                full.start()

            @pl.when(e >= count)
            def _():
                none.start()

    pending = []
    for it in range(ITERS):
        last = it == ITERS - 1
        new = {f: fields_at[n] for f, n in zip(RENEWED, range(S2_OUT + 1, S2_OUT + 6))}
        new[S1_OUT], new[S2_OUT] = fields_at[S1_OUT], fields_at[S2_OUT]

        def stress_step(g, carry):
            stress_rows(g, new, last)
            return carry

        lax.fori_loop(0, groups, stress_step, 0, unroll=UNROLL_STRESS)
        stress_rows(groups, new, last)
        for f in (SXX, SYY, S12):
            n = S2_OUT + 1 + RENEWED.index(f)
            fields_at[f], fields_at[n] = fields_at[n], fields_at[f]
        if last:
            made = copies((S1_OUT, S2_OUT, S12), stress_out, 0, BS, 0)
            start(made)
            pending += made
        else:
            beyond = (row < 4) & (band == NLAT - 1) | (row >= 4) & (band == 0)
            velocity_rows(groups, new, beyond)

        def velocity_step(g, carry):
            velocity_rows(g, new, None, last)
            return carry

        if last:
            for h in range(2):
                half = groups // 2
                lax.fori_loop(h * half, (h + 1) * half, velocity_step, 0, unroll=UNROLL_VELOCITY)
                made = copies((U_NEW, V_NEW), vel_out, h * BS // 2, BS // 2, 24 + 16 * h)
                start(made)
                pending += made
        else:
            lax.fori_loop(0, groups, velocity_step, 0, unroll=UNROLL_VELOCITY)
            for f in (U, V):
                n = S2_OUT + 1 + RENEWED.index(f)
                fields_at[f], fields_at[n] = fields_at[n], fields_at[f]
    for _, full, _ in pending:
        full.wait()


def dynamics(lens, band, lon, vel, stress, area, thick, got, coriolis):
    width = SLOTS * BS
    vmem = pl.BlockSpec(memory_space=pltpu.VMEM)
    smem = pl.BlockSpec(memory_space=pltpu.SMEM)
    return pl.pallas_call(
        dynamics_kernel,
        in_specs=[smem] * 3 + [vmem] * 6,
        out_specs=[pl.BlockSpec(memory_space=pl.ANY)] * 2 + [vmem],
        scratch_shapes=[
            *[pltpu.VMEM((ROWS, STRIP), F32) for _ in range(S2_OUT + 6)],
            pltpu.VMEM((BS, BS), F32),
            pltpu.SemaphoreType.DMA((24 + 32,)),
        ],
        out_shape=[
            jax.ShapeDtypeStruct((2, BS, width), F32),
            jax.ShapeDtypeStruct((3, BS, width), F32),
            jax.ShapeDtypeStruct((NLON, M3_ROWS, BS), BF16),
        ],
        compiler_params=pltpu.CompilerParams(vmem_limit_bytes=32 * 2**20),
        name="dynamics",
    )(lens, band, lon, vel, stress, area, thick, got, coriolis)


def sort_kernel(lens, band, got, out, table):
    odd = lax.rem(band[0], 2) == 1

    def owner(k, start):
        note_slots(table, k, lens[band[0], k], start, odd)
        return start + lens[band[0], k]

    lax.fori_loop(0, NLON, owner, 0, unroll=NLON)

    def block(c, carry):
        out[c] = got[table[c]]
        return carry

    lax.fori_loop(0, NBB, block, 0, unroll=16)


def sort_back(lens, band, got):
    return pl.pallas_call(
        sort_kernel,
        out_shape=jax.ShapeDtypeStruct((NBB, 16, BS), BF16),
        in_specs=[pl.BlockSpec(memory_space=pltpu.SMEM)] * 2
        + [pl.BlockSpec(memory_space=pltpu.VMEM)],
        out_specs=pl.BlockSpec(memory_space=pltpu.VMEM),
        scratch_shapes=[pltpu.SMEM((NBB + 1,), jnp.int32)],
        compiler_params=pltpu.CompilerParams(vmem_limit_bytes=16 * 2**20),
        name="sort_back",
    )(lens, band, got)


def settle_kernel(got, out):
    def rows16(pair, carry):
        rows = pl.ds(pl.multiple_of(pair * 16, 16), 16)
        for cb in range(TILE):
            a = got[2 * pair, cb * 16 : (cb + 1) * 16, :].astype(F32)
            b = got[2 * pair + 1, cb * 16 : (cb + 1) * 16, :].astype(F32)
            lanes = slice(cb * BS, (cb + 1) * BS)
            out[0, rows, lanes] = jnp.concatenate([a[0:8], b[0:8]], axis=0).astype(BF16)
            out[1, rows, lanes] = jnp.concatenate([a[8:16], b[8:16]], axis=0).astype(BF16)
        return carry

    lax.fori_loop(0, BS // 16, rows16, 0, unroll=8)


def settle(got):
    return pl.pallas_call(
        settle_kernel,
        out_shape=jax.ShapeDtypeStruct((2, BS, TILE * BS), BF16),
        in_specs=[pl.BlockSpec(memory_space=pltpu.VMEM)],
        out_specs=pl.BlockSpec(memory_space=pltpu.VMEM),
        compiler_params=pltpu.CompilerParams(vmem_limit_bytes=16 * 2**20),
        name="settle",
    )(got)


def to_all(block):
    return lax.all_to_all(block, "lon", 0, 0, tiled=True)


def body(ocean_forcing, ice_velocity, ice_stress, cat_area, cat_thick, run_lengths):
    band_idx = lax.axis_index("lat")
    lon_idx = lax.axis_index("lon")
    lens = run_lengths
    place = (jnp.reshape(band_idx, (1,)), jnp.reshape(lon_idx, (1,)))
    ice = (ice_velocity, ice_stress, cat_area, cat_thick)
    place_of = jnp.arange(ROWS, dtype=jnp.int32)
    place_of = jnp.where(place_of < BS + 4, place_of, place_of - ROWS)
    rows = (band_idx * BS + place_of).astype(F32)
    latitude = -78.0 + 168.0 * (rows + 0.5) / (BS * NLAT)
    coriolis = jnp.broadcast_to(jnp.sin(latitude * (jnp.pi / 180.0))[:, None], (ROWS, BS))
    to_mate, to_other, edges = make_edges(lens, *place, *ice, ocean_forcing)
    message = spread(ocean_forcing, edges)
    pairs = [(b, b ^ 1) for b in range(NLAT)]
    from_mate = lax.ppermute(to_mate, "lat", pairs)
    pairs = [(b, b + 1 if b % 2 else b - 1) for b in range(1, NLAT - 1)]
    from_other = lax.ppermute(to_other, "lat", pairs)
    from_mate, from_other, coriolis = lax.optimization_barrier((from_mate, from_other, coriolis))
    message = spread_strips(place[0], message, from_mate, from_other)
    dealt = to_all(deal(lens, *place, to_all(message)))
    velocity_out, stress_out, handed = dynamics(lens, *place, *ice, dealt, coriolis)
    handed = to_all(handed).reshape(NLON * SLOTS, 16, BS)
    back = sort_back(lens, place[0], handed).reshape(NLON, M4_ROWS, BS)
    return (velocity_out, stress_out, settle(to_all(back)))


def solution(mesh):
    slots = P(None, None, ("lat", "lon"))
    grid = P(None, "lat", "lon")
    return jax.shard_map(
        body,
        mesh=mesh,
        in_specs=(grid, slots, slots, slots, slots, P()),
        out_specs=(slots, slots, grid),
        check_vma=False,
    )
```

```python
import functools

import jax
import jax.numpy as jnp
from jax import lax
from jax.experimental import pallas as pl
from jax.experimental.pallas import tpu as pltpu
from jax.sharding import PartitionSpec as P

BS = 128
ITERS = 3
NLAT = 8
NLON = 16
SLOTS = 8
NBB = 64
TILE = 4
DEEP = 3
PSTAR = 2.0
CSTAR = 20.0
DMIN_SQ = 0.01
SPEED_SQ = 0.01
ICE = 7
U, V, SXX, SYY, S12, AREA, MASS, STR, UO, VO, TX, TY, TURN, S1_OUT, S2_OUT, U_NEW, V_NEW = range(17)
RENEWED = (U, V, SXX, SYY, S12)
EDGE_LANES = 3 * ICE
EAST_AT = 4 * EDGE_LANES
WEST_AT = EAST_AT + 12
STRIP = (SLOTS + 1) * BS
UNROLL = 4
UNROLL_OWN = 8
UNROLL_STRESS = 16
UNROLL_VELOCITY = 8
WIDE = 3 * BS
ROWS = BS + 8
SEND_ROWS = 24
MASS_AT, FORCE_AT = 18, 20
M1_ROWS = TILE * 32 + SLOTS * 8
M2_ROWS = SLOTS * 32 + (SLOTS + 1) * 8 + 8
M3_ROWS = SLOTS * 16
M4_ROWS = TILE * 16
F32 = jnp.float32
BF16 = jnp.bfloat16


def lanes_of(shape):
    return lax.broadcasted_iota(jnp.int32, shape, len(shape) - 1)


def ice_fields(vel, stress, area, thick):
    conc = area[0] + area[1] + area[2] + area[3] + area[4]
    mass = area[0] * thick[0]
    for n in range(1, 5):
        mass = mass + area[n] * thick[n]
    sxx, syy = 0.5 * (stress[0] + stress[1]), 0.5 * (stress[0] - stress[1])
    return [vel[0], vel[1], sxx, syy, stress[2], conc, mass]


def strength_of(conc, mass):
    return (PSTAR / 6.0) * mass * jnp.exp(-CSTAR * (1.0 - conc))


def edges_kernel(lens, band, lon, *refs):
    ice = [refs[4 * i : 4 * i + 4] for i in range(4)]
    f_low, f_high, to_mate, to_other, packed_out = refs[16:]
    odd = lax.rem(band[0], 2) == 1

    def strips(out, which, force, row0, frow0):
        arrays = [ice[i][which] for i in range(4)]
        fields = ice_fields(*[[a[n] for n in range(a.shape[0])] for a in arrays])
        for f in range(MASS):
            out[3 * f : 3 * f + 3, :] = fields[f][row0 : row0 + 3, :]
        near = row0 if row0 == 0 else row0 + 1
        out[MASS_AT : MASS_AT + 2, :] = fields[MASS][near : near + 2, :]
        if row0:
            strength = strength_of(fields[AREA], fields[MASS])
            out[3 * AREA : 3 * AREA + 1, :] = strength[row0 : row0 + 1, :]
        for f in range(4):
            rows = force[f].astype(F32)
            at = FORCE_AT + f
            out[at : at + 1, 0:512] = rows[frow0 : frow0 + 1, :]
            out[at : at + 1, 512:1024] = rows[frow0 + 1 : frow0 + 2, :]

    low, high = (0, f_low, 0, 0), (1, f_high, 5, 14)

    @pl.when(odd)
    def _():
        strips(to_mate, *low)
        strips(to_other, *high)

    @pl.when(jnp.logical_not(odd))
    def _():
        strips(to_mate, *high)
        strips(to_other, *low)

    lane = lanes_of((BS, BS))
    total = jnp.zeros((BS, BS), F32)
    for side in range(2):
        arrays = [ice[i][2 + side] for i in range(4)]
        fields = ice_fields(*[[a[n] for n in range(a.shape[0])] for a in arrays])
        first_columns = jnp.broadcast_to(odd if side else jnp.logical_not(odd), (BS, BS))
        packed = jnp.zeros((BS, BS), F32)
        for f in range(ICE):
            at_zero = jnp.where(first_columns, fields[f], pltpu.roll(fields[f], 3, 1))
            moved = pltpu.roll(at_zero, 3 * f, 1) if f else at_zero
            packed = jnp.where((lane >= 3 * f) & (lane < 3 * f + 3), moved, packed)
        high = packed.astype(BF16).astype(F32)
        both = high + pltpu.roll(packed - high, EDGE_LANES, 1)
        total = total + (pltpu.roll(both, 2 * EDGE_LANES, 1) if side else both)
    packed_out[...] = total


def make_edges(lens, band, lon, vel, stress, area, thick, forcing):
    width = SLOTS * BS

    def at(*index):
        return lambda i, lens, band, lon: index

    def specs(n):
        return [
            pl.BlockSpec((n, 8, width), at(0, 0, 0)),
            pl.BlockSpec((n, 8, width), at(0, BS // 8 - 1, 0)),
            pl.BlockSpec((n, BS, BS), at(0, 0, 0)),
            pl.BlockSpec(
                (n, BS, BS), lambda i, lens, band, lon: (0, 0, lens[band[0], lon[0]] - 1)
            ),
        ]

    in_specs = specs(2) + specs(3) + specs(5) + specs(5)
    in_specs += [
        pl.BlockSpec((4, 16, 512), at(0, 0, 0)),
        pl.BlockSpec((4, 16, 512), at(0, BS // 16 - 1, 0)),
    ]
    return pl.pallas_call(
        edges_kernel,
        grid_spec=pltpu.PrefetchScalarGridSpec(
            num_scalar_prefetch=3,
            grid=(1,),
            in_specs=in_specs,
            out_specs=[pl.BlockSpec((SEND_ROWS, width), at(0, 0))] * 2
            + [pl.BlockSpec((BS, BS), at(0, 0))],
        ),
        out_shape=[jax.ShapeDtypeStruct((SEND_ROWS, width), F32)] * 2
        + [jax.ShapeDtypeStruct((BS, BS), F32)],
        compiler_params=pltpu.CompilerParams(vmem_limit_bytes=60 * 2**20),
        name="edges",
    )(lens, band, lon, *([vel] * 4), *([stress] * 4), *([area] * 4), *([thick] * 4), forcing, forcing)


def spread_kernel(forcing, edges, out):
    def rows16(pair, carry):
        base = pl.multiple_of(pair * 16, 16)
        for cb in range(TILE):
            parts = [
                forcing[f, pl.ds(base, 16), cb * BS : (cb + 1) * BS].astype(F32) for f in range(4)
            ]
            low = jnp.concatenate([p[0:8] for p in parts], axis=0)
            high = jnp.concatenate([p[8:16] for p in parts], axis=0)
            out[2 * pair, cb * 32 : (cb + 1) * 32, :] = low.astype(BF16)
            out[2 * pair + 1, cb * 32 : (cb + 1) * 32, :] = high.astype(BF16)
        return carry

    lax.fori_loop(0, BS // 16, rows16, 0, unroll=2)
    row = lax.broadcasted_iota(jnp.int32, (SLOTS, 8, BS), 1)
    for j in range(NLON):
        rows = edges[8 * j : 8 * j + 8, :].reshape(SLOTS, 1, BS)
        rows = jnp.where(row == 7, jnp.broadcast_to(rows, (SLOTS, 8, BS)), 0.0)
        out[j, TILE * 32 :, :] = rows.reshape(SLOTS * 8, BS).astype(BF16)


def spread(forcing, edges):
    return pl.pallas_call(
        spread_kernel,
        out_shape=jax.ShapeDtypeStruct((NLON, M1_ROWS, BS), BF16),
        in_specs=[pl.BlockSpec(memory_space=pltpu.VMEM)] * 2,
        out_specs=pl.BlockSpec(memory_space=pltpu.VMEM),
        compiler_params=pltpu.CompilerParams(vmem_limit_bytes=16 * 2**20),
        name="spread",
    )(forcing, edges)


def spread_strips_kernel(band, message, from_mate, from_other, out, hold):
    odd = lax.rem(band[0], 2) == 1

    def beside(is_north, row, rows, at, width):
        from_chip, from_next = (
            ref[row : row + rows, at : at + width] for ref in (from_mate, from_other)
        )
        use_chip = jnp.logical_not(odd) if is_north else odd
        return jnp.where(jnp.broadcast_to(use_chip, from_chip.shape), from_chip, from_next)

    for j in range(NLON):
        hold[...] = jnp.zeros(hold.shape, F32)
        f = j % 8
        if f < ICE:
            if f < MASS:
                rows = beside(j < 8, 3 * f, 3, 0, SLOTS * BS)
            else:
                rows = beside(j < 8, MASS_AT, 2, 0, SLOTS * BS)
                spare = jnp.zeros((1, SLOTS * BS), F32)
                rows = jnp.concatenate([rows, spare] if j < 8 else [spare, rows], axis=0)
            high = rows.astype(BF16).astype(F32)
            low = rows - high
            for s in range(SLOTS):
                hold[8 * s : 8 * s + 3, :] = high[:, s * BS : (s + 1) * BS]
                hold[8 * s + 3 : 8 * s + 6, :] = low[:, s * BS : (s + 1) * BS]
        field, h = j // 4, j % 4
        for cb in range(TILE):
            at = (h % 2) * 512 + cb * BS
            hold[8 * cb + 6 : 8 * cb + 7, :] = beside(h >= 2, FORCE_AT + field, 1, at, BS)
        edges = message[j, TILE * 32 :, :].astype(F32)
        out[j, TILE * 32 :, :] = (hold[...] + edges).astype(BF16)


def spread_strips(band, message, from_mate, from_other):
    return pl.pallas_call(
        spread_strips_kernel,
        out_shape=jax.ShapeDtypeStruct((NLON, M1_ROWS, BS), BF16),
        in_specs=[pl.BlockSpec(memory_space=pltpu.SMEM)]
        + [pl.BlockSpec(memory_space=pltpu.VMEM)] * 3,
        out_specs=pl.BlockSpec(memory_space=pltpu.VMEM),
        scratch_shapes=[pltpu.VMEM((SLOTS * 8, BS), F32)],
        input_output_aliases={1: 0},
        compiler_params=pltpu.CompilerParams(vmem_limit_bytes=16 * 2**20),
        name="spread_strips",
    )(band, message, from_mate, from_other)


def note_slots(table, k, count, start, odd):
    for s in range(SLOTS):
        at = start + s
        column = jnp.where(odd, NBB - 1 - at, at)
        table[jnp.where(s < count, column, NBB)] = k * SLOTS + s


def deal_kernel(lens, band, lon, got, out, groups, halos, table):
    band, lon = band[0], lon[0]
    odd = lax.rem(band, 2) == 1
    other = jnp.where(lon < 8, jnp.minimum(band + 1, NLAT - 1), jnp.maximum(band - 1, 0))
    other_odd = lax.rem(other, 2) == 1

    def fill(l, start):
        groups[pl.ds(pl.multiple_of(l * SLOTS, SLOTS), SLOTS)] = (
            got[l, TILE * 32 :, :].astype(F32).reshape(SLOTS, 8, BS)
        )
        note_slots(table, l, lens[other, l], start, other_odd)
        return start + lens[other, l]

    lax.fori_loop(0, NLON, fill, 0, unroll=NLON)
    row6 = lax.broadcasted_iota(jnp.int32, (8, BS), 0) == 6

    def halo(c, carry):
        own = (c // TILE) * SLOTS + lax.rem(c, TILE)
        halos[c] = jnp.where(row6, groups[own], groups[table[c]])
        return carry

    lax.fori_loop(0, NBB, halo, 0, unroll=32)
    lane = lanes_of((8, BS))

    def column_at(p):
        p = jnp.minimum(p, NBB - 1)
        return jnp.where(odd, NBB - 1 - p, p)

    def forcing(c):
        at = pl.multiple_of(lax.rem(c, TILE) * 32, 32)
        return got[c // TILE, pl.ds(at, 32), :]

    def edges(k):
        at = pl.multiple_of(lax.rem(k, NLON) * SLOTS, SLOTS)
        return groups[pl.ds(at, SLOTS), 7, :]

    def owner(k, start):
        count = lens[band, k]
        last = start + count - 1
        east = jnp.where(odd, NBB - 1 - start, last) + 1
        west = jnp.where(odd, NBB - 1 - last, start) - 1
        east, west = lax.rem(east, NBB), lax.rem(west + NBB, NBB)
        parts = []
        for e in range(SLOTS):
            c = column_at(start + e)
            out[k, e * 32 : (e + 1) * 32, :] = forcing(c)
            parts.append(halos[c])
        parts.append(jnp.where(lane < 64, halos[east], halos[west]))
        side = jnp.where(lane < 2 * EDGE_LANES, edges(k + 1), edges(k + NLON - 1))
        by_east, by_west = forcing(east).astype(F32), forcing(west).astype(F32)
        for f in range(4):
            for rows, at, col in ((by_east, EAST_AT, 0), (by_west, WEST_AT, 125)):
                there = at + 3 * f
                moved = pltpu.roll(rows[8 * f : 8 * f + 8, :], (there - col) % BS, 1)
                side = jnp.where((lane >= there) & (lane < there + 3), moved, side)
        parts.append(side)
        out[k, SLOTS * 32 :, :] = jnp.concatenate(parts, axis=0).astype(BF16)
        return start + count

    lax.fori_loop(0, NLON, owner, 0, unroll=NLON)


def deal(lens, band, lon, got):
    return pl.pallas_call(
        deal_kernel,
        out_shape=jax.ShapeDtypeStruct((NLON, M2_ROWS, BS), BF16),
        in_specs=[pl.BlockSpec(memory_space=pltpu.SMEM)] * 3
        + [pl.BlockSpec(memory_space=pltpu.VMEM)],
        out_specs=pl.BlockSpec(memory_space=pltpu.VMEM),
        scratch_shapes=[
            pltpu.VMEM((NLON * SLOTS, 8, BS), F32),
            pltpu.VMEM((NBB, 8, BS), F32),
            pltpu.SMEM((NBB + 1,), jnp.int32),
        ],
        compiler_params=pltpu.CompilerParams(vmem_limit_bytes=32 * 2**20),
        name="deal",
    )(lens, band, lon, got)


def dynamics_kernel(
    lens, band, lon, vel, stress, area, thick, got, coriolis,
    vel_out, stress_out, handed, *scratch,
):
    fields_at, (empty, sems) = list(scratch[:-2]), scratch[-2:]
    band, lon = band[0], lon[0]
    odd = lax.rem(band, 2) == 1
    count = lens[band, lon]
    groups = BS // 8

    def rows_at(g):
        return pl.ds(g * 8 if isinstance(g, int) else pl.multiple_of(g * 8, 8), 8)

    def slot_lanes(slot):
        return pl.ds(pl.multiple_of(jnp.where(odd, SLOTS - 1 - slot, slot) * BS, BS), BS)

    edge_lanes = pl.ds(SLOTS * BS, BS)

    def strips_of(j):
        group = got[j, SLOTS * 32 : SLOTS * 32 + 8 * (SLOTS + 1), :].astype(F32)
        return group.reshape(SLOTS + 1, 8, BS)

    empty[...] = jnp.zeros(empty.shape, F32)

    below4 = lax.broadcasted_iota(jnp.int32, (SLOTS + 1, 8, BS), 1) < 4
    groups_of = []
    for j in range(NLON):
        group = strips_of(j)
        groups_of.append(group)
        force_row = (BS + 6, BS + 7, BS, BS + 1)[j % 4]
        for e in range(SLOTS + 1):
            lanes = slot_lanes(e) if e < SLOTS else edge_lanes
            mine = jnp.broadcast_to(e < count, (8, BS))
            rows = jnp.where(mine, group[e], group[SLOTS])
            fields_at[UO + j // 4][force_row : force_row + 1, lanes] = rows[6:7, :]
    for f in range(ICE):
        north, south = groups_of[f], groups_of[f + 8]
        north = north + pltpu.roll(north, 5, 1)
        south = pltpu.roll(south + pltpu.roll(south, 5, 1), 5, 1)
        both = jnp.where(below4, north, south)
        for e in range(SLOTS + 1):
            lanes = slot_lanes(e) if e < SLOTS else edge_lanes
            mine = jnp.broadcast_to(e < count, (8, BS))
            fields_at[f][rows_at(groups), lanes] = jnp.where(mine, both[e], both[SLOTS])

    def derived(conc, mass, g, lanes):
        turn = coriolis[rows_at(g), :]
        if conc.shape[1] > BS:
            turn = jnp.concatenate([turn] * (conc.shape[1] // BS), axis=1)
        fields_at[STR][rows_at(g), lanes] = strength_of(conc, mass)
        fields_at[TURN][rows_at(g), lanes] = turn * mass

    derived(fields_at[AREA][rows_at(groups), :], fields_at[MASS][rows_at(groups), :], groups, slice(0, STRIP))
    far = ROWS - DEEP
    fields_at[STR][far : far + 1, :] = fields_at[AREA][far : far + 1, :]

    def own_rows(j, carry):
        packed = got[j, M2_ROWS - 16 :, :].astype(F32)[8:16, :]
        near = lanes_of((8, BS)) < 64

        def joined(east, east_lane, west, west_lane):
            return jnp.where(
                near,
                pltpu.roll(east, (BS - east_lane) % BS, 1),
                pltpu.roll(west, (125 - west_lane) % BS, 1),
            )

        forced = [joined(packed, EAST_AT + 3 * f, packed, WEST_AT + 3 * f) for f in range(4)]
        packed = packed + pltpu.roll(packed, BS - EDGE_LANES, 1)
        at_zero = pltpu.roll(packed, BS - 2 * EDGE_LANES, 1)
        east = jnp.where(odd, at_zero, packed)
        west = jnp.where(odd, packed, at_zero)
        beside = [joined(east, 3 * f, west, 3 * f) for f in range(ICE)]
        rows = rows_at(j)
        for e in range(SLOTS + 1):
            if e == SLOTS:
                fields, lanes = beside, edge_lanes
            else:
                lanes = slot_lanes(e)
                at = slice(e * BS, (e + 1) * BS)
                fields = ice_fields(
                    [vel[n, rows, at] for n in range(2)],
                    [stress[n, rows, at] for n in range(3)],
                    [area[n, rows, at] for n in range(5)],
                    [thick[n, rows, at] for n in range(5)],
                )
                mine = jnp.broadcast_to(e < count, (8, BS))
                fields = [jnp.where(mine, fields[f], beside[f]) for f in range(ICE)]
            force = forced
            if e < SLOTS:
                force = got[j, e * 32 : (e + 1) * 32, :].astype(F32)
                force = [jnp.where(mine, force[8 * f : 8 * f + 8], forced[f]) for f in range(4)]
            for f in range(4):
                fields_at[UO + f][rows_at(j), lanes] = force[f]
            for f in range(ICE):
                fields_at[f][rows_at(j), lanes] = fields[f]
            derived(fields[AREA], fields[MASS], j, lanes)
        return carry

    lax.fori_loop(0, groups, own_rows, 0, unroll=UNROLL_OWN)

    cells = (8, WIDE)
    row = lax.broadcasted_iota(jnp.int32, cells, 0)

    def load(f, g, c, width=WIDE):
        return fields_at[f][rows_at(g), c : c + width]

    def north_of(f, x, g, c):
        above = 0 if isinstance(g, int) and g == groups else g + 1
        return pltpu.roll(jnp.where(row == 0, load(f, above, c), x), 7, 0)

    def south_of(f, x, g, c):
        below = lax.rem(g + groups, groups + 1)
        return pltpu.roll(jnp.where(row == 7, load(f, below, c), x), 1, 0)

    def east_of(f, x, g, c):
        if WIDE == STRIP:
            return pltpu.roll(x, STRIP - 1, 1)
        more = load(f, g, (c + WIDE) % STRIP, BS)
        return pltpu.roll(jnp.concatenate([x, more], axis=1), WIDE + BS - 1, 1)[:, :WIDE]

    def west_of(f, x, g, c):
        if WIDE == STRIP:
            return pltpu.roll(x, 1, 1)
        more = load(f, g, (c - BS) % STRIP, BS)
        return pltpu.roll(jnp.concatenate([more, x], axis=1), 1, 1)[:, BS:]

    def stress_rows(g, new, last):
        for c in range(0, STRIP, WIDE):
            u, v = load(U, g, c), load(V, g, c)
            exx = east_of(U, u, g, c) - u
            eyy = north_of(V, v, g, c) - v
            shr = (north_of(U, u, g, c) - u) + (east_of(V, v, g, c) - v)
            div = exx + eyy
            ten = exx - eyy
            square = div * div + 0.25 * (ten * ten + shr * shr) + DMIN_SQ
            sixth = load(STR, g, c)
            half = sixth * lax.rsqrt(square)
            eighth = 0.25 * half
            both = half * div - sixth
            apart = eighth * ten
            sxx = (2.0 / 3.0) * load(SXX, g, c) + (both + apart)
            syy = (2.0 / 3.0) * load(SYY, g, c) + (both - apart)
            at = slice(c, c + WIDE)
            new[SXX][rows_at(g), at] = sxx
            new[SYY][rows_at(g), at] = syy
            new[S12][rows_at(g), at] = (2.0 / 3.0) * load(S12, g, c) + eighth * shr
            if last:
                new[S1_OUT][rows_at(g), at] = sxx + syy
                new[S2_OUT][rows_at(g), at] = sxx - syy

    def velocity_rows(g, new, beyond=None, last=False):
        for c in range(0, STRIP, WIDE):
            sxx, syy, s12 = load(SXX, g, c), load(SYY, g, c), load(S12, g, c)
            fx = sxx - west_of(SXX, sxx, g, c) + s12 - south_of(S12, s12, g, c)
            fy = s12 - west_of(S12, s12, g, c) + syy - south_of(SYY, syy, g, c)
            u, v, uo, vo = [load(f, g, c) for f in (U, V, UO, VO)]
            m, conc, tx, ty = [load(f, g, c) for f in (MASS, AREA, TX, TY)]
            du, dv = uo - u, vo - v
            square = du * du + dv * dv + SPEED_SQ
            drag = conc * (square * lax.rsqrt(square))
            d = m + drag
            q = load(TURN, g, c)
            ru = m * u + fx + tx + drag * uo
            rv = m * v + fy + ty + drag * vo
            inv = 1.0 / (d * d + q * q)
            u = (d * ru + q * rv) * inv
            v = (d * rv - q * ru) * inv
            if beyond is not None:
                u = jnp.where(beyond, 0.0, u)
                v = jnp.where(beyond, 0.0, v)
            at = slice(c, c + WIDE)
            new[U][rows_at(g), at] = u
            new[V][rows_at(g), at] = v
            if last:
                du, dv = u - uo, v - vo
                square = du * du + dv * dv + SPEED_SQ
                drag = conc * (square * lax.rsqrt(square))
                x = (1.0 - conc) * tx + drag * du
                y = (1.0 - conc) * ty + drag * dv
                for i in range(WIDE // BS):
                    p = c // BS + i
                    if p < SLOTS:
                        slot = jnp.where(odd, SLOTS - 1 - p, p)
                        pair = [x[:, i * BS : (i + 1) * BS], y[:, i * BS : (i + 1) * BS]]
                        handed[g, pl.ds(pl.multiple_of(slot * 16, 16), 16), :] = (
                            jnp.concatenate(pair, axis=0).astype(BF16)
                        )

    def copies(fields, out, row0, rows, sem0):
        made = []
        for n, f in enumerate(fields):
            for e in range(SLOTS):
                to = out.at[n, pl.ds(row0, rows), pl.ds(e * BS, BS)]
                sem = sems.at[sem0 + n * SLOTS + e]
                block = fields_at[f].at[pl.ds(row0, rows), slot_lanes(e)]
                made.append((e, pltpu.make_async_copy(block, to, sem),
                             pltpu.make_async_copy(empty.at[pl.ds(0, rows), :], to, sem)))
        return made

    def start(made):
        for e, full, none in made:
            @pl.when(e < count)
            def _():
                full.start()

            @pl.when(e >= count)
            def _():
                none.start()

    pending = []
    for it in range(ITERS):
        last = it == ITERS - 1
        new = {f: fields_at[n] for f, n in zip(RENEWED, range(S2_OUT + 1, S2_OUT + 6))}
        new[S1_OUT], new[S2_OUT] = fields_at[S1_OUT], fields_at[S2_OUT]

        def stress_step(g, carry):
            stress_rows(g, new, last)
            return carry

        lax.fori_loop(0, groups, stress_step, 0, unroll=UNROLL_STRESS)
        stress_rows(groups, new, last)
        for f in (SXX, SYY, S12):
            n = S2_OUT + 1 + RENEWED.index(f)
            fields_at[f], fields_at[n] = fields_at[n], fields_at[f]
        if last:
            made = copies((S1_OUT, S2_OUT, S12), stress_out, 0, BS, 0)
            start(made)
            pending += made
        else:
            beyond = (row < 4) & (band == NLAT - 1) | (row >= 4) & (band == 0)
            velocity_rows(groups, new, beyond)

        def velocity_step(g, carry):
            velocity_rows(g, new, None, last)
            return carry

        if last:
            for h in range(2):
                half = groups // 2
                lax.fori_loop(h * half, (h + 1) * half, velocity_step, 0, unroll=UNROLL_VELOCITY)
                made = copies((U_NEW, V_NEW), vel_out, h * BS // 2, BS // 2, 24 + 16 * h)
                start(made)
                pending += made
        else:
            lax.fori_loop(0, groups, velocity_step, 0, unroll=UNROLL_VELOCITY)
            for f in (U, V):
                n = S2_OUT + 1 + RENEWED.index(f)
                fields_at[f], fields_at[n] = fields_at[n], fields_at[f]
    for _, full, _ in pending:
        full.wait()


def dynamics(lens, band, lon, vel, stress, area, thick, got, coriolis):
    width = SLOTS * BS
    vmem = pl.BlockSpec(memory_space=pltpu.VMEM)
    smem = pl.BlockSpec(memory_space=pltpu.SMEM)
    return pl.pallas_call(
        dynamics_kernel,
        in_specs=[smem] * 3 + [vmem] * 6,
        out_specs=[pl.BlockSpec(memory_space=pl.ANY)] * 2 + [vmem],
        scratch_shapes=[
            *[pltpu.VMEM((ROWS, STRIP), F32) for _ in range(S2_OUT + 6)],
            pltpu.VMEM((BS, BS), F32),
            pltpu.SemaphoreType.DMA((24 + 32,)),
        ],
        out_shape=[
            jax.ShapeDtypeStruct((2, BS, width), F32),
            jax.ShapeDtypeStruct((3, BS, width), F32),
            jax.ShapeDtypeStruct((NLON, M3_ROWS, BS), BF16),
        ],
        compiler_params=pltpu.CompilerParams(vmem_limit_bytes=32 * 2**20),
        name="dynamics",
    )(lens, band, lon, vel, stress, area, thick, got, coriolis)


def sort_kernel(lens, band, got, out, table):
    odd = lax.rem(band[0], 2) == 1

    def owner(k, start):
        note_slots(table, k, lens[band[0], k], start, odd)
        return start + lens[band[0], k]

    lax.fori_loop(0, NLON, owner, 0, unroll=NLON)

    def block(c, carry):
        out[c] = got[table[c]]
        return carry

    lax.fori_loop(0, NBB, block, 0, unroll=NBB)


def sort_back(lens, band, got):
    return pl.pallas_call(
        sort_kernel,
        out_shape=jax.ShapeDtypeStruct((NBB, 16, BS), BF16),
        in_specs=[pl.BlockSpec(memory_space=pltpu.SMEM)] * 2
        + [pl.BlockSpec(memory_space=pltpu.VMEM)],
        out_specs=pl.BlockSpec(memory_space=pltpu.VMEM),
        scratch_shapes=[pltpu.SMEM((NBB + 1,), jnp.int32)],
        compiler_params=pltpu.CompilerParams(vmem_limit_bytes=16 * 2**20),
        name="sort_back",
    )(lens, band, got)


def settle_kernel(got, out):
    def rows16(pair, carry):
        rows = pl.ds(pl.multiple_of(pair * 16, 16), 16)
        for cb in range(TILE):
            a = got[2 * pair, cb * 16 : (cb + 1) * 16, :].astype(F32)
            b = got[2 * pair + 1, cb * 16 : (cb + 1) * 16, :].astype(F32)
            lanes = slice(cb * BS, (cb + 1) * BS)
            out[0, rows, lanes] = jnp.concatenate([a[0:8], b[0:8]], axis=0).astype(BF16)
            out[1, rows, lanes] = jnp.concatenate([a[8:16], b[8:16]], axis=0).astype(BF16)
        return carry

    lax.fori_loop(0, BS // 16, rows16, 0, unroll=8)


def settle(got):
    return pl.pallas_call(
        settle_kernel,
        out_shape=jax.ShapeDtypeStruct((2, BS, TILE * BS), BF16),
        in_specs=[pl.BlockSpec(memory_space=pltpu.VMEM)],
        out_specs=pl.BlockSpec(memory_space=pltpu.VMEM),
        compiler_params=pltpu.CompilerParams(vmem_limit_bytes=16 * 2**20),
        name="settle",
    )(got)


def to_all(block):
    return lax.all_to_all(block, "lon", 0, 0, tiled=True)


def body(ocean_forcing, ice_velocity, ice_stress, cat_area, cat_thick, run_lengths):
    band_idx = lax.axis_index("lat")
    lon_idx = lax.axis_index("lon")
    lens = run_lengths
    place = (jnp.reshape(band_idx, (1,)), jnp.reshape(lon_idx, (1,)))
    ice = (ice_velocity, ice_stress, cat_area, cat_thick)
    place_of = jnp.arange(ROWS, dtype=jnp.int32)
    place_of = jnp.where(place_of < BS + 4, place_of, place_of - ROWS)
    rows = (band_idx * BS + place_of).astype(F32)
    latitude = -78.0 + 168.0 * (rows + 0.5) / (BS * NLAT)
    coriolis = jnp.broadcast_to(jnp.sin(latitude * (jnp.pi / 180.0))[:, None], (ROWS, BS))
    to_mate, to_other, edges = make_edges(lens, *place, *ice, ocean_forcing)
    message = spread(ocean_forcing, edges)
    pairs = [(b, b ^ 1) for b in range(NLAT)]
    from_mate = lax.ppermute(to_mate, "lat", pairs)
    pairs = [(b, b + 1 if b % 2 else b - 1) for b in range(1, NLAT - 1)]
    from_other = lax.ppermute(to_other, "lat", pairs)
    from_mate, from_other, coriolis = lax.optimization_barrier((from_mate, from_other, coriolis))
    message = spread_strips(place[0], message, from_mate, from_other)
    dealt = to_all(deal(lens, *place, to_all(message)))
    velocity_out, stress_out, handed = dynamics(lens, *place, *ice, dealt, coriolis)
    handed = to_all(handed).reshape(NLON * SLOTS, 16, BS)
    back = sort_back(lens, place[0], handed).reshape(NLON, M4_ROWS, BS)
    return (velocity_out, stress_out, settle(to_all(back)))


def solution(mesh):
    slots = P(None, None, ("lat", "lon"))
    grid = P(None, "lat", "lon")
    return jax.shard_map(
        body,
        mesh=mesh,
        in_specs=(grid, slots, slots, slots, slots, P()),
        out_specs=(slots, slots, grid),
        check_vma=False,
    )
```
